256 devices in a mesh: ch: 8 (over z), seq: 32 (over y, x, core).
Axes of the slice: x: 4, y: 4, z: 8, core: 2. Of those that a mesh axis runs over, the one named last changes fastest.
Arguments:
- inputs: bfloat16 [4096, 4096], P('seq', 'ch'), may hold values from -6 to 6
- in_weight: bfloat16 [4096, 3, 4096], P('seq'), may hold values from -0.09375 to 0.09375
- out_weight: bfloat16 [4096, 4096], P('seq', 'ch'), may hold values from -0.09375 to 0.09375
- short_filter: float32 [3, 3, 4096], P(None, None, 'ch'), may hold values from -3 to 3
- decay: float32 [4096, 2], P('ch'), may hold values from 7.324219e-05 to 0.025
- angle: float32 [4096, 2], P('ch'), may hold values from 0 to 0.5
- residue: float32 [2, 4096, 2], P(None, 'ch'), may hold values from -4 to 4
- bias: float32 [4096], P('ch'), may hold values from -4 to 4
Outputs:
- mixed: bfloat16 [4096, 4096], P('seq', 'ch')
The draws below stay inside these ranges and needn't reach their ends.
All inputs are finite; a program needn't handle non-finite values.
Results may differ from the reference program's by a relative error of at most 0.007.
Values may be sent and summed in bfloat16 or wider, within the bound.
No kernel may reach another device: no remote copies, remote signals or barrier semaphores. Data moves between devices by JAX's collectives and lax.ppermute only.
A program may use at most 64 MiB of HBM per device.

```python
import math
import jax
import jax.numpy as jnp
from jax import lax

D = 4096
MODES = 2
TOKENS = 4096


def decay_rates(key, low, high):
    unit = jax.random.uniform(key, (D, MODES), jnp.float32)
    return jnp.exp(low + (high - low) * unit)


def draw_decay(key, part):
    rates = decay_rates(key, math.log(0.5 / TOKENS), math.log(1.0 / 40.0))
    return rates


def draw_residue(key, part):
    rates = decay_rates(key, math.log(0.5 / TOKENS), math.log(1.0 / 40.0))
    key = jax.random.fold_in(key, 12)
    values = jnp.clip(jax.random.normal(key, (2, D, MODES), jnp.float32), -4.0, 4.0)
    return values * jnp.sqrt(rates)[None] * 2.0


def level_of(own_key, shape, shards, least, top_value):
    factor_of = 1.0
    for position, blocks in shards:
        draws = jax.random.uniform(jax.random.fold_in(jax.random.fold_in(own_key, 6), position), (blocks,), jnp.float32, least / len(shards), top_value / len(shards))
        factor_of = factor_of * jnp.repeat(jnp.exp(draws), shape[position] // blocks).reshape((-1,) + (1,) * (len(shape) - 1 - position))
    return factor_of


def gaussian(key, shape, scale, bound, split=(), dtype=jnp.bfloat16):
    values = scale * jax.random.normal(key, shape, jnp.float32)
    if split:
        values = values * level_of(key, shape, split, -0.22, 0.18)
    return jnp.clip(values, -bound, bound).astype(dtype)


def setup_inputs(seed: int = 0) -> dict:
    seeds = jax.random.split(jax.random.key(seed), 9)
    return {
        "inputs": gaussian(seeds[0], (TOKENS, D), 1.0, 6.0, ((0, 32), (1, 8))),
        "in_weight": gaussian(seeds[1], (D, 3, D), D ** -0.5, 0.09375, ((0, 32),)),
        "out_weight": gaussian(seeds[2], (D, D), D ** -0.5, 0.09375, ((0, 32), (1, 8))),
        "short_filter": gaussian(seeds[3], (3, 3, D), 0.6, 3.0, ((2, 8),), jnp.float32),
        "decay": draw_decay(jax.random.fold_in(seeds[8], 71), 0),
        "angle": jnp.clip(0.5 * jax.random.uniform(seeds[5], (D, MODES), jnp.float32) ** level_of(seeds[5], (D, MODES), ((0, 8),), -0.2, 0.2), 0.0, 0.5),
        "residue": draw_residue(jax.random.fold_in(seeds[8], 71), 0),
        "bias": gaussian(seeds[7], (D,), 1.0, 4.0, ((0, 8),), jnp.float32),
    }


def reference(inputs, in_weight, out_weight, short_filter, decay, angle, residue, bias):
    width = inputs.shape[1]
    length = inputs.shape[0]
    projected = jnp.dot(inputs, in_weight.reshape(width, 3 * width), preferred_element_type=jnp.float32)
    projected = projected.astype(jnp.bfloat16).reshape(length, 3, width).astype(jnp.float32)
    padded = jnp.concatenate([jnp.zeros((2, 3, width), jnp.float32), projected], axis=0)
    filtered = short_filter[0] * padded[2:] + short_filter[1] * padded[1:-1] + short_filter[2] * padded[:-2]
    mixin = filtered[:, 1, :] * filtered[:, 2, :]
    group = math.gcd(width, 256)
    count = width // group
    lags = jnp.arange(length).astype(jnp.float32)

    def convolve(pieces):
        signal, rate, turn, real_part, imag_part = pieces
        mag = jnp.exp(-lags[:, None, None] * rate[None])
        phase = lags[:, None, None] * turn[None]
        kernel = jnp.sum(mag * (real_part[None] * jnp.cos(phase) - imag_part[None] * jnp.sin(phase)), axis=2)
        spectrum = jnp.fft.rfft(signal, n=2 * length, axis=0) * jnp.fft.rfft(kernel, n=2 * length, axis=0)
        return jnp.fft.irfft(spectrum, n=2 * length, axis=0)[:length]

    signal_blocks = mixin.reshape(length, count, group).transpose(1, 0, 2)
    rate_blocks = decay.reshape(count, group, -1)
    turn_blocks = angle.reshape(count, group, -1)
    real_blocks = residue[0].reshape(count, group, -1)
    imag_blocks = residue[1].reshape(count, group, -1)
    conv = lax.map(convolve, (signal_blocks, rate_blocks, turn_blocks, real_blocks, imag_blocks))
    conv = conv.transpose(1, 0, 2).reshape(length, width)
    long_term = conv + bias[None, :] * mixin
    gated = (filtered[:, 0, :] * long_term).astype(jnp.bfloat16)
    return jnp.dot(gated, out_weight, preferred_element_type=jnp.float32).astype(jnp.bfloat16)
```

```python
import functools

import jax
import jax.numpy as jnp
from jax import lax
from jax.experimental import pallas as pl
from jax.experimental.pallas import tpu as pltpu
from jax.sharding import PartitionSpec as P

HALO = 16
LANES = 128
SUB = 8
VMEM = 58 * 1024 * 1024


def spread(x, axis):
    count = lax.axis_size(axis)
    return lax.all_to_all(
        jnp.broadcast_to(x[None], (count,) + x.shape), axis, 0, 0, tiled=True
    )


def powers(exponent, rate, turn):
    mag = jnp.exp(-exponent[:, None, None] * rate[None])
    phase = exponent[:, None, None] * turn[None]
    return mag * jnp.cos(phase), mag * jnp.sin(phase)


def project_kernel(
    rows, chans, x_ref, w_ref, taps_ref, step_ref, join_ref, mixin_ref, query_ref, begin_ref, final_ref, acc
):
    place = pl.program_id(0)

    @pl.when(place == 0)
    def _():
        acc[...] = jnp.zeros_like(acc)

    acc[...] += jnp.dot(x_ref[0], w_ref[...], preferred_element_type=jnp.float32)

    @pl.when(place == pl.num_programs(0) - 1)
    def _():
        length = rows // SUB

        def filtered(branch):
            cols = slice(branch * chans, (branch + 1) * chans)
            now = acc[:rows, cols].astype(jnp.bfloat16).astype(jnp.float32)
            past = acc[rows : rows + 8, cols].astype(jnp.bfloat16).astype(jnp.float32)
            one = jnp.concatenate([past[1:2], now[:-1]], axis=0)
            two = jnp.concatenate([past[0:2], now[:-2]], axis=0)
            tap = [taps_ref[3 * j + branch : 3 * j + branch + 1, :] for j in range(3)]
            return tap[0] * now + tap[1] * one + tap[2] * two

        query = filtered(0)
        mixin = filtered(1) * filtered(2)
        for q in range(chans // LANES):
            cols = slice(q * LANES, (q + 1) * LANES)
            query_ref[q] = query[:, cols]
            mixin_ref[q] = mixin[:, cols]
        for q in range(chans // LANES):
            cols = slice(q * LANES, (q + 1) * LANES)
            wide = lambda row: jnp.broadcast_to(row, (SUB, LANES))
            ar = [wide(step_ref[n : n + 1, cols]) for n in range(2)]
            ai = [wide(step_ref[2 + n : 3 + n, cols]) for n in range(2)]
            re = [jnp.zeros((SUB, LANES), jnp.float32)] * 2
            im = [jnp.zeros((SUB, LANES), jnp.float32)] * 2
            for i in range(length):
                u = mixin_ref[q, pl.ds(i, SUB, stride=length), :]
                for n in range(2):
                    re[n], im[n] = ar[n] * re[n] - ai[n] * im[n] + u, ar[n] * im[n] + ai[n] * re[n]
            for n in range(2):
                jr = join_ref[n : n + 1, cols]
                ji = join_ref[2 + n : 3 + n, cols]
                er = jnp.zeros((1, LANES), jnp.float32)
                ei = jnp.zeros((1, LANES), jnp.float32)
                for b in range(SUB):
                    begin_ref[n, b : b + 1, cols] = er
                    begin_ref[2 + n, b : b + 1, cols] = ei
                    er, ei = (
                        jr * er - ji * ei + re[n][b : b + 1],
                        jr * ei + ji * er + im[n][b : b + 1],
                    )
                final_ref[n : n + 1, cols] = er
                final_ref[2 + n : 3 + n, cols] = ei


def gate_kernel(
    rows, chans, all_ref, jump_ref, begin_ref, reach_ref, step_ref, residue_ref, bias_ref, mixin_ref, query_ref, out_ref, long
):
    length = rows // SUB
    entry = []
    for n in range(2):
        fr, fi = all_ref[:, n, :], all_ref[:, 2 + n, :]
        cr, ci = jump_ref[n], jump_ref[2 + n]
        gr = jnp.sum(cr * fr - ci * fi, axis=0, keepdims=True)
        gi = jnp.sum(cr * fi + ci * fr, axis=0, keepdims=True)
        rr, ri = reach_ref[n], reach_ref[2 + n]
        entry.append((begin_ref[n] + rr * gr - ri * gi, begin_ref[2 + n] + rr * gi + ri * gr))
    for q in range(chans // LANES):
        cols = slice(q * LANES, (q + 1) * LANES)
        wide = lambda row: jnp.broadcast_to(row, (SUB, LANES))
        ar = [wide(step_ref[n : n + 1, cols]) for n in range(2)]
        ai = [wide(step_ref[2 + n : 3 + n, cols]) for n in range(2)]
        pr = [wide(residue_ref[n : n + 1, cols]) for n in range(2)]
        pi = [wide(residue_ref[2 + n : 3 + n, cols]) for n in range(2)]
        direct = wide(bias_ref[:, cols])
        re = [entry[n][0][:, cols] for n in range(2)]
        im = [entry[n][1][:, cols] for n in range(2)]
        for i in range(length):
            u = mixin_ref[q, pl.ds(i, SUB, stride=length), :]
            y = direct * u
            for n in range(2):
                re[n], im[n] = ar[n] * re[n] - ai[n] * im[n] + u, ar[n] * im[n] + ai[n] * re[n]
                y = y + (pr[n] * re[n] - pi[n] * im[n])
            long[q, pl.ds(i, SUB, stride=length), :] = y
        out_ref[:, cols] = (query_ref[q] * long[q]).astype(out_ref.dtype)


def mix_kernel(x_ref, w_ref, out_ref, acc):
    place = pl.program_id(0)

    @pl.when(place == 0)
    def _():
        acc[...] = jnp.zeros_like(acc)

    acc[...] += jnp.dot(x_ref[0], w_ref[...], preferred_element_type=jnp.float32)

    @pl.when(place == pl.num_programs(0) - 1)
    def _():
        out_ref[...] = acc[...].astype(out_ref.dtype)


def body(inputs, in_weight, out_weight, short_filter, decay, angle, residue, bias):
    rows, chans = inputs.shape
    place, blocks = lax.axis_index("seq"), lax.axis_size("seq")
    count = lax.axis_size("ch")
    col_start = lax.axis_index("ch") * chans
    own_weight = jnp.concatenate(
        [lax.dynamic_slice(in_weight[:, g, :], (0, col_start), (in_weight.shape[0], chans)) for g in range(3)],
        axis=1,
    )
    weight = lax.all_gather(own_weight, "seq", axis=0, tiled=True)
    second = lax.all_gather(out_weight, "seq", axis=0, tiled=True)

    rim = lax.ppermute(inputs[-2:], "seq", [(i, i + 1) for i in range(blocks - 1)])
    tokens = jnp.concatenate([inputs, rim, jnp.zeros((HALO - 2, chans), inputs.dtype)], axis=0)
    features = spread(tokens, "ch")

    rate, turn = decay.T, angle.T
    length = rows // SUB
    pack = lambda pair: jnp.concatenate(pair, axis=1)
    step = pack(powers(jnp.ones((1,), jnp.float32), rate, turn))[0]
    join = pack(powers(jnp.full((1,), length, jnp.float32), rate, turn))[0]
    reach = pack(powers((jnp.arange(SUB) * length).astype(jnp.float32), rate, turn))
    reach = reach.transpose(1, 0, 2)
    gap = place - 1 - jnp.arange(blocks)
    jump = pack(powers((jnp.maximum(gap, 0) * rows).astype(jnp.float32), rate, turn))
    jump = jnp.where((gap >= 0)[:, None, None], jump, 0.0).transpose(1, 0, 2)
    poles = jnp.concatenate([residue[0].T, residue[1].T], axis=0)

    f32 = jnp.float32
    whole = lambda shape: pl.BlockSpec(shape, lambda k: (0,) * len(shape))
    mixin, query, begin, final = pl.pallas_call(
        functools.partial(project_kernel, rows, chans),
        grid=(count,),
        in_specs=[
            pl.BlockSpec((1, rows + HALO, chans), lambda k: (k, 0, 0)),
            pl.BlockSpec((chans, 3 * chans), lambda k: (k, 0)),
            whole((9, chans)),
            whole((4, chans)),
            whole((4, chans)),
        ],
        out_specs=[
            whole((chans // LANES, rows, LANES)),
            whole((chans // LANES, rows, LANES)),
            whole((4, SUB, chans)),
            whole((4, chans)),
        ],
        out_shape=[
            jax.ShapeDtypeStruct((chans // LANES, rows, LANES), f32),
            jax.ShapeDtypeStruct((chans // LANES, rows, LANES), f32),
            jax.ShapeDtypeStruct((4, SUB, chans), f32),
            jax.ShapeDtypeStruct((4, chans), f32),
        ],
        scratch_shapes=[pltpu.VMEM((rows + HALO, 3 * chans), f32)],
        compiler_params=pltpu.CompilerParams(vmem_limit_bytes=VMEM),
        name="project",
    )(features, weight, short_filter.reshape(9, chans), step, join)

    states = spread(final, "seq")
    gated = pl.pallas_call(
        functools.partial(gate_kernel, rows, chans),
        out_shape=jax.ShapeDtypeStruct((rows, chans), jnp.bfloat16),
        scratch_shapes=[pltpu.VMEM((chans // LANES, rows, LANES), f32)],
        compiler_params=pltpu.CompilerParams(vmem_limit_bytes=VMEM),
        name="gate",
    )(states, jump, begin, reach, step, poles, bias[None, :], mixin, query)

    gathered = spread(gated, "ch")
    return pl.pallas_call(
        mix_kernel,
        grid=(count,),
        in_specs=[
            pl.BlockSpec((1, rows, chans), lambda k: (k, 0, 0)),
            pl.BlockSpec((chans, chans), lambda k: (k, 0)),
        ],
        out_specs=pl.BlockSpec((rows, chans), lambda k: (0, 0)),
        out_shape=jax.ShapeDtypeStruct((rows, chans), jnp.bfloat16),
        scratch_shapes=[pltpu.VMEM((rows, chans), f32)],
        compiler_params=pltpu.CompilerParams(vmem_limit_bytes=VMEM),
        name="mix",
    )(gathered, second)


def solution(mesh):
    placed = (
        P("seq", "ch"),
        P("seq", None, None),
        P("seq", "ch"),
        P(None, None, "ch"),
        P("ch", None),
        P("ch", None),
        P(None, "ch", None),
        P("ch"),
    )
    return jax.shard_map(
        body, mesh=mesh, in_specs=placed, out_specs=P("seq", "ch"), check_vma=False
    )
```

```python
import functools

import jax
import jax.numpy as jnp
from jax import lax
from jax.experimental import pallas as pl
from jax.experimental.pallas import tpu as pltpu
from jax.sharding import PartitionSpec as P

HALO = 16
LANES = 128
SUB = 8
VMEM = 58 * 1024 * 1024
SMALL = 16 * 1024 * 1024


def spread(x, axis):
    count = lax.axis_size(axis)
    return lax.all_to_all(
        jnp.broadcast_to(x[None], (count,) + x.shape), axis, 0, 0, tiled=True
    )


def powers(exponent, rate, turn):
    mag = jnp.exp(-exponent[:, None, None] * rate[None])
    phase = exponent[:, None, None] * turn[None]
    return mag * jnp.cos(phase), mag * jnp.sin(phase)


def project_kernel(half_ref, own_ref, other_ref, w_ref, keep_ref, send_ref, acc):
    place = pl.program_id(0)
    rows = own_ref.shape[1]

    @pl.when(place == 0)
    def _():
        acc[...] = jnp.zeros_like(acc)

    both = jnp.concatenate([own_ref[0], other_ref[0]], axis=0)
    acc[...] += jnp.dot(both, w_ref[...], preferred_element_type=jnp.float32)

    @pl.when(place == pl.num_programs(0) - 1)
    def _():
        keep_ref[...] = acc[:rows]
        send_ref[...] = acc[rows:].astype(send_ref.dtype)


def scan_kernel(
    rows, chans, keep_ref, more_ref, taps_ref, step_ref, join_ref, mixin_ref, query_ref, begin_ref, final_ref
):
    length = rows // SUB

    def filtered(branch):
        cols = slice(branch * chans, (branch + 1) * chans)
        total = keep_ref[:, cols] + more_ref[:, cols].astype(jnp.float32)
        total = total.astype(jnp.bfloat16).astype(jnp.float32)
        now = total[:rows]
        past = total[rows : rows + 8]
        one = jnp.concatenate([past[1:2], now[:-1]], axis=0)
        two = jnp.concatenate([past[0:2], now[:-2]], axis=0)
        tap = [taps_ref[3 * j + branch : 3 * j + branch + 1, :] for j in range(3)]
        return tap[0] * now + tap[1] * one + tap[2] * two

    query = filtered(0)
    mixin = filtered(1) * filtered(2)
    for q in range(chans // LANES):
        cols = slice(q * LANES, (q + 1) * LANES)
        query_ref[q] = query[:, cols]
        mixin_ref[q] = mixin[:, cols]
    for q in range(chans // LANES):
        cols = slice(q * LANES, (q + 1) * LANES)
        wide = lambda row: jnp.broadcast_to(row, (SUB, LANES))
        ar = [wide(step_ref[n : n + 1, cols]) for n in range(2)]
        ai = [wide(step_ref[2 + n : 3 + n, cols]) for n in range(2)]
        re = [jnp.zeros((SUB, LANES), jnp.float32)] * 2
        im = [jnp.zeros((SUB, LANES), jnp.float32)] * 2
        for i in range(length):
            u = mixin_ref[q, pl.ds(i, SUB, stride=length), :]
            for n in range(2):
                re[n], im[n] = ar[n] * re[n] - ai[n] * im[n] + u, ar[n] * im[n] + ai[n] * re[n]
        for n in range(2):
            jr = join_ref[n : n + 1, cols]
            ji = join_ref[2 + n : 3 + n, cols]
            er = jnp.zeros((1, LANES), jnp.float32)
            ei = jnp.zeros((1, LANES), jnp.float32)
            for b in range(SUB):
                begin_ref[n, b : b + 1, cols] = er
                begin_ref[2 + n, b : b + 1, cols] = ei
                er, ei = (
                    jr * er - ji * ei + re[n][b : b + 1],
                    jr * ei + ji * er + im[n][b : b + 1],
                )
            final_ref[n : n + 1, cols] = er
            final_ref[2 + n : 3 + n, cols] = ei


def gate_kernel(
    rows, chans, all_ref, jump_ref, begin_ref, reach_ref, step_ref, residue_ref, bias_ref, mixin_ref, query_ref, out_ref, long
):
    length = rows // SUB
    entry = []
    for n in range(2):
        fr, fi = all_ref[:, n, :], all_ref[:, 2 + n, :]
        cr, ci = jump_ref[n], jump_ref[2 + n]
        gr = jnp.sum(cr * fr - ci * fi, axis=0, keepdims=True)
        gi = jnp.sum(cr * fi + ci * fr, axis=0, keepdims=True)
        rr, ri = reach_ref[n], reach_ref[2 + n]
        entry.append((begin_ref[n] + rr * gr - ri * gi, begin_ref[2 + n] + rr * gi + ri * gr))
    for q in range(chans // LANES):
        cols = slice(q * LANES, (q + 1) * LANES)
        wide = lambda row: jnp.broadcast_to(row, (SUB, LANES))
        ar = [wide(step_ref[n : n + 1, cols]) for n in range(2)]
        ai = [wide(step_ref[2 + n : 3 + n, cols]) for n in range(2)]
        pr = [wide(residue_ref[n : n + 1, cols]) for n in range(2)]
        pi = [wide(residue_ref[2 + n : 3 + n, cols]) for n in range(2)]
        direct = wide(bias_ref[:, cols])
        re = [entry[n][0][:, cols] for n in range(2)]
        im = [entry[n][1][:, cols] for n in range(2)]
        for i in range(length):
            u = mixin_ref[q, pl.ds(i, SUB, stride=length), :]
            y = direct * u
            for n in range(2):
                re[n], im[n] = ar[n] * re[n] - ai[n] * im[n] + u, ar[n] * im[n] + ai[n] * re[n]
                y = y + (pr[n] * re[n] - pi[n] * im[n])
            long[q, pl.ds(i, SUB, stride=length), :] = y
        out_ref[:, cols] = (query_ref[q] * long[q]).astype(out_ref.dtype)


def mix_kernel(count, which_ref, *refs):
    x_refs, (w_ref, base_ref, out_ref, acc) = refs[:count], refs[count:]
    place = pl.program_id(0)

    @pl.when(place == 0)
    def _():
        acc[...] = base_ref[...].astype(jnp.float32)

    for j in range(count):

        @pl.when(place == j)
        def _(j=j):
            acc[...] += jnp.dot(x_refs[j][...], w_ref[...], preferred_element_type=jnp.float32)

    @pl.when(place == count - 1)
    def _():
        out_ref[...] = acc[...].astype(out_ref.dtype)


def mix(blocks, which, weight, base, dtype):
    rows, chans = blocks[0].shape
    cols = weight.shape[1]
    whole = lambda shape: pl.BlockSpec(shape, lambda k, w: (0,) * len(shape))
    return pl.pallas_call(
        functools.partial(mix_kernel, len(blocks)),
        grid_spec=pltpu.PrefetchScalarGridSpec(
            num_scalar_prefetch=1,
            grid=(len(blocks),),
            in_specs=[whole((rows, chans)) for _ in blocks]
            + [pl.BlockSpec((chans, cols), lambda k, w: (w[k], 0)), whole((rows, cols))],
            out_specs=whole((rows, cols)),
            scratch_shapes=[pltpu.VMEM((rows, cols), jnp.float32)],
        ),
        out_shape=jax.ShapeDtypeStruct((rows, cols), dtype),
        compiler_params=pltpu.CompilerParams(vmem_limit_bytes=SMALL),
        cost_estimate=pl.CostEstimate(
            flops=2 * len(blocks) * rows * chans * cols,
            bytes_accessed=2 * len(blocks) * chans * cols,
            transcendentals=0,
        ),
        name="mix",
    )(which, *blocks, weight, base)


def body(inputs, in_weight, out_weight, short_filter, decay, angle, residue, bias):
    rows, chans = inputs.shape
    place, blocks = lax.axis_index("seq"), lax.axis_size("seq")
    count = lax.axis_size("ch")
    col_start = lax.axis_index("ch") * chans
    own_weight = jnp.concatenate(
        [lax.dynamic_slice(in_weight[:, g, :], (0, col_start), (in_weight.shape[0], chans)) for g in range(3)],
        axis=1,
    )
    half = blocks // 2
    weight = lax.all_gather(
        own_weight,
        "seq",
        axis=0,
        tiled=True,
        axis_index_groups=[list(range(half)), list(range(half, blocks))],
    )
    second = lax.all_gather(out_weight, "seq", axis=0, tiled=True)

    rim = lax.ppermute(inputs[-2:], "seq", [(i, i + 1) for i in range(blocks - 1)])
    tokens = jnp.concatenate([inputs, rim, jnp.zeros((HALO - 2, chans), inputs.dtype)], axis=0)
    group = blocks // 4
    mirror = lambda s: (3 - s // group) * group + s % group
    swaps = []
    for c in range(count):
        for s in range(blocks):
            near = c // (count // 2) == s // half
            to = (c, s) if near else (count - 1 - c, mirror(s))
            swaps.append((c * blocks + s, to[0] * blocks + to[1]))
    features = spread(lax.ppermute(tokens, ("ch", "seq"), swaps), "ch")

    rate, turn = decay.T, angle.T
    length = rows // SUB
    pack = lambda pair: jnp.concatenate(pair, axis=1)
    step = pack(powers(jnp.ones((1,), jnp.float32), rate, turn))[0]
    join = pack(powers(jnp.full((1,), length, jnp.float32), rate, turn))[0]
    reach = pack(powers((jnp.arange(SUB) * length).astype(jnp.float32), rate, turn))
    reach = reach.transpose(1, 0, 2)
    gap = place - 1 - jnp.arange(blocks)
    jump = pack(powers((jnp.maximum(gap, 0) * rows).astype(jnp.float32), rate, turn))
    jump = jnp.where((gap >= 0)[:, None, None], jump, 0.0).transpose(1, 0, 2)
    poles = jnp.concatenate([residue[0].T, residue[1].T], axis=0)

    f32 = jnp.float32
    whole = lambda shape: pl.BlockSpec(shape, lambda k: (0,) * len(shape))
    quarter = count // 2
    padded = rows + HALO
    keep, send = pl.pallas_call(
        project_kernel,
        grid_spec=pltpu.PrefetchScalarGridSpec(
            num_scalar_prefetch=1,
            grid=(quarter,),
            in_specs=[
                pl.BlockSpec((1, padded, chans), lambda k, h: (h[0] * quarter + k, 0, 0)),
                pl.BlockSpec((1, padded, chans), lambda k, h: (count - 1 - h[0] * quarter - k, 0, 0)),
                pl.BlockSpec((chans, 3 * chans), lambda k, h: (k, 0)),
            ],
            out_specs=[
                pl.BlockSpec((padded, 3 * chans), lambda k, h: (0, 0)),
                pl.BlockSpec((padded, 3 * chans), lambda k, h: (0, 0)),
            ],
            scratch_shapes=[pltpu.VMEM((2 * padded, 3 * chans), f32)],
        ),
        out_shape=[
            jax.ShapeDtypeStruct((padded, 3 * chans), f32),
            jax.ShapeDtypeStruct((padded, 3 * chans), jnp.bfloat16),
        ],
        compiler_params=pltpu.CompilerParams(vmem_limit_bytes=VMEM),
        name="project",
    )((place // half).reshape(1).astype(jnp.int32), features, features, weight)
    more = lax.ppermute(send, "seq", [(s, mirror(s)) for s in range(blocks)])
    mixin, query, begin, final = pl.pallas_call(
        functools.partial(scan_kernel, rows, chans),
        out_shape=[
            jax.ShapeDtypeStruct((chans // LANES, rows, LANES), f32),
            jax.ShapeDtypeStruct((chans // LANES, rows, LANES), f32),
            jax.ShapeDtypeStruct((4, SUB, chans), f32),
            jax.ShapeDtypeStruct((4, chans), f32),
        ],
        compiler_params=pltpu.CompilerParams(vmem_limit_bytes=SMALL),
        name="scan",
    )(keep, more, short_filter.reshape(9, chans), step, join)

    states = spread(final, "seq")
    gated = pl.pallas_call(
        functools.partial(gate_kernel, rows, chans),
        out_shape=jax.ShapeDtypeStruct((rows, chans), jnp.bfloat16),
        scratch_shapes=[pltpu.VMEM((chans // LANES, rows, LANES), f32)],
        compiler_params=pltpu.CompilerParams(vmem_limit_bytes=SMALL),
        name="gate",
    )(states, jump, begin, reach, step, poles, bias[None, :], mixin, query)

    here = lax.axis_index("ch")
    up = [(c, (c + 1) % count) for c in range(count)]
    down = [(c, (c - 1) % count) for c in range(count)]
    arrived, origin = [gated], [here]
    below = above = gated
    for hop in range(1, count // 2 + 1):
        below = lax.ppermute(below, "ch", up)
        arrived.append(below)
        origin.append(here - hop)
        if 2 * hop < count:
            above = lax.ppermute(above, "ch", down)
            arrived.append(above)
            origin.append(here + hop)
    which = jnp.stack([lax.rem(o + count, count) for o in origin]).astype(jnp.int32)
    base = jnp.zeros((rows, chans), f32)
    first = mix(arrived[:5], which[:5], second, base, f32)
    return mix(arrived[5:], which[5:], second, first, jnp.bfloat16)


def solution(mesh):
    placed = (
        P("seq", "ch"),
        P("seq", None, None),
        P("seq", "ch"),
        P(None, None, "ch"),
        P("ch", None),
        P("ch", None),
        P(None, "ch", None),
        P("ch"),
    )
    return jax.shard_map(
        body, mesh=mesh, in_specs=placed, out_specs=P("seq", "ch"), check_vma=False
    )
```

```python
import functools

import jax
import jax.numpy as jnp
from jax import lax
from jax.experimental import pallas as pl
from jax.experimental.pallas import tpu as pltpu
from jax.sharding import PartitionSpec as P

HALO = 16
LANES = 128
SUB = 8
VMEM = 58 * 1024 * 1024
SMALL = 16 * 1024 * 1024


def spread(x, axis):
    count = lax.axis_size(axis)
    return lax.all_to_all(
        jnp.broadcast_to(x[None], (count,) + x.shape), axis, 0, 0, tiled=True
    )


def ring_hops(count):
    hops = [0]
    for hop in range(1, count // 2 + 1):
        hops += [-hop, hop] if 2 * hop < count else [-hop]
    return hops


def ring(x, axis):
    count = lax.axis_size(axis)
    up = [(c, (c + 1) % count) for c in range(count)]
    down = [(c, (c - 1) % count) for c in range(count)]
    arrived = [x]
    below = above = x
    for hop in range(1, count // 2 + 1):
        below = lax.ppermute(below, axis, up)
        arrived.append(below)
        if 2 * hop < count:
            above = lax.ppermute(above, axis, down)
            arrived.append(above)
    return arrived


def powers(exponent, rate, turn):
    mag = jnp.exp(-exponent[:, None, None] * rate[None])
    phase = exponent[:, None, None] * turn[None]
    return mag * jnp.cos(phase), mag * jnp.sin(phase)


def project_kernel(count, place_ref, *refs):
    x_refs, (w_ref, keep_ref, send_ref, features, acc) = refs[:count], refs[count:]
    step = pl.program_id(0)
    quarter = pl.num_programs(0)
    rows = x_refs[0].shape[0]
    half, here = place_ref[0], place_ref[1]

    @pl.when(step == 0)
    def _():
        for x_ref, hop in zip(x_refs, ring_hops(count)):
            features[lax.rem(here + hop + count, count)] = x_ref[...]
        acc[...] = jnp.zeros_like(acc)

    own = features[half * quarter + step]
    other = features[count - 1 - half * quarter - step]
    both = jnp.concatenate([own, other], axis=0)
    acc[...] += jnp.dot(both, w_ref[...], preferred_element_type=jnp.float32)

    @pl.when(step == quarter - 1)
    def _():
        keep_ref[...] = acc[:rows]
        send_ref[...] = acc[rows:].astype(send_ref.dtype)


def scan_kernel(
    rows, chans, keep_ref, more_ref, taps_ref, step_ref, join_ref, mixin_ref, query_ref, begin_ref, final_ref
):
    length = rows // SUB

    def filtered(branch):
        cols = slice(branch * chans, (branch + 1) * chans)
        total = keep_ref[:, cols] + more_ref[:, cols].astype(jnp.float32)
        now = total[:rows]
        past = total[rows : rows + 8]
        one = jnp.concatenate([past[1:2], now[:-1]], axis=0)
        two = jnp.concatenate([past[0:2], now[:-2]], axis=0)
        tap = [taps_ref[3 * j + branch : 3 * j + branch + 1, :] for j in range(3)]
        return tap[0] * now + tap[1] * one + tap[2] * two

    query = filtered(0)
    mixin = filtered(1) * filtered(2)
    for q in range(chans // LANES):
        cols = slice(q * LANES, (q + 1) * LANES)
        query_ref[q] = query[:, cols]
        mixin_ref[q] = mixin[:, cols]
    for q in range(chans // LANES):
        cols = slice(q * LANES, (q + 1) * LANES)
        wide = lambda row: jnp.broadcast_to(row, (SUB, LANES))
        ar = [wide(step_ref[n : n + 1, cols]) for n in range(2)]
        ai = [wide(step_ref[2 + n : 3 + n, cols]) for n in range(2)]
        re = [jnp.zeros((SUB, LANES), jnp.float32)] * 2
        im = [jnp.zeros((SUB, LANES), jnp.float32)] * 2
        for i in range(length):
            u = mixin_ref[q, pl.ds(i, SUB, stride=length), :]
            for n in range(2):
                re[n], im[n] = ar[n] * re[n] - ai[n] * im[n] + u, ar[n] * im[n] + ai[n] * re[n]
        for n in range(2):
            jr = join_ref[n : n + 1, cols]
            ji = join_ref[2 + n : 3 + n, cols]
            er = jnp.zeros((1, LANES), jnp.float32)
            ei = jnp.zeros((1, LANES), jnp.float32)
            for b in range(SUB):
                begin_ref[n, b : b + 1, cols] = er
                begin_ref[2 + n, b : b + 1, cols] = ei
                er, ei = (
                    jr * er - ji * ei + re[n][b : b + 1],
                    jr * ei + ji * er + im[n][b : b + 1],
                )
            final_ref[n : n + 1, cols] = er
            final_ref[2 + n : 3 + n, cols] = ei


def gate_kernel(
    rows, chans, all_ref, jump_ref, begin_ref, reach_ref, step_ref, residue_ref, bias_ref, mixin_ref, query_ref, out_ref, long
):
    length = rows // SUB
    entry = []
    for n in range(2):
        fr, fi = all_ref[:, n, :], all_ref[:, 2 + n, :]
        cr, ci = jump_ref[n], jump_ref[2 + n]
        gr = jnp.sum(cr * fr - ci * fi, axis=0, keepdims=True)
        gi = jnp.sum(cr * fi + ci * fr, axis=0, keepdims=True)
        rr, ri = reach_ref[n], reach_ref[2 + n]
        entry.append((begin_ref[n] + rr * gr - ri * gi, begin_ref[2 + n] + rr * gi + ri * gr))
    for q in range(chans // LANES):
        cols = slice(q * LANES, (q + 1) * LANES)
        wide = lambda row: jnp.broadcast_to(row, (SUB, LANES))
        ar = [wide(step_ref[n : n + 1, cols]) for n in range(2)]
        ai = [wide(step_ref[2 + n : 3 + n, cols]) for n in range(2)]
        pr = [wide(residue_ref[n : n + 1, cols]) for n in range(2)]
        pi = [wide(residue_ref[2 + n : 3 + n, cols]) for n in range(2)]
        direct = wide(bias_ref[:, cols])
        re = [entry[n][0][:, cols] for n in range(2)]
        im = [entry[n][1][:, cols] for n in range(2)]
        for i in range(length):
            u = mixin_ref[q, pl.ds(i, SUB, stride=length), :]
            y = direct * u
            for n in range(2):
                re[n], im[n] = ar[n] * re[n] - ai[n] * im[n] + u, ar[n] * im[n] + ai[n] * re[n]
                y = y + (pr[n] * re[n] - pi[n] * im[n])
            long[q, pl.ds(i, SUB, stride=length), :] = y
        out_ref[:, cols] = (query_ref[q] * long[q]).astype(out_ref.dtype)


def mix_kernel(count, which_ref, *refs):
    x_refs, (w_ref, out_ref, acc) = refs[:count], refs[count:]
    place = pl.program_id(0)

    @pl.when(place == 0)
    def _():
        acc[...] = jnp.zeros_like(acc)

    for j in range(count):

        @pl.when(place == j)
        def _(j=j):
            acc[...] += jnp.dot(x_refs[j][...], w_ref[...], preferred_element_type=jnp.float32)

    @pl.when(place == count - 1)
    def _():
        out_ref[...] = acc[...].astype(out_ref.dtype)


def mix(blocks, which, weight):
    rows, chans = blocks[0].shape
    cols = weight.shape[1]
    whole = lambda shape: pl.BlockSpec(shape, lambda k, w: (0,) * len(shape))
    return pl.pallas_call(
        functools.partial(mix_kernel, len(blocks)),
        grid_spec=pltpu.PrefetchScalarGridSpec(
            num_scalar_prefetch=1,
            grid=(len(blocks),),
            in_specs=[whole((rows, chans)) for _ in blocks]
            + [pl.BlockSpec((chans, cols), lambda k, w: (w[k], 0))],
            out_specs=whole((rows, cols)),
            scratch_shapes=[pltpu.VMEM((rows, cols), jnp.float32)],
        ),
        out_shape=jax.ShapeDtypeStruct((rows, cols), jnp.bfloat16),
        compiler_params=pltpu.CompilerParams(vmem_limit_bytes=VMEM),
        name="mix",
    )(which, *blocks, weight)


def body(inputs, in_weight, out_weight, short_filter, decay, angle, residue, bias):
    rows, chans = inputs.shape
    place, blocks = lax.axis_index("seq"), lax.axis_size("seq")
    count = lax.axis_size("ch")
    col_start = lax.axis_index("ch") * chans
    own_weight = jnp.concatenate(
        [lax.dynamic_slice(in_weight[:, g, :], (0, col_start), (in_weight.shape[0], chans)) for g in range(3)],
        axis=1,
    )
    half = blocks // 2
    weight = lax.all_gather(
        own_weight,
        "seq",
        axis=0,
        tiled=True,
        axis_index_groups=[list(range(half)), list(range(half, blocks))],
    )
    second = lax.all_gather(out_weight, "seq", axis=0, tiled=True)

    rim = lax.ppermute(inputs[-2:], "seq", [(i, i + 1) for i in range(blocks - 1)])
    tokens = jnp.concatenate([inputs, rim, jnp.zeros((HALO - 2, chans), inputs.dtype)], axis=0)
    group = blocks // 4
    mirror = lambda s: (3 - s // group) * group + s % group
    swaps = []
    for c in range(count):
        for s in range(blocks):
            near = c // (count // 2) == s // half
            to = (c, s) if near else (count - 1 - c, mirror(s))
            swaps.append((c * blocks + s, to[0] * blocks + to[1]))
    features = ring(lax.ppermute(tokens, ("ch", "seq"), swaps), "ch")
    here = lax.axis_index("ch")

    rate, turn = decay.T, angle.T
    length = rows // SUB
    pack = lambda pair: jnp.concatenate(pair, axis=1)
    step = pack(powers(jnp.ones((1,), jnp.float32), rate, turn))[0]
    join = pack(powers(jnp.full((1,), length, jnp.float32), rate, turn))[0]
    reach = pack(powers((jnp.arange(SUB) * length).astype(jnp.float32), rate, turn))
    reach = reach.transpose(1, 0, 2)
    gap = place - 1 - jnp.arange(blocks)
    jump = pack(powers((jnp.maximum(gap, 0) * rows).astype(jnp.float32), rate, turn))
    jump = jnp.where((gap >= 0)[:, None, None], jump, 0.0).transpose(1, 0, 2)
    poles = jnp.concatenate([residue[0].T, residue[1].T], axis=0)

    f32 = jnp.float32
    whole = lambda shape: pl.BlockSpec(shape, lambda k: (0,) * len(shape))
    quarter = count // 2
    padded = rows + HALO
    keep, send = pl.pallas_call(
        functools.partial(project_kernel, count),
        grid_spec=pltpu.PrefetchScalarGridSpec(
            num_scalar_prefetch=1,
            grid=(quarter,),
            in_specs=[pl.BlockSpec((padded, chans), lambda k, h: (0, 0))] * count
            + [pl.BlockSpec((chans, 3 * chans), lambda k, h: (k, 0))],
            out_specs=[
                pl.BlockSpec((padded, 3 * chans), lambda k, h: (0, 0)),
                pl.BlockSpec((padded, 3 * chans), lambda k, h: (0, 0)),
            ],
            scratch_shapes=[
                pltpu.VMEM((count, padded, chans), jnp.bfloat16),
                pltpu.VMEM((2 * padded, 3 * chans), f32),
            ],
        ),
        out_shape=[
            jax.ShapeDtypeStruct((padded, 3 * chans), f32),
            jax.ShapeDtypeStruct((padded, 3 * chans), jnp.bfloat16),
        ],
        compiler_params=pltpu.CompilerParams(vmem_limit_bytes=VMEM),
        name="project",
    )(jnp.stack([place // half, here]).astype(jnp.int32), *features, weight)
    more = lax.ppermute(send, "seq", [(s, mirror(s)) for s in range(blocks)])
    mixin, query, begin, final = pl.pallas_call(
        functools.partial(scan_kernel, rows, chans),
        out_shape=[
            jax.ShapeDtypeStruct((chans // LANES, rows, LANES), f32),
            jax.ShapeDtypeStruct((chans // LANES, rows, LANES), f32),
            jax.ShapeDtypeStruct((4, SUB, chans), f32),
            jax.ShapeDtypeStruct((4, chans), f32),
        ],
        compiler_params=pltpu.CompilerParams(vmem_limit_bytes=SMALL),
        name="scan",
    )(keep, more, short_filter.reshape(9, chans), step, join)

    states = spread(final, "seq")
    gated = pl.pallas_call(
        functools.partial(gate_kernel, rows, chans),
        out_shape=jax.ShapeDtypeStruct((rows, chans), jnp.bfloat16),
        scratch_shapes=[pltpu.VMEM((chans // LANES, rows, LANES), f32)],
        compiler_params=pltpu.CompilerParams(vmem_limit_bytes=SMALL),
        name="gate",
    )(states, jump, begin, reach, step, poles, bias[None, :], mixin, query)

    which = jnp.stack([lax.rem(here + hop + count, count) for hop in ring_hops(count)])
    return mix(ring(gated, "ch"), which.astype(jnp.int32), second)


def solution(mesh):
    placed = (
        P("seq", "ch"),
        P("seq", None, None),
        P("seq", "ch"),
        P(None, None, "ch"),
        P("ch", None),
        P("ch", None),
        P(None, "ch", None),
        P("ch"),
    )
    return jax.shard_map(
        body, mesh=mesh, in_specs=placed, out_specs=P("seq", "ch"), check_vma=False
    )
```

```python
import functools

import jax
import jax.numpy as jnp
from jax import lax
from jax.experimental import pallas as pl
from jax.experimental.pallas import tpu as pltpu
from jax.sharding import PartitionSpec as P

HALO = 16
LANES = 128
SUB = 8
VMEM = 24 * 1024 * 1024


def spread(x, axis):
    count = lax.axis_size(axis)
    return lax.all_to_all(
        jnp.broadcast_to(x[None], (count,) + x.shape), axis, 0, 0, tiled=True
    )


def ring_hops(count):
    hops = [0]
    for hop in range(1, count // 2 + 1):
        hops += [-hop, hop] if 2 * hop < count else [-hop]
    return hops


def ring(x, axis):
    count = lax.axis_size(axis)
    up = [(c, (c + 1) % count) for c in range(count)]
    down = [(c, (c - 1) % count) for c in range(count)]
    arrived = [x]
    below = above = x
    for hop in range(1, count // 2 + 1):
        below = lax.ppermute(below, axis, up)
        arrived.append(below)
        if 2 * hop < count:
            above = lax.ppermute(above, axis, down)
            arrived.append(above)
    return arrived


def powers(exponent, rate, turn):
    mag = jnp.exp(-exponent[:, None, None] * rate[None])
    phase = exponent[:, None, None] * turn[None]
    return mag * jnp.cos(phase), mag * jnp.sin(phase)


def fetch(w_ref, w, sems, starts, sizes):
    copies = []
    for j, (start, size) in enumerate(zip(starts, sizes)):
        at = sum(sizes[:j])
        copies.append(
            pltpu.make_async_copy(w_ref.at[:, pl.ds(start, size)], w.at[:, pl.ds(at, size)], sems.at[j])
        )
        copies[-1].start()
    return copies


def product(lhs_ref, w, copies, chans, keep_ref, send_ref):
    sides, rows, depth = lhs_ref.shape
    both = lhs_ref[...].reshape(sides * rows, depth)
    for j, copy in enumerate(copies):
        copy.wait()
        cols = slice(j * chans, (j + 1) * chans)
        part = jnp.dot(both, w[:, cols], preferred_element_type=jnp.float32)
        keep_ref[:, cols] = part[:rows]
        send_ref[:, cols] = part[rows:].astype(send_ref.dtype)


def mixin_project_kernel(count, place_ref, *refs):
    x_refs, (w_ref, keep_ref, send_ref, lhs_ref, w, sems) = refs[:count], refs[count:]
    chans = x_refs[0].shape[1]
    copies = fetch(w_ref, w, sems, (chans, 2 * chans), (chans, chans))
    half, here = place_ref[0], place_ref[1]
    for x_ref, hop in zip(x_refs, ring_hops(count)):
        origin = lax.rem(here + hop + count, count)
        side = jnp.where(lax.rem(origin, 2) == half, 0, 1)
        at = pl.multiple_of(lax.div(origin, 2) * chans, chans)
        lhs_ref[side, :, pl.ds(at, chans)] = x_ref[...]
    product(lhs_ref, w, copies, chans, keep_ref, send_ref)


def query_project_kernel(lhs_ref, w_ref, keep_ref, send_ref, w, sems):
    chans = keep_ref.shape[1]
    copies = fetch(w_ref, w, sems, (0,), (chans,))
    product(lhs_ref, w, copies, chans, keep_ref, send_ref)


def short_conv(rows, branch, total, taps_ref):
    now = total[:rows]
    past = total[rows : rows + 8]
    one = jnp.concatenate([past[1:2], now[:-1]], axis=0)
    two = jnp.concatenate([past[0:2], now[:-2]], axis=0)
    tap = [taps_ref[3 * j + branch : 3 * j + branch + 1, :] for j in range(3)]
    return tap[0] * now + tap[1] * one + tap[2] * two


def scan_kernel(
    rows, chans, keep_ref, more_ref, taps_ref, step_ref, join_ref, mixin_ref, begin_ref, final_ref
):
    length = rows // SUB

    def filtered(branch):
        cols = slice((branch - 1) * chans, branch * chans)
        total = keep_ref[:, cols] + more_ref[:, cols].astype(jnp.float32)
        return short_conv(rows, branch, total, taps_ref)

    mixin = filtered(1) * filtered(2)
    for q in range(chans // LANES):
        mixin_ref[q] = mixin[:, q * LANES : (q + 1) * LANES]
    for q in range(chans // LANES):
        cols = slice(q * LANES, (q + 1) * LANES)
        wide = lambda row: jnp.broadcast_to(row, (SUB, LANES))
        ar = [wide(step_ref[n : n + 1, cols]) for n in range(2)]
        ai = [wide(step_ref[2 + n : 3 + n, cols]) for n in range(2)]
        re = [jnp.zeros((SUB, LANES), jnp.float32)] * 2
        im = [jnp.zeros((SUB, LANES), jnp.float32)] * 2
        for i in range(length):
            u = mixin_ref[q, pl.ds(i, SUB, stride=length), :]
            for n in range(2):
                re[n], im[n] = ar[n] * re[n] - ai[n] * im[n] + u, ar[n] * im[n] + ai[n] * re[n]
        for n in range(2):
            jr = join_ref[n : n + 1, cols]
            ji = join_ref[2 + n : 3 + n, cols]
            er = jnp.zeros((1, LANES), jnp.float32)
            ei = jnp.zeros((1, LANES), jnp.float32)
            for b in range(SUB):
                begin_ref[n, b : b + 1, cols] = er
                begin_ref[2 + n, b : b + 1, cols] = ei
                er, ei = (
                    jr * er - ji * ei + re[n][b : b + 1],
                    jr * ei + ji * er + im[n][b : b + 1],
                )
            final_ref[n : n + 1, cols] = er
            final_ref[2 + n : 3 + n, cols] = ei


def gate_kernel(
    rows, chans, all_ref, jump_ref, begin_ref, reach_ref, step_ref, residue_ref, bias_ref, mixin_ref, keep_ref, more_ref, taps_ref, out_ref, long
):
    query = short_conv(rows, 0, keep_ref[...] + more_ref[...].astype(jnp.float32), taps_ref)
    length = rows // SUB
    entry = []
    for n in range(2):
        fr, fi = all_ref[:, n, :], all_ref[:, 2 + n, :]
        cr, ci = jump_ref[n], jump_ref[2 + n]
        gr = jnp.sum(cr * fr - ci * fi, axis=0, keepdims=True)
        gi = jnp.sum(cr * fi + ci * fr, axis=0, keepdims=True)
        rr, ri = reach_ref[n], reach_ref[2 + n]
        entry.append((begin_ref[n] + rr * gr - ri * gi, begin_ref[2 + n] + rr * gi + ri * gr))
    for q in range(chans // LANES):
        cols = slice(q * LANES, (q + 1) * LANES)
        wide = lambda row: jnp.broadcast_to(row, (SUB, LANES))
        ar = [wide(step_ref[n : n + 1, cols]) for n in range(2)]
        ai = [wide(step_ref[2 + n : 3 + n, cols]) for n in range(2)]
        pr = [wide(residue_ref[n : n + 1, cols]) for n in range(2)]
        pi = [wide(residue_ref[2 + n : 3 + n, cols]) for n in range(2)]
        direct = wide(bias_ref[:, cols])
        re = [entry[n][0][:, cols] for n in range(2)]
        im = [entry[n][1][:, cols] for n in range(2)]
        for i in range(length):
            u = mixin_ref[q, pl.ds(i, SUB, stride=length), :]
            y = direct * u
            for n in range(2):
                re[n], im[n] = ar[n] * re[n] - ai[n] * im[n] + u, ar[n] * im[n] + ai[n] * re[n]
                y = y + (pr[n] * re[n] - pi[n] * im[n])
            long[q, pl.ds(i, SUB, stride=length), :] = y
        out_ref[:, cols] = (query[:, cols] * long[q]).astype(out_ref.dtype)


def mix_kernel(count, which_ref, *refs):
    x_refs, (w_ref, base_ref, out_ref, w, sems) = refs[:count], refs[count:]
    chans = x_refs[0].shape[1]
    copies = []
    for j in range(count):
        at = pl.multiple_of(which_ref[j] * chans, chans)
        copies.append(pltpu.make_async_copy(w_ref.at[pl.ds(at, chans)], w.at[j], sems.at[j]))
        copies[-1].start()
    total = base_ref[...]
    for j in range(count):
        copies[j].wait()
        total = total + jnp.dot(x_refs[j][...], w[j], preferred_element_type=jnp.float32)
    out_ref[...] = total.astype(out_ref.dtype)


IN_VMEM = pl.BlockSpec(memory_space=pltpu.VMEM)
IN_SMEM = pl.BlockSpec(memory_space=pltpu.SMEM)
IN_HBM = pl.BlockSpec(memory_space=pltpu.HBM)
in_hbm = functools.partial(pltpu.with_memory_space_constraint, memory_space=pltpu.HBM)


def mix(blocks, which, weight, base, dtype):
    rows, chans = blocks[0].shape
    cols = weight.shape[1]
    count = len(blocks)
    return pl.pallas_call(
        functools.partial(mix_kernel, count),
        in_specs=[IN_SMEM] + [IN_VMEM] * count + [IN_HBM, IN_VMEM],
        out_shape=jax.ShapeDtypeStruct((rows, cols), dtype),
        scratch_shapes=[
            pltpu.VMEM((count, chans, cols), weight.dtype),
            pltpu.SemaphoreType.DMA((count,)),
        ],
        compiler_params=pltpu.CompilerParams(vmem_limit_bytes=VMEM),
        cost_estimate=pl.CostEstimate(
            flops=2 * count * rows * chans * cols,
            bytes_accessed=2 * count * chans * cols,
            transcendentals=0,
        ),
        name="mix",
    )(which, *blocks, in_hbm(weight), base)


def body(inputs, in_weight, out_weight, short_filter, decay, angle, residue, bias):
    rows, chans = inputs.shape
    place, blocks = lax.axis_index("seq"), lax.axis_size("seq")
    count = lax.axis_size("ch")
    col_start = lax.axis_index("ch") * chans
    near = [(s % 8) // 4 for s in range(blocks)]
    mirror = [s + 6 - 4 * ((s % 8) // 2) for s in range(blocks)]
    cut = lax.dynamic_slice(in_weight, (0, 0, col_start), (in_weight.shape[0], 3, chans))
    own_weight = jnp.concatenate([cut[:, g] for g in range(3)], axis=1)
    weight = lax.all_gather(
        own_weight,
        "seq",
        axis=0,
        tiled=True,
        axis_index_groups=[[s for s in range(blocks) if near[s] == h] for h in range(2)],
    )
    second = lax.all_gather(out_weight, "seq", axis=0, tiled=True)

    rim = lax.ppermute(inputs[-2:], "seq", [(i, i + 1) for i in range(blocks - 1)])
    tokens = jnp.concatenate([inputs, rim, jnp.zeros((HALO - 2, chans), inputs.dtype)], axis=0)
    swaps = []
    for c in range(count):
        for s in range(blocks):
            to = (c, s) if c % 2 == near[s] else (c ^ 1, mirror[s])
            swaps.append((c * blocks + s, to[0] * blocks + to[1]))
    features = ring(lax.ppermute(tokens, ("ch", "seq"), swaps), "ch")
    here = lax.axis_index("ch")

    rate, turn = decay.T, angle.T
    length = rows // SUB
    pack = lambda pair: jnp.concatenate(pair, axis=1)
    step = pack(powers(jnp.ones((1,), jnp.float32), rate, turn))[0]
    join = pack(powers(jnp.full((1,), length, jnp.float32), rate, turn))[0]
    reach = pack(powers((jnp.arange(SUB) * length).astype(jnp.float32), rate, turn))
    reach = reach.transpose(1, 0, 2)
    gap = place - 1 - jnp.arange(blocks)
    jump = pack(powers((jnp.maximum(gap, 0) * rows).astype(jnp.float32), rate, turn))
    jump = jnp.where((gap >= 0)[:, None, None], jump, 0.0).transpose(1, 0, 2)
    poles = jnp.concatenate([residue[0].T, residue[1].T], axis=0)

    f32, b16 = jnp.float32, jnp.bfloat16
    padded, depth = rows + HALO, chans * count // 2
    params = pltpu.CompilerParams(vmem_limit_bytes=VMEM)
    shape = jax.ShapeDtypeStruct
    half = lax.rem(place, 8) // 4
    keep, send, lhs = pl.pallas_call(
        functools.partial(mixin_project_kernel, count),
        in_specs=[IN_SMEM] + [IN_VMEM] * count + [IN_HBM],
        out_shape=[
            shape((padded, 2 * chans), f32),
            shape((padded, 2 * chans), b16),
            shape((2, padded, depth), b16),
        ],
        scratch_shapes=[pltpu.VMEM((depth, 2 * chans), b16), pltpu.SemaphoreType.DMA((2,))],
        compiler_params=params,
        cost_estimate=pl.CostEstimate(
            flops=8 * padded * depth * chans, bytes_accessed=4 * depth * chans, transcendentals=0
        ),
        name="project_mixin",
    )(jnp.stack([half, here]).astype(jnp.int32), *features, in_hbm(weight))
    pairs = [(s, mirror[s]) for s in range(blocks)]
    more = lax.ppermute(send, "seq", pairs)
    query_keep, query_send = pl.pallas_call(
        query_project_kernel,
        in_specs=[IN_VMEM, IN_HBM],
        out_shape=[shape((padded, chans), f32), shape((padded, chans), b16)],
        scratch_shapes=[pltpu.VMEM((depth, chans), b16), pltpu.SemaphoreType.DMA((1,))],
        compiler_params=params,
        cost_estimate=pl.CostEstimate(
            flops=4 * padded * depth * chans, bytes_accessed=2 * depth * chans, transcendentals=0
        ),
        name="project_query",
    )(lhs, in_hbm(weight))
    taps = short_filter.reshape(9, chans)
    mixin, begin, final = pl.pallas_call(
        functools.partial(scan_kernel, rows, chans),
        out_shape=[
            shape((chans // LANES, rows, LANES), f32),
            shape((4, SUB, chans), f32),
            shape((4, chans), f32),
        ],
        compiler_params=params,
        name="scan",
    )(keep, more, taps, step, join)
    query_more = lax.ppermute(query_send, "seq", pairs)

    states = spread(final, "seq")
    gated = pl.pallas_call(
        functools.partial(gate_kernel, rows, chans),
        out_shape=shape((rows, chans), b16),
        scratch_shapes=[pltpu.VMEM((chans // LANES, rows, LANES), f32)],
        compiler_params=params,
        name="gate",
    )(states, jump, begin, reach, step, poles, bias[None, :], mixin, query_keep, query_more, taps)

    which = jnp.stack([lax.rem(here + hop + count, count) for hop in ring_hops(count)])
    which = which.astype(jnp.int32)
    parts = ring(gated, "ch")
    first = mix(parts[:-1], which[:-1], second, jnp.zeros((rows, chans), f32), f32)
    return mix(parts[-1:], which[-1:], second, first, b16)


def solution(mesh):
    placed = (
        P("seq", "ch"),
        P("seq", None, None),
        P("seq", "ch"),
        P(None, None, "ch"),
        P("ch", None),
        P("ch", None),
        P(None, "ch", None),
        P("ch"),
    )
    return jax.shard_map(
        body, mesh=mesh, in_specs=placed, out_specs=P("seq", "ch"), check_vma=False
    )
```

```python
import functools

import jax
import jax.numpy as jnp
from jax import lax
from jax.experimental import pallas as pl
from jax.experimental.pallas import tpu as pltpu
from jax.sharding import PartitionSpec as P

HALO = 16
LANES = 128
SUB = 8
VMEM = 24 * 1024 * 1024


def spread(x, axis):
    count = lax.axis_size(axis)
    return lax.all_to_all(
        jnp.broadcast_to(x[None], (count,) + x.shape), axis, 0, 0, tiled=True
    )


def ring_hops(count):
    hops = [0]
    for hop in range(1, count // 2 + 1):
        hops += [-hop, hop] if 2 * hop < count else [-hop]
    return hops


def ring(x, axis):
    count = lax.axis_size(axis)
    up = [(c, (c + 1) % count) for c in range(count)]
    down = [(c, (c - 1) % count) for c in range(count)]
    arrived = [x]
    below = above = x
    for hop in range(1, count // 2 + 1):
        below = lax.ppermute(below, axis, up)
        arrived.append(below)
        if 2 * hop < count:
            above = lax.ppermute(above, axis, down)
            arrived.append(above)
    return arrived


def powers(exponent, rate, turn):
    mag = jnp.exp(-exponent[:, None, None] * rate[None])
    phase = exponent[:, None, None] * turn[None]
    return mag * jnp.cos(phase), mag * jnp.sin(phase)


def fetch(w_ref, w, sems, starts, sizes):
    copies = []
    for j, (start, size) in enumerate(zip(starts, sizes)):
        at = sum(sizes[:j])
        copies.append(
            pltpu.make_async_copy(w_ref.at[:, pl.ds(start, size)], w.at[:, pl.ds(at, size)], sems.at[j])
        )
        copies[-1].start()
    return copies


def product(lhs_ref, w, copies, chans, keep_ref, send_ref):
    sides, rows, depth = lhs_ref.shape
    both = lhs_ref[...].reshape(sides * rows, depth)
    for j, copy in enumerate(copies):
        copy.wait()
        cols = slice(j * chans, (j + 1) * chans)
        part = jnp.dot(both, w[:, cols], preferred_element_type=jnp.float32)
        keep_ref[:, cols] = part[:rows]
        send_ref[:, cols] = part[rows:].astype(send_ref.dtype)


def mixin_project_kernel(count, place_ref, *refs):
    x_refs, (w_ref, keep_ref, send_ref, lhs_ref, w, sems) = refs[:count], refs[count:]
    chans = x_refs[0].shape[1]
    copies = fetch(w_ref, w, sems, (chans, 2 * chans), (chans, chans))
    half, here = place_ref[0], place_ref[1]
    for x_ref, hop in zip(x_refs, ring_hops(count)):
        origin = lax.rem(here + hop + count, count)
        side = jnp.where(lax.rem(origin, 2) == half, 0, 1)
        at = pl.multiple_of(lax.div(origin, 2) * chans, chans)
        lhs_ref[side, :, pl.ds(at, chans)] = x_ref[...]
    product(lhs_ref, w, copies, chans, keep_ref, send_ref)


def query_project_kernel(lhs_ref, w_ref, keep_ref, send_ref, w, sems):
    chans = keep_ref.shape[1]
    copies = fetch(w_ref, w, sems, (0,), (chans,))
    product(lhs_ref, w, copies, chans, keep_ref, send_ref)


def short_conv(rows, branch, total, taps_ref):
    now = total[:rows]
    past = total[rows : rows + 8]
    one = jnp.concatenate([past[1:2], now[:-1]], axis=0)
    two = jnp.concatenate([past[0:2], now[:-2]], axis=0)
    tap = [taps_ref[3 * j + branch : 3 * j + branch + 1, :] for j in range(3)]
    return tap[0] * now + tap[1] * one + tap[2] * two


def scan_kernel(
    rows,
    chans,
    keep_ref,
    more_ref,
    query_ref,
    taps_ref,
    step_ref,
    join_ref,
    mixin_ref,
    begin_ref,
    final_ref,
    send_ref,
):
    send_ref[...] = query_ref[...]
    length = rows // SUB

    def filtered(branch):
        cols = slice((branch - 1) * chans, branch * chans)
        total = keep_ref[:, cols] + more_ref[:, cols].astype(jnp.float32)
        return short_conv(rows, branch, total, taps_ref)

    mixin = filtered(1) * filtered(2)
    for q in range(chans // LANES):
        mixin_ref[q] = mixin[:, q * LANES : (q + 1) * LANES]
    for q in range(chans // LANES):
        cols = slice(q * LANES, (q + 1) * LANES)
        wide = lambda row: jnp.broadcast_to(row, (SUB, LANES))
        ar = [wide(step_ref[n : n + 1, cols]) for n in range(2)]
        ai = [wide(step_ref[2 + n : 3 + n, cols]) for n in range(2)]
        re = [jnp.zeros((SUB, LANES), jnp.float32)] * 2
        im = [jnp.zeros((SUB, LANES), jnp.float32)] * 2
        for i in range(length):
            u = mixin_ref[q, pl.ds(i, SUB, stride=length), :]
            for n in range(2):
                re[n], im[n] = ar[n] * re[n] - ai[n] * im[n] + u, ar[n] * im[n] + ai[n] * re[n]
        for n in range(2):
            jr = join_ref[n : n + 1, cols]
            ji = join_ref[2 + n : 3 + n, cols]
            er = jnp.zeros((1, LANES), jnp.float32)
            ei = jnp.zeros((1, LANES), jnp.float32)
            for b in range(SUB):
                begin_ref[n, b : b + 1, cols] = er
                begin_ref[2 + n, b : b + 1, cols] = ei
                er, ei = (
                    jr * er - ji * ei + re[n][b : b + 1],
                    jr * ei + ji * er + im[n][b : b + 1],
                )
            final_ref[n : n + 1, cols] = er
            final_ref[2 + n : 3 + n, cols] = ei


def gate_kernel(
    rows, chans, all_ref, jump_ref, begin_ref, reach_ref, step_ref, residue_ref, bias_ref, mixin_ref, keep_ref, more_ref, taps_ref, out_ref, long
):
    query = short_conv(rows, 0, keep_ref[...] + more_ref[...].astype(jnp.float32), taps_ref)
    length = rows // SUB
    entry = []
    for n in range(2):
        fr, fi = all_ref[:, n, :], all_ref[:, 2 + n, :]
        cr, ci = jump_ref[n], jump_ref[2 + n]
        gr = jnp.sum(cr * fr - ci * fi, axis=0, keepdims=True)
        gi = jnp.sum(cr * fi + ci * fr, axis=0, keepdims=True)
        rr, ri = reach_ref[n], reach_ref[2 + n]
        entry.append((begin_ref[n] + rr * gr - ri * gi, begin_ref[2 + n] + rr * gi + ri * gr))
    for q in range(chans // LANES):
        cols = slice(q * LANES, (q + 1) * LANES)
        wide = lambda row: jnp.broadcast_to(row, (SUB, LANES))
        ar = [wide(step_ref[n : n + 1, cols]) for n in range(2)]
        ai = [wide(step_ref[2 + n : 3 + n, cols]) for n in range(2)]
        pr = [wide(residue_ref[n : n + 1, cols]) for n in range(2)]
        pi = [wide(residue_ref[2 + n : 3 + n, cols]) for n in range(2)]
        direct = wide(bias_ref[:, cols])
        re = [entry[n][0][:, cols] for n in range(2)]
        im = [entry[n][1][:, cols] for n in range(2)]
        for i in range(length):
            u = mixin_ref[q, pl.ds(i, SUB, stride=length), :]
            y = direct * u
            for n in range(2):
                re[n], im[n] = ar[n] * re[n] - ai[n] * im[n] + u, ar[n] * im[n] + ai[n] * re[n]
                y = y + (pr[n] * re[n] - pi[n] * im[n])
            long[q, pl.ds(i, SUB, stride=length), :] = y
        out_ref[:, cols] = (query[:, cols] * long[q]).astype(out_ref.dtype)


def mix_kernel(count, which_ref, *refs):
    x_refs, (w_ref, out_ref, rest_ref, w, sems) = refs[: count - 1], refs[count - 1 :]
    chans = x_refs[0].shape[1]
    part = chans // 2
    copies = []
    for j in range(count):
        block = which_ref[j]
        other = jnp.where(lax.rem(block, 2) == which_ref[count], 0, 1)
        col = pl.multiple_of(other * chans, chans)
        pair = []
        for e in range(2):
            row = pl.multiple_of(lax.div(block, 2) * chans + jnp.where(other == e, 0, part), part)
            dst = rest_ref if j == count - 1 else w.at[j]
            pair.append(
                pltpu.make_async_copy(
                    w_ref.at[pl.ds(row, part), pl.ds(col, out_ref.shape[1])],
                    dst.at[pl.ds(e * part, part)],
                    sems.at[j, e],
                )
            )
            pair[-1].start()
        copies.append(pair)
    total = jnp.zeros(out_ref.shape, jnp.float32)
    for j in range(count):
        for copy in copies[j]:
            copy.wait()
        if j < count - 1:
            total = total + jnp.dot(x_refs[j][...], w[j], preferred_element_type=jnp.float32)
    out_ref[...] = total


def last_mix_kernel(x_ref, w_ref, base_ref, out_ref):
    total = base_ref[...] + jnp.dot(x_ref[...], w_ref[...], preferred_element_type=jnp.float32)
    out_ref[...] = total.astype(out_ref.dtype)


IN_VMEM = pl.BlockSpec(memory_space=pltpu.VMEM)
IN_SMEM = pl.BlockSpec(memory_space=pltpu.SMEM)
IN_HBM = pl.BlockSpec(memory_space=pltpu.HBM)
in_hbm = functools.partial(pltpu.with_memory_space_constraint, memory_space=pltpu.HBM)


def mix(blocks, which, weight, cols):
    rows, chans = blocks[0].shape
    count = len(blocks) + 1
    return pl.pallas_call(
        functools.partial(mix_kernel, count),
        in_specs=[IN_SMEM] + [IN_VMEM] * (count - 1) + [IN_HBM],
        out_shape=[
            jax.ShapeDtypeStruct((rows, cols), jnp.float32),
            jax.ShapeDtypeStruct((chans, cols), weight.dtype),
        ],
        scratch_shapes=[
            pltpu.VMEM((count - 1, chans, cols), weight.dtype),
            pltpu.SemaphoreType.DMA((count, 2)),
        ],
        compiler_params=pltpu.CompilerParams(vmem_limit_bytes=VMEM),
        cost_estimate=pl.CostEstimate(
            flops=2 * count * rows * chans * cols,
            bytes_accessed=2 * count * chans * cols,
            transcendentals=0,
        ),
        name="mix",
    )(which, *blocks, in_hbm(weight))


def body(inputs, in_weight, out_weight, short_filter, decay, angle, residue, bias):
    rows, chans = inputs.shape
    place, blocks = lax.axis_index("seq"), lax.axis_size("seq")
    count = lax.axis_size("ch")
    col_start = lax.axis_index("ch") * chans
    near = [(s % 8) // 4 for s in range(blocks)]
    mirror = [s + 6 - 4 * ((s % 8) // 2) for s in range(blocks)]
    cut = lax.dynamic_slice(in_weight, (0, 0, col_start), (in_weight.shape[0], 3, chans))
    own_weight = jnp.concatenate([cut[:, g] for g in range(3)], axis=1)
    pairs = [(s, mirror[s]) for s in range(blocks)]
    halves = [[s for s in range(blocks) if near[s] == h] for h in range(2)]
    gather = lambda x: lax.all_gather(x, "seq", axis=0, tiled=True, axis_index_groups=halves)
    weight = gather(own_weight)
    both = jnp.concatenate([out_weight, lax.ppermute(out_weight, "seq", pairs)], axis=1)
    second = gather(both)

    rim = lax.ppermute(inputs[-2:], "seq", [(i, i + 1) for i in range(blocks - 1)])
    tokens = jnp.concatenate([inputs, rim, jnp.zeros((HALO - 2, chans), inputs.dtype)], axis=0)
    swaps = []
    for c in range(count):
        for s in range(blocks):
            to = (c, s) if c % 2 == near[s] else (c ^ 1, mirror[s])
            swaps.append((c * blocks + s, to[0] * blocks + to[1]))
    features = ring(lax.ppermute(tokens, ("ch", "seq"), swaps), "ch")
    here = lax.axis_index("ch")

    rate, turn = decay.T, angle.T
    length = rows // SUB
    pack = lambda pair: jnp.concatenate(pair, axis=1)
    step = pack(powers(jnp.ones((1,), jnp.float32), rate, turn))[0]
    join = pack(powers(jnp.full((1,), length, jnp.float32), rate, turn))[0]
    reach = pack(powers((jnp.arange(SUB) * length).astype(jnp.float32), rate, turn))
    reach = reach.transpose(1, 0, 2)
    gap = place - 1 - jnp.arange(blocks)
    jump = pack(powers((jnp.maximum(gap, 0) * rows).astype(jnp.float32), rate, turn))
    jump = jnp.where((gap >= 0)[:, None, None], jump, 0.0).transpose(1, 0, 2)
    poles = jnp.concatenate([residue[0].T, residue[1].T], axis=0)

    f32, b16 = jnp.float32, jnp.bfloat16
    padded, depth = rows + HALO, chans * count // 2
    params = pltpu.CompilerParams(vmem_limit_bytes=VMEM)
    shape = jax.ShapeDtypeStruct
    half = lax.rem(place, 8) // 4
    keep, send, lhs = pl.pallas_call(
        functools.partial(mixin_project_kernel, count),
        in_specs=[IN_SMEM] + [IN_VMEM] * count + [IN_HBM],
        out_shape=[
            shape((padded, 2 * chans), f32),
            shape((padded, 2 * chans), b16),
            shape((2, padded, depth), b16),
        ],
        scratch_shapes=[pltpu.VMEM((depth, 2 * chans), b16), pltpu.SemaphoreType.DMA((2,))],
        compiler_params=params,
        cost_estimate=pl.CostEstimate(
            flops=8 * padded * depth * chans, bytes_accessed=4 * depth * chans, transcendentals=0
        ),
        name="project_mixin",
    )(jnp.stack([half, here]).astype(jnp.int32), *features, in_hbm(weight))
    more = lax.ppermute(send, "seq", pairs)
    query_keep, query_send = pl.pallas_call(
        query_project_kernel,
        in_specs=[IN_VMEM, IN_HBM],
        out_shape=[shape((padded, chans), f32), shape((padded, chans), b16)],
        scratch_shapes=[pltpu.VMEM((depth, chans), b16), pltpu.SemaphoreType.DMA((1,))],
        compiler_params=params,
        cost_estimate=pl.CostEstimate(
            flops=4 * padded * depth * chans, bytes_accessed=2 * depth * chans, transcendentals=0
        ),
        name="project_query",
    )(lhs, in_hbm(weight))
    taps = short_filter.reshape(9, chans)
    mixin, begin, final, query_send = pl.pallas_call(
        functools.partial(scan_kernel, rows, chans),
        out_shape=[
            shape((chans // LANES, rows, LANES), f32),
            shape((4, SUB, chans), f32),
            shape((4, chans), f32),
            shape((padded, chans), b16),
        ],
        compiler_params=params,
        name="scan",
    )(keep, more, query_send, taps, step, join)
    query_more = lax.ppermute(query_send, "seq", pairs)

    states = spread(final, "seq")
    gated = pl.pallas_call(
        functools.partial(gate_kernel, rows, chans),
        out_shape=shape((rows, chans), b16),
        scratch_shapes=[pltpu.VMEM((chans // LANES, rows, LANES), f32)],
        compiler_params=params,
        name="gate",
    )(states, jump, begin, reach, step, poles, bias[None, :], mixin, query_keep, query_more, taps)

    which = jnp.stack([lax.rem(here + hop + count, count) for hop in ring_hops(count)] + [half])
    parts = ring(gated, "ch")
    first, rest = mix(parts[:-1], which.astype(jnp.int32), second, out_weight.shape[1])
    return pl.pallas_call(
        last_mix_kernel,
        out_shape=shape(first.shape, b16),
        compiler_params=params,
        name="last_mix",
    )(parts[-1], rest, first)


def solution(mesh):
    placed = (
        P("seq", "ch"),
        P("seq", None, None),
        P("seq", "ch"),
        P(None, None, "ch"),
        P("ch", None),
        P("ch", None),
        P(None, "ch", None),
        P("ch"),
    )
    return jax.shard_map(
        body, mesh=mesh, in_specs=placed, out_specs=P("seq", "ch"), check_vma=False
    )
```

```python
import functools

import jax
import jax.numpy as jnp
from jax import lax
from jax.experimental import pallas as pl
from jax.experimental.pallas import tpu as pltpu
from jax.sharding import PartitionSpec as P

HALO = 16
LANES = 128
SUB = 8
VMEM = 24 * 1024 * 1024


def ring_hops(count):
    hops = [0]
    for hop in range(1, count // 2 + 1):
        hops += [-hop, hop] if 2 * hop < count else [-hop]
    return hops


def ring(x, axis):
    count = lax.axis_size(axis)
    up = [(c, (c + 1) % count) for c in range(count)]
    down = [(c, (c - 1) % count) for c in range(count)]
    arrived = [x]
    below = above = x
    for hop in range(1, count // 2 + 1):
        below = lax.ppermute(below, axis, up)
        arrived.append(below)
        if 2 * hop < count:
            above = lax.ppermute(above, axis, down)
            arrived.append(above)
    return arrived


def powers(exponent, rate, turn):
    mag = jnp.exp(-exponent[:, None, None] * rate[None])
    phase = exponent[:, None, None] * turn[None]
    return mag * jnp.cos(phase), mag * jnp.sin(phase)


def product(lhs_ref, w, cols, keep_ref, send_ref, out):
    sides, rows, depth = lhs_ref.shape
    part = jnp.dot(
        lhs_ref[...].reshape(sides * rows, depth), w[:, cols], preferred_element_type=jnp.float32
    )
    keep_ref[:, out] = part[:rows]
    send_ref[:, out] = part[rows:].astype(send_ref.dtype)


def mixin_project_kernel(count, place_ref, *refs):
    x_refs, (w_ref, keep_ref, send_ref, lhs_ref, rest_ref, w, sems) = refs[:count], refs[count:]
    chans = x_refs[0].shape[1]
    copies = []
    for j, branch in enumerate((1, 2, 0)):
        cols = slice(j * chans, (j + 1) * chans)
        dst = w.at[:, cols] if branch else rest_ref
        src = w_ref.at[:, pl.ds(branch * chans, chans)]
        copies.append(pltpu.make_async_copy(src, dst, sems.at[j]))
        copies[-1].start()
    half, here = place_ref[0], place_ref[1]
    for x_ref, hop in zip(x_refs, ring_hops(count)):
        origin = lax.rem(here + hop + count, count)
        side = jnp.where(lax.rem(origin, 2) == half, 0, 1)
        at = pl.multiple_of(lax.div(origin, 2) * chans, chans)
        lhs_ref[side, :, pl.ds(at, chans)] = x_ref[...]
    for j in range(2):
        cols = slice(j * chans, (j + 1) * chans)
        copies[j].wait()
        product(lhs_ref, w, cols, keep_ref, send_ref, cols)
    copies[2].wait()


def query_project_kernel(lhs_ref, w_ref, keep_ref, send_ref):
    cols = slice(0, w_ref.shape[1])
    product(lhs_ref, w_ref, cols, keep_ref, send_ref, cols)


def after_kernel(x_ref, done_ref, also_ref, out_ref):
    out_ref[...] = x_ref[...]


def short_conv(rows, branch, total, taps_ref):
    now = total[:rows]
    past = total[rows : rows + 8]
    one = jnp.concatenate([past[1:2], now[:-1]], axis=0)
    two = jnp.concatenate([past[0:2], now[:-2]], axis=0)
    tap = [taps_ref[3 * j + branch : 3 * j + branch + 1, :] for j in range(3)]
    return tap[0] * now + tap[1] * one + tap[2] * two


def scan_kernel(
    rows,
    chans,
    keep_ref,
    more_ref,
    query_keep_ref,
    query_more_ref,
    taps_ref,
    step_ref,
    join_ref,
    mixin_ref,
    query_ref,
    begin_ref,
    final_ref,
):
    query = query_keep_ref[...] + query_more_ref[...].astype(jnp.float32)
    query_ref[...] = short_conv(rows, 0, query, taps_ref)
    length = rows // SUB

    def filtered(branch):
        cols = slice((branch - 1) * chans, branch * chans)
        total = keep_ref[:, cols] + more_ref[:, cols].astype(jnp.float32)
        return short_conv(rows, branch, total, taps_ref)

    mixin = filtered(1) * filtered(2)
    for q in range(chans // LANES):
        mixin_ref[q] = mixin[:, q * LANES : (q + 1) * LANES]
    for q in range(chans // LANES):
        cols = slice(q * LANES, (q + 1) * LANES)
        wide = lambda row: jnp.broadcast_to(row, (SUB, LANES))
        ar = [wide(step_ref[n : n + 1, cols]) for n in range(2)]
        ai = [wide(step_ref[2 + n : 3 + n, cols]) for n in range(2)]
        re = [jnp.zeros((SUB, LANES), jnp.float32)] * 2
        im = [jnp.zeros((SUB, LANES), jnp.float32)] * 2
        for i in range(length):
            u = mixin_ref[q, pl.ds(i, SUB, stride=length), :]
            for n in range(2):
                re[n], im[n] = ar[n] * re[n] - ai[n] * im[n] + u, ar[n] * im[n] + ai[n] * re[n]
        for n in range(2):
            jr = join_ref[n : n + 1, cols]
            ji = join_ref[2 + n : 3 + n, cols]
            er = jnp.zeros((1, LANES), jnp.float32)
            ei = jnp.zeros((1, LANES), jnp.float32)
            for b in range(SUB):
                begin_ref[n, b : b + 1, cols] = er
                begin_ref[2 + n, b : b + 1, cols] = ei
                er, ei = (
                    jr * er - ji * ei + re[n][b : b + 1],
                    jr * ei + ji * er + im[n][b : b + 1],
                )
            for copy in range(final_ref.shape[0]):
                final_ref[copy, n : n + 1, cols] = er
                final_ref[copy, 2 + n : 3 + n, cols] = ei


def gate_kernel(
    rows, chans, all_ref, jump_ref, begin_ref, reach_ref, step_ref, residue_ref, bias_ref, mixin_ref, query_ref, out_ref, long
):
    length = rows // SUB
    entry = []
    for n in range(2):
        fr, fi = all_ref[:, n, :], all_ref[:, 2 + n, :]
        cr, ci = jump_ref[n], jump_ref[2 + n]
        gr = jnp.sum(cr * fr - ci * fi, axis=0, keepdims=True)
        gi = jnp.sum(cr * fi + ci * fr, axis=0, keepdims=True)
        rr, ri = reach_ref[n], reach_ref[2 + n]
        entry.append((begin_ref[n] + rr * gr - ri * gi, begin_ref[2 + n] + rr * gi + ri * gr))
    for q in range(chans // LANES):
        cols = slice(q * LANES, (q + 1) * LANES)
        wide = lambda row: jnp.broadcast_to(row, (SUB, LANES))
        ar = [wide(step_ref[n : n + 1, cols]) for n in range(2)]
        ai = [wide(step_ref[2 + n : 3 + n, cols]) for n in range(2)]
        pr = [wide(residue_ref[n : n + 1, cols]) for n in range(2)]
        pi = [wide(residue_ref[2 + n : 3 + n, cols]) for n in range(2)]
        direct = wide(bias_ref[:, cols])
        re = [entry[n][0][:, cols] for n in range(2)]
        im = [entry[n][1][:, cols] for n in range(2)]
        for i in range(length):
            u = mixin_ref[q, pl.ds(i, SUB, stride=length), :]
            y = direct * u
            for n in range(2):
                re[n], im[n] = ar[n] * re[n] - ai[n] * im[n] + u, ar[n] * im[n] + ai[n] * re[n]
                y = y + (pr[n] * re[n] - pi[n] * im[n])
            long[q, pl.ds(i, SUB, stride=length), :] = y
        out_ref[:, cols] = (query_ref[:, cols] * long[q]).astype(out_ref.dtype)


def mix_kernel(count, which_ref, *refs):
    x_refs, (w_ref, out_ref, rest_ref, w, sems) = refs[: count - 1], refs[count - 1 :]
    chans = x_refs[0].shape[1]
    part = chans // 2
    copies = []
    for j in range(count):
        block = which_ref[j]
        other = jnp.where(lax.rem(block, 2) == which_ref[count], 0, 1)
        col = pl.multiple_of(other * chans, chans)
        pair = []
        for e in range(2):
            row = pl.multiple_of(lax.div(block, 2) * chans + jnp.where(other == e, 0, part), part)
            dst = rest_ref if j == count - 1 else w.at[j]
            pair.append(
                pltpu.make_async_copy(
                    w_ref.at[pl.ds(row, part), pl.ds(col, out_ref.shape[1])],
                    dst.at[pl.ds(e * part, part)],
                    sems.at[j, e],
                )
            )
            pair[-1].start()
        copies.append(pair)
    total = jnp.zeros(out_ref.shape, jnp.float32)
    for j in range(count):
        for copy in copies[j]:
            copy.wait()
        if j < count - 1:
            total = total + jnp.dot(x_refs[j][...], w[j], preferred_element_type=jnp.float32)
    out_ref[...] = total


def last_mix_kernel(x_ref, w_ref, base_ref, out_ref):
    total = base_ref[...] + jnp.dot(x_ref[...], w_ref[...], preferred_element_type=jnp.float32)
    out_ref[...] = total.astype(out_ref.dtype)


IN_VMEM = pl.BlockSpec(memory_space=pltpu.VMEM)
IN_SMEM = pl.BlockSpec(memory_space=pltpu.SMEM)
IN_HBM = pl.BlockSpec(memory_space=pltpu.HBM)
in_hbm = functools.partial(pltpu.with_memory_space_constraint, memory_space=pltpu.HBM)


def mix(blocks, which, weight, cols):
    rows, chans = blocks[0].shape
    count = len(blocks) + 1
    return pl.pallas_call(
        functools.partial(mix_kernel, count),
        in_specs=[IN_SMEM] + [IN_VMEM] * (count - 1) + [IN_HBM],
        out_shape=[
            jax.ShapeDtypeStruct((rows, cols), jnp.float32),
            jax.ShapeDtypeStruct((chans, cols), weight.dtype),
        ],
        scratch_shapes=[
            pltpu.VMEM((count - 1, chans, cols), weight.dtype),
            pltpu.SemaphoreType.DMA((count, 2)),
        ],
        compiler_params=pltpu.CompilerParams(vmem_limit_bytes=VMEM),
        cost_estimate=pl.CostEstimate(
            flops=2 * count * rows * chans * cols,
            bytes_accessed=2 * count * chans * cols,
            transcendentals=0,
        ),
        name="mix",
    )(which, *blocks, in_hbm(weight))


def body(inputs, in_weight, out_weight, short_filter, decay, angle, residue, bias):
    rows, chans = inputs.shape
    place, blocks = lax.axis_index("seq"), lax.axis_size("seq")
    count = lax.axis_size("ch")
    col_start = lax.axis_index("ch") * chans
    near = [(s % 8) // 4 for s in range(blocks)]
    mirror = [s + 6 - 4 * ((s % 8) // 2) for s in range(blocks)]
    cut = lax.dynamic_slice(in_weight, (0, 0, col_start), (in_weight.shape[0], 3, chans))
    own_weight = jnp.concatenate([cut[:, g] for g in range(3)], axis=1)
    pairs = [(s, mirror[s]) for s in range(blocks)]
    halves = [[s for s in range(blocks) if near[s] == h] for h in range(2)]
    gather = lambda x: lax.all_gather(x, "seq", axis=0, tiled=True, axis_index_groups=halves)
    weight = gather(own_weight)
    rim = lax.ppermute(inputs[-2:], "seq", [(i, i + 1) for i in range(blocks - 1)])
    tokens = jnp.concatenate([inputs, rim, jnp.zeros((HALO - 2, chans), inputs.dtype)], axis=0)
    swaps = []
    for c in range(count):
        for s in range(blocks):
            to = (c, s) if c % 2 == near[s] else (c ^ 1, mirror[s])
            swaps.append((c * blocks + s, to[0] * blocks + to[1]))
    features = ring(lax.ppermute(tokens, ("ch", "seq"), swaps), "ch")
    here = lax.axis_index("ch")

    rate, turn = decay.T, angle.T
    length = rows // SUB
    pack = lambda pair: jnp.concatenate(pair, axis=1)
    step = pack(powers(jnp.ones((1,), jnp.float32), rate, turn))[0]
    join = pack(powers(jnp.full((1,), length, jnp.float32), rate, turn))[0]
    reach = pack(powers((jnp.arange(SUB) * length).astype(jnp.float32), rate, turn))
    reach = reach.transpose(1, 0, 2)
    gap = place - 1 - jnp.arange(blocks)
    jump = pack(powers((jnp.maximum(gap, 0) * rows).astype(jnp.float32), rate, turn))
    jump = jnp.where((gap >= 0)[:, None, None], jump, 0.0).transpose(1, 0, 2)
    poles = jnp.concatenate([residue[0].T, residue[1].T], axis=0)

    f32, b16 = jnp.float32, jnp.bfloat16
    padded, depth = rows + HALO, chans * count // 2
    params = pltpu.CompilerParams(vmem_limit_bytes=VMEM)
    shape = jax.ShapeDtypeStruct
    half = lax.rem(place, 8) // 4
    held = pl.pallas_call(
        after_kernel,
        in_specs=[IN_VMEM] * 3,
        out_shape=shape(out_weight.shape, b16),
        compiler_params=params,
        name="after",
    )(out_weight, features[-2], features[-1])
    second = gather(jnp.concatenate([out_weight, lax.ppermute(held, "seq", pairs)], axis=1))
    cost = lambda width: pl.CostEstimate(
        flops=4 * padded * depth * width, bytes_accessed=2 * depth * width, transcendentals=0
    )
    keep, send, lhs, query_weight = pl.pallas_call(
        functools.partial(mixin_project_kernel, count),
        in_specs=[IN_SMEM] + [IN_VMEM] * count + [IN_HBM],
        out_shape=[
            shape((padded, 2 * chans), f32),
            shape((padded, 2 * chans), b16),
            shape((2, padded, depth), b16),
            shape((depth, chans), b16),
        ],
        scratch_shapes=[pltpu.VMEM((depth, 2 * chans), b16), pltpu.SemaphoreType.DMA((3,))],
        compiler_params=params,
        cost_estimate=cost(2 * chans),
        name="project_mixin",
    )(jnp.stack([half, here]).astype(jnp.int32), *features, in_hbm(weight))
    more = lax.ppermute(send, "seq", pairs)
    query_keep, query_send = pl.pallas_call(
        query_project_kernel,
        out_shape=[shape((padded, chans), f32), shape((padded, chans), b16)],
        compiler_params=params,
        cost_estimate=cost(chans),
        name="project_query",
    )(lhs, query_weight)
    query_more = lax.ppermute(query_send, "seq", pairs)
    taps = short_filter.reshape(9, chans)
    mixin, query, begin, final = pl.pallas_call(
        functools.partial(scan_kernel, rows, chans),
        out_shape=[
            shape((chans // LANES, rows, LANES), f32),
            shape((rows, chans), f32),
            shape((4, SUB, chans), f32),
            shape((blocks, 4, chans), f32),
        ],
        compiler_params=params,
        name="scan",
    )(keep, more, query_keep, query_more, taps, step, join)

    states = lax.all_to_all(final, "seq", 0, 0, tiled=True)
    gated = pl.pallas_call(
        functools.partial(gate_kernel, rows, chans),
        out_shape=shape((rows, chans), b16),
        scratch_shapes=[pltpu.VMEM((chans // LANES, rows, LANES), f32)],
        compiler_params=params,
        name="gate",
    )(states, jump, begin, reach, step, poles, bias[None, :], mixin, query)

    which = jnp.stack([lax.rem(here + hop + count, count) for hop in ring_hops(count)] + [half])
    parts = ring(gated, "ch")
    first, rest = mix(parts[:-1], which.astype(jnp.int32), second, out_weight.shape[1])
    return pl.pallas_call(
        last_mix_kernel,
        out_shape=shape(first.shape, b16),
        compiler_params=params,
        name="last_mix",
    )(parts[-1], rest, first)


def solution(mesh):
    placed = (
        P("seq", "ch"),
        P("seq", None, None),
        P("seq", "ch"),
        P(None, None, "ch"),
        P("ch", None),
        P("ch", None),
        P(None, "ch", None),
        P("ch"),
    )
    return jax.shard_map(
        body, mesh=mesh, in_specs=placed, out_specs=P("seq", "ch"), check_vma=False
    )
```

```python
import functools

import jax
import jax.numpy as jnp
from jax import lax
from jax.experimental import pallas as pl
from jax.experimental.pallas import tpu as pltpu
from jax.sharding import PartitionSpec as P

HALO = 16
LANES = 128
SUB = 8
VMEM = 24 * 1024 * 1024


def ring_hops(count):
    hops = [0]
    for hop in range(1, count // 2 + 1):
        hops += [-hop, hop] if 2 * hop < count else [-hop]
    return hops


def ring(x, axis):
    count = lax.axis_size(axis)
    up = [(c, (c + 1) % count) for c in range(count)]
    down = [(c, (c - 1) % count) for c in range(count)]
    arrived = [x]
    below = above = x
    for hop in range(1, count // 2 + 1):
        below = lax.ppermute(below, axis, up)
        arrived.append(below)
        if 2 * hop < count:
            above = lax.ppermute(above, axis, down)
            arrived.append(above)
    return arrived


def powers(exponent, rate, turn):
    mag = jnp.exp(-exponent[:, None, None] * rate[None])
    phase = exponent[:, None, None] * turn[None]
    return mag * jnp.cos(phase), mag * jnp.sin(phase)


def product(lhs_ref, w, cols, keep_ref, send_ref, out):
    sides, rows, depth = lhs_ref.shape
    part = jnp.dot(
        lhs_ref[...].reshape(sides * rows, depth), w[:, cols], preferred_element_type=jnp.float32
    )
    keep_ref[:, out] = part[:rows]
    send_ref[:, out] = part[rows:].astype(send_ref.dtype)


def mixin_project_kernel(count, place_ref, *refs):
    x_refs, (w_ref, keep_ref, send_ref, lhs_ref, rest_ref, w, sems) = refs[:count], refs[count:]
    chans = x_refs[0].shape[1]
    copies = []
    for j, branch in enumerate((1, 2, 0)):
        cols = slice(j * chans, (j + 1) * chans)
        dst = w.at[:, cols] if branch else rest_ref
        src = w_ref.at[:, pl.ds(branch * chans, chans)]
        copies.append(pltpu.make_async_copy(src, dst, sems.at[j]))
        copies[-1].start()
    half, here = place_ref[0], place_ref[1]
    for x_ref, hop in zip(x_refs, ring_hops(count)):
        origin = lax.rem(here + hop + count, count)
        side = jnp.where(lax.rem(origin, 2) == half, 0, 1)
        at = pl.multiple_of(lax.div(origin, 2) * chans, chans)
        lhs_ref[side, :, pl.ds(at, chans)] = x_ref[...]
    for j in range(2):
        cols = slice(j * chans, (j + 1) * chans)
        copies[j].wait()
        product(lhs_ref, w, cols, keep_ref, send_ref, cols)
    copies[2].wait()


def query_project_kernel(lhs_ref, w_ref, keep_ref, send_ref):
    cols = slice(0, w_ref.shape[1])
    product(lhs_ref, w_ref, cols, keep_ref, send_ref, cols)


def beside_kernel(x_ref, y_ref, done_ref, also_ref, out_ref, sems):
    cols = x_ref.shape[1]
    left = pltpu.make_async_copy(x_ref, out_ref.at[:, pl.ds(0, cols)], sems.at[0])
    right = pltpu.make_async_copy(y_ref, out_ref.at[:, pl.ds(cols, cols)], sems.at[1])
    left.start()
    right.start()
    left.wait()
    right.wait()


def short_conv(rows, branch, total, taps_ref):
    now = total[:rows]
    past = total[rows : rows + 8]
    one = jnp.concatenate([past[1:2], now[:-1]], axis=0)
    two = jnp.concatenate([past[0:2], now[:-2]], axis=0)
    tap = [taps_ref[3 * j + branch : 3 * j + branch + 1, :] for j in range(3)]
    return tap[0] * now + tap[1] * one + tap[2] * two


def scan_kernel(
    rows,
    chans,
    keep_ref,
    more_ref,
    query_keep_ref,
    query_more_ref,
    taps_ref,
    step_ref,
    join_ref,
    mixin_ref,
    query_ref,
    begin_ref,
    final_ref,
    last,
):
    query = query_keep_ref[...] + query_more_ref[...].astype(jnp.float32)
    query_ref[...] = short_conv(rows, 0, query, taps_ref)
    length = rows // SUB

    def filtered(branch):
        cols = slice((branch - 1) * chans, branch * chans)
        total = keep_ref[:, cols] + more_ref[:, cols].astype(jnp.float32)
        return short_conv(rows, branch, total, taps_ref)

    mixin = filtered(1) * filtered(2)
    for q in range(chans // LANES):
        mixin_ref[q] = mixin[:, q * LANES : (q + 1) * LANES]
    for q in range(chans // LANES):
        cols = slice(q * LANES, (q + 1) * LANES)
        wide = lambda row: jnp.broadcast_to(row, (SUB, LANES))
        ar = [wide(step_ref[n : n + 1, cols]) for n in range(2)]
        ai = [wide(step_ref[2 + n : 3 + n, cols]) for n in range(2)]
        re = [jnp.zeros((SUB, LANES), jnp.float32)] * 2
        im = [jnp.zeros((SUB, LANES), jnp.float32)] * 2
        for i in range(length):
            u = mixin_ref[q, pl.ds(i, SUB, stride=length), :]
            for n in range(2):
                re[n], im[n] = ar[n] * re[n] - ai[n] * im[n] + u, ar[n] * im[n] + ai[n] * re[n]
        for n in range(2):
            jr = join_ref[n : n + 1, cols]
            ji = join_ref[2 + n : 3 + n, cols]
            er = jnp.zeros((1, LANES), jnp.float32)
            ei = jnp.zeros((1, LANES), jnp.float32)
            for b in range(SUB):
                begin_ref[n, b : b + 1, cols] = er
                begin_ref[2 + n, b : b + 1, cols] = ei
                er, ei = (
                    jr * er - ji * ei + re[n][b : b + 1],
                    jr * ei + ji * er + im[n][b : b + 1],
                )
            last[n : n + 1, cols] = er
            last[2 + n : 3 + n, cols] = ei
    for copy in range(final_ref.shape[0]):
        final_ref[copy] = last[...]


def gate_kernel(
    rows, chans, all_ref, jump_ref, begin_ref, reach_ref, step_ref, residue_ref, bias_ref, mixin_ref, query_ref, out_ref, long
):
    length = rows // SUB
    entry = []
    for n in range(2):
        fr, fi = all_ref[:, n, :], all_ref[:, 2 + n, :]
        cr, ci = jump_ref[n], jump_ref[2 + n]
        gr = jnp.sum(cr * fr - ci * fi, axis=0, keepdims=True)
        gi = jnp.sum(cr * fi + ci * fr, axis=0, keepdims=True)
        rr, ri = reach_ref[n], reach_ref[2 + n]
        entry.append((begin_ref[n] + rr * gr - ri * gi, begin_ref[2 + n] + rr * gi + ri * gr))
    for q in range(chans // LANES):
        cols = slice(q * LANES, (q + 1) * LANES)
        wide = lambda row: jnp.broadcast_to(row, (SUB, LANES))
        ar = [wide(step_ref[n : n + 1, cols]) for n in range(2)]
        ai = [wide(step_ref[2 + n : 3 + n, cols]) for n in range(2)]
        pr = [wide(residue_ref[n : n + 1, cols]) for n in range(2)]
        pi = [wide(residue_ref[2 + n : 3 + n, cols]) for n in range(2)]
        direct = wide(bias_ref[:, cols])
        re = [entry[n][0][:, cols] for n in range(2)]
        im = [entry[n][1][:, cols] for n in range(2)]
        for i in range(length):
            u = mixin_ref[q, pl.ds(i, SUB, stride=length), :]
            y = direct * u
            for n in range(2):
                re[n], im[n] = ar[n] * re[n] - ai[n] * im[n] + u, ar[n] * im[n] + ai[n] * re[n]
                y = y + (pr[n] * re[n] - pi[n] * im[n])
            long[q, pl.ds(i, SUB, stride=length), :] = y
        out_ref[:, cols] = (query_ref[:, cols] * long[q]).astype(out_ref.dtype)


def mix_kernel(count, which_ref, *refs):
    x_refs, (w_ref, out_ref, rest_ref, w, sems) = refs[: count - 1], refs[count - 1 :]
    chans = x_refs[0].shape[1]
    part = chans // 2
    copies = []
    for j in range(count):
        block = which_ref[j]
        other = jnp.where(lax.rem(block, 2) == which_ref[count], 0, 1)
        col = pl.multiple_of(other * chans, chans)
        pair = []
        for e in range(2):
            row = pl.multiple_of(lax.div(block, 2) * chans + jnp.where(other == e, 0, part), part)
            dst = rest_ref if j == count - 1 else w.at[j]
            pair.append(
                pltpu.make_async_copy(
                    w_ref.at[pl.ds(row, part), pl.ds(col, out_ref.shape[1])],
                    dst.at[pl.ds(e * part, part)],
                    sems.at[j, e],
                )
            )
            pair[-1].start()
        copies.append(pair)
    total = jnp.zeros(out_ref.shape, jnp.float32)
    for j in range(count):
        for copy in copies[j]:
            copy.wait()
        if j < count - 1:
            total = total + jnp.dot(x_refs[j][...], w[j], preferred_element_type=jnp.float32)
    out_ref[...] = total


def last_mix_kernel(x_ref, w_ref, base_ref, out_ref):
    total = base_ref[...] + jnp.dot(x_ref[...], w_ref[...], preferred_element_type=jnp.float32)
    out_ref[...] = total.astype(out_ref.dtype)


IN_VMEM = pl.BlockSpec(memory_space=pltpu.VMEM)
IN_SMEM = pl.BlockSpec(memory_space=pltpu.SMEM)
IN_HBM = pl.BlockSpec(memory_space=pltpu.HBM)
in_hbm = functools.partial(pltpu.with_memory_space_constraint, memory_space=pltpu.HBM)


def mix(blocks, which, weight, cols):
    rows, chans = blocks[0].shape
    count = len(blocks) + 1
    return pl.pallas_call(
        functools.partial(mix_kernel, count),
        in_specs=[IN_SMEM] + [IN_VMEM] * (count - 1) + [IN_HBM],
        out_shape=[
            jax.ShapeDtypeStruct((rows, cols), jnp.float32),
            jax.ShapeDtypeStruct((chans, cols), weight.dtype),
        ],
        scratch_shapes=[
            pltpu.VMEM((count - 1, chans, cols), weight.dtype),
            pltpu.SemaphoreType.DMA((count, 2)),
        ],
        compiler_params=pltpu.CompilerParams(vmem_limit_bytes=VMEM),
        cost_estimate=pl.CostEstimate(
            flops=2 * count * rows * chans * cols,
            bytes_accessed=2 * count * chans * cols,
            transcendentals=0,
        ),
        name="mix",
    )(which, *blocks, in_hbm(weight))


def body(inputs, in_weight, out_weight, short_filter, decay, angle, residue, bias):
    rows, chans = inputs.shape
    place, blocks = lax.axis_index("seq"), lax.axis_size("seq")
    count = lax.axis_size("ch")
    col_start = lax.axis_index("ch") * chans
    near = [(s % 8) // 4 for s in range(blocks)]
    mirror = [s + 6 - 4 * ((s % 8) // 2) for s in range(blocks)]
    cut = lax.dynamic_slice(in_weight, (0, 0, col_start), (in_weight.shape[0], 3, chans))
    own_weight = jnp.concatenate([cut[:, g] for g in range(3)], axis=1)
    pairs = [(s, mirror[s]) for s in range(blocks)]
    halves = [[s for s in range(blocks) if near[s] == h] for h in range(2)]
    gather = lambda x: lax.all_gather(x, "seq", axis=0, tiled=True, axis_index_groups=halves)
    weight = gather(own_weight)
    rim = lax.ppermute(inputs[-2:], "seq", [(i, i + 1) for i in range(blocks - 1)])
    tokens = jnp.concatenate([inputs, rim, jnp.zeros((HALO - 2, chans), inputs.dtype)], axis=0)
    swaps = []
    for c in range(count):
        for s in range(blocks):
            to = (c, s) if c % 2 == near[s] else (c ^ 1, mirror[s])
            swaps.append((c * blocks + s, to[0] * blocks + to[1]))
    features = ring(lax.ppermute(tokens, ("ch", "seq"), swaps), "ch")
    here = lax.axis_index("ch")

    rate, turn = decay.T, angle.T
    length = rows // SUB
    pack = lambda pair: jnp.concatenate(pair, axis=1)
    step = pack(powers(jnp.ones((1,), jnp.float32), rate, turn))[0]
    join = pack(powers(jnp.full((1,), length, jnp.float32), rate, turn))[0]
    reach = pack(powers((jnp.arange(SUB) * length).astype(jnp.float32), rate, turn))
    reach = reach.transpose(1, 0, 2)
    gap = place - 1 - jnp.arange(blocks)
    jump = pack(powers((jnp.maximum(gap, 0) * rows).astype(jnp.float32), rate, turn))
    jump = jnp.where((gap >= 0)[:, None, None], jump, 0.0).transpose(1, 0, 2)
    poles = jnp.concatenate([residue[0].T, residue[1].T], axis=0)

    f32, b16 = jnp.float32, jnp.bfloat16
    padded, depth = rows + HALO, chans * count // 2
    params = pltpu.CompilerParams(vmem_limit_bytes=VMEM)
    shape = jax.ShapeDtypeStruct
    half = lax.rem(place, 8) // 4
    both = pl.pallas_call(
        beside_kernel,
        in_specs=[IN_HBM] + [pl.BlockSpec(memory_space=pl.ANY)] * 3,
        out_specs=IN_HBM,
        out_shape=shape((out_weight.shape[0], 2 * out_weight.shape[1]), b16),
        scratch_shapes=[pltpu.SemaphoreType.DMA((2,))],
        compiler_params=params,
        name="beside",
    )(in_hbm(out_weight), lax.ppermute(out_weight, "seq", pairs), features[-2], features[-1])
    second = gather(both)
    cost = lambda width: pl.CostEstimate(
        flops=4 * padded * depth * width, bytes_accessed=2 * depth * width, transcendentals=0
    )
    keep, send, lhs, query_weight = pl.pallas_call(
        functools.partial(mixin_project_kernel, count),
        in_specs=[IN_SMEM] + [IN_VMEM] * count + [IN_HBM],
        out_shape=[
            shape((padded, 2 * chans), f32),
            shape((padded, 2 * chans), b16),
            shape((2, padded, depth), b16),
            shape((depth, chans), b16),
        ],
        scratch_shapes=[pltpu.VMEM((depth, 2 * chans), b16), pltpu.SemaphoreType.DMA((3,))],
        compiler_params=params,
        cost_estimate=cost(2 * chans),
        name="project_mixin",
    )(jnp.stack([half, here]).astype(jnp.int32), *features, in_hbm(weight))
    more = lax.ppermute(send, "seq", pairs)
    query_keep, query_send = pl.pallas_call(
        query_project_kernel,
        out_shape=[shape((padded, chans), f32), shape((padded, chans), b16)],
        compiler_params=params,
        cost_estimate=cost(chans),
        name="project_query",
    )(lhs, query_weight)
    query_more = lax.ppermute(query_send, "seq", pairs)
    taps = short_filter.reshape(9, chans)
    mixin, query, begin, final = pl.pallas_call(
        functools.partial(scan_kernel, rows, chans),
        out_shape=[
            shape((chans // LANES, rows, LANES), f32),
            shape((rows, chans), f32),
            shape((4, SUB, chans), f32),
            shape((blocks, 4, chans), f32),
        ],
        scratch_shapes=[pltpu.VMEM((4, chans), f32)],
        compiler_params=params,
        name="scan",
    )(keep, more, query_keep, query_more, taps, step, join)

    states = lax.all_to_all(final, "seq", 0, 0, tiled=True)
    gated = pl.pallas_call(
        functools.partial(gate_kernel, rows, chans),
        out_shape=shape((rows, chans), b16),
        scratch_shapes=[pltpu.VMEM((chans // LANES, rows, LANES), f32)],
        compiler_params=params,
        name="gate",
    )(states, jump, begin, reach, step, poles, bias[None, :], mixin, query)

    which = jnp.stack([lax.rem(here + hop + count, count) for hop in ring_hops(count)] + [half])
    parts = ring(gated, "ch")
    first, rest = mix(parts[:-1], which.astype(jnp.int32), second, out_weight.shape[1])
    return pl.pallas_call(
        last_mix_kernel,
        out_shape=shape(first.shape, b16),
        compiler_params=params,
        name="last_mix",
    )(parts[-1], rest, first)


def solution(mesh):
    placed = (
        P("seq", "ch"),
        P("seq", None, None),
        P("seq", "ch"),
        P(None, None, "ch"),
        P("ch", None),
        P("ch", None),
        P(None, "ch", None),
        P("ch"),
    )
    return jax.shard_map(
        body, mesh=mesh, in_specs=placed, out_specs=P("seq", "ch"), check_vma=False
    )
```

```python
import functools

import jax
import jax.numpy as jnp
from jax import lax
from jax.experimental import pallas as pl
from jax.experimental.pallas import tpu as pltpu
from jax.sharding import PartitionSpec as P

HALO = 16
LANES = 128
SUB = 8
VMEM = 24 * 1024 * 1024


def spread(x, axis):
    count = lax.axis_size(axis)
    return lax.all_to_all(
        jnp.broadcast_to(x[None], (count,) + x.shape), axis, 0, 0, tiled=True
    )


def ring_hops(count):
    hops = [0]
    for hop in range(1, count // 2 + 1):
        hops += [-hop, hop] if 2 * hop < count else [-hop]
    return hops


def ring(x, axis):
    count = lax.axis_size(axis)
    up = [(c, (c + 1) % count) for c in range(count)]
    down = [(c, (c - 1) % count) for c in range(count)]
    arrived = [x]
    below = above = x
    for hop in range(1, count // 2 + 1):
        below = lax.ppermute(below, axis, up)
        arrived.append(below)
        if 2 * hop < count:
            above = lax.ppermute(above, axis, down)
            arrived.append(above)
    return arrived


def powers(exponent, rate, turn):
    mag = jnp.exp(-exponent[:, None, None] * rate[None])
    phase = exponent[:, None, None] * turn[None]
    return mag * jnp.cos(phase), mag * jnp.sin(phase)


def fetch(w_ref, w, sems, starts, sizes):
    copies = []
    for j, (start, size) in enumerate(zip(starts, sizes)):
        at = sum(sizes[:j])
        copies.append(
            pltpu.make_async_copy(w_ref.at[:, pl.ds(start, size)], w.at[:, pl.ds(at, size)], sems.at[j])
        )
        copies[-1].start()
    return copies


def product(lhs_ref, w, copies, chans, keep_ref, send_ref):
    sides, rows, depth = lhs_ref.shape
    both = lhs_ref[...].reshape(sides * rows, depth)
    for j, copy in enumerate(copies):
        copy.wait()
        cols = slice(j * chans, (j + 1) * chans)
        part = jnp.dot(both, w[:, cols], preferred_element_type=jnp.float32)
        keep_ref[:, cols] = part[:rows]
        send_ref[:, cols] = part[rows:].astype(send_ref.dtype)


def mixin_project_kernel(count, place_ref, *refs):
    x_refs, (w_ref, keep_ref, send_ref, lhs_ref, w, sems) = refs[:count], refs[count:]
    chans = x_refs[0].shape[1]
    copies = fetch(w_ref, w, sems, (chans, 2 * chans), (chans, chans))
    half, here = place_ref[0], place_ref[1]
    for x_ref, hop in zip(x_refs, ring_hops(count)):
        origin = lax.rem(here + hop + count, count)
        side = jnp.where(lax.rem(origin, 2) == half, 0, 1)
        at = pl.multiple_of(lax.div(origin, 2) * chans, chans)
        lhs_ref[side, :, pl.ds(at, chans)] = x_ref[...]
    product(lhs_ref, w, copies, chans, keep_ref, send_ref)


def query_project_kernel(lhs_ref, w_ref, keep_ref, send_ref, w, sems):
    chans = keep_ref.shape[1]
    copies = fetch(w_ref, w, sems, (0,), (chans,))
    product(lhs_ref, w, copies, chans, keep_ref, send_ref)


def beside_kernel(x_ref, y_ref, done_ref, also_ref, out_ref, sem):
    cols = x_ref.shape[1]
    copy = pltpu.make_async_copy(x_ref, out_ref.at[:, pl.ds(0, cols)], sem)
    copy.start()
    out_ref[:, cols:] = y_ref[...]
    copy.wait()


def short_conv(rows, branch, total, taps_ref):
    now = total[:rows]
    past = total[rows : rows + 8]
    one = jnp.concatenate([past[1:2], now[:-1]], axis=0)
    two = jnp.concatenate([past[0:2], now[:-2]], axis=0)
    tap = [taps_ref[3 * j + branch : 3 * j + branch + 1, :] for j in range(3)]
    return tap[0] * now + tap[1] * one + tap[2] * two


def scan_kernel(
    rows,
    chans,
    keep_ref,
    more_ref,
    query_ref,
    taps_ref,
    step_ref,
    join_ref,
    mixin_ref,
    begin_ref,
    final_ref,
    send_ref,
):
    send_ref[...] = query_ref[...]
    length = rows // SUB

    def filtered(branch):
        cols = slice((branch - 1) * chans, branch * chans)
        total = keep_ref[:, cols] + more_ref[:, cols].astype(jnp.float32)
        return short_conv(rows, branch, total, taps_ref)

    mixin = filtered(1) * filtered(2)
    for q in range(chans // LANES):
        mixin_ref[q] = mixin[:, q * LANES : (q + 1) * LANES]
    for q in range(chans // LANES):
        cols = slice(q * LANES, (q + 1) * LANES)
        wide = lambda row: jnp.broadcast_to(row, (SUB, LANES))
        ar = [wide(step_ref[n : n + 1, cols]) for n in range(2)]
        ai = [wide(step_ref[2 + n : 3 + n, cols]) for n in range(2)]
        re = [jnp.zeros((SUB, LANES), jnp.float32)] * 2
        im = [jnp.zeros((SUB, LANES), jnp.float32)] * 2
        for i in range(length):
            u = mixin_ref[q, pl.ds(i, SUB, stride=length), :]
            for n in range(2):
                re[n], im[n] = ar[n] * re[n] - ai[n] * im[n] + u, ar[n] * im[n] + ai[n] * re[n]
        for n in range(2):
            jr = join_ref[n : n + 1, cols]
            ji = join_ref[2 + n : 3 + n, cols]
            er = jnp.zeros((1, LANES), jnp.float32)
            ei = jnp.zeros((1, LANES), jnp.float32)
            for b in range(SUB):
                begin_ref[n, b : b + 1, cols] = er
                begin_ref[2 + n, b : b + 1, cols] = ei
                er, ei = (
                    jr * er - ji * ei + re[n][b : b + 1],
                    jr * ei + ji * er + im[n][b : b + 1],
                )
            final_ref[n : n + 1, cols] = er
            final_ref[2 + n : 3 + n, cols] = ei


def gate_kernel(
    rows, chans, all_ref, jump_ref, begin_ref, reach_ref, step_ref, residue_ref, bias_ref, mixin_ref, keep_ref, more_ref, taps_ref, out_ref, long
):
    query = short_conv(rows, 0, keep_ref[...] + more_ref[...].astype(jnp.float32), taps_ref)
    length = rows // SUB
    entry = []
    for n in range(2):
        fr, fi = all_ref[:, n, :], all_ref[:, 2 + n, :]
        cr, ci = jump_ref[n], jump_ref[2 + n]
        gr = jnp.sum(cr * fr - ci * fi, axis=0, keepdims=True)
        gi = jnp.sum(cr * fi + ci * fr, axis=0, keepdims=True)
        rr, ri = reach_ref[n], reach_ref[2 + n]
        entry.append((begin_ref[n] + rr * gr - ri * gi, begin_ref[2 + n] + rr * gi + ri * gr))
    for q in range(chans // LANES):
        cols = slice(q * LANES, (q + 1) * LANES)
        wide = lambda row: jnp.broadcast_to(row, (SUB, LANES))
        ar = [wide(step_ref[n : n + 1, cols]) for n in range(2)]
        ai = [wide(step_ref[2 + n : 3 + n, cols]) for n in range(2)]
        pr = [wide(residue_ref[n : n + 1, cols]) for n in range(2)]
        pi = [wide(residue_ref[2 + n : 3 + n, cols]) for n in range(2)]
        direct = wide(bias_ref[:, cols])
        re = [entry[n][0][:, cols] for n in range(2)]
        im = [entry[n][1][:, cols] for n in range(2)]
        for i in range(length):
            u = mixin_ref[q, pl.ds(i, SUB, stride=length), :]
            y = direct * u
            for n in range(2):
                re[n], im[n] = ar[n] * re[n] - ai[n] * im[n] + u, ar[n] * im[n] + ai[n] * re[n]
                y = y + (pr[n] * re[n] - pi[n] * im[n])
            long[q, pl.ds(i, SUB, stride=length), :] = y
        out_ref[:, cols] = (query[:, cols] * long[q]).astype(out_ref.dtype)


def mix_kernel(count, which_ref, *refs):
    x_refs, (w_ref, out_ref, rest_ref, w, sems) = refs[: count - 1], refs[count - 1 :]
    chans = x_refs[0].shape[1]
    part = chans // 2
    copies = []
    for j in range(count):
        block = which_ref[j]
        other = jnp.where(lax.rem(block, 2) == which_ref[count], 0, 1)
        col = pl.multiple_of(other * chans, chans)
        pair = []
        for e in range(2):
            row = pl.multiple_of(lax.div(block, 2) * chans + jnp.where(other == e, 0, part), part)
            dst = rest_ref if j == count - 1 else w.at[j]
            pair.append(
                pltpu.make_async_copy(
                    w_ref.at[pl.ds(row, part), pl.ds(col, out_ref.shape[1])],
                    dst.at[pl.ds(e * part, part)],
                    sems.at[j, e],
                )
            )
            pair[-1].start()
        copies.append(pair)
    total = jnp.zeros(out_ref.shape, jnp.float32)
    for j in range(count):
        for copy in copies[j]:
            copy.wait()
        if j < count - 1:
            total = total + jnp.dot(x_refs[j][...], w[j], preferred_element_type=jnp.float32)
    out_ref[...] = total


def last_mix_kernel(x_ref, w_ref, base_ref, out_ref):
    total = base_ref[...] + jnp.dot(x_ref[...], w_ref[...], preferred_element_type=jnp.float32)
    out_ref[...] = total.astype(out_ref.dtype)


IN_VMEM = pl.BlockSpec(memory_space=pltpu.VMEM)
IN_SMEM = pl.BlockSpec(memory_space=pltpu.SMEM)
IN_HBM = pl.BlockSpec(memory_space=pltpu.HBM)
in_hbm = functools.partial(pltpu.with_memory_space_constraint, memory_space=pltpu.HBM)


def mix(blocks, which, weight, cols):
    rows, chans = blocks[0].shape
    count = len(blocks) + 1
    return pl.pallas_call(
        functools.partial(mix_kernel, count),
        in_specs=[IN_SMEM] + [IN_VMEM] * (count - 1) + [IN_HBM],
        out_shape=[
            jax.ShapeDtypeStruct((rows, cols), jnp.float32),
            jax.ShapeDtypeStruct((chans, cols), weight.dtype),
        ],
        scratch_shapes=[
            pltpu.VMEM((count - 1, chans, cols), weight.dtype),
            pltpu.SemaphoreType.DMA((count, 2)),
        ],
        compiler_params=pltpu.CompilerParams(vmem_limit_bytes=VMEM),
        cost_estimate=pl.CostEstimate(
            flops=2 * count * rows * chans * cols,
            bytes_accessed=2 * count * chans * cols,
            transcendentals=0,
        ),
        name="mix",
    )(which, *blocks, in_hbm(weight))


def body(inputs, in_weight, out_weight, short_filter, decay, angle, residue, bias):
    rows, chans = inputs.shape
    place, blocks = lax.axis_index("seq"), lax.axis_size("seq")
    count = lax.axis_size("ch")
    col_start = lax.axis_index("ch") * chans
    near = [(s % 8) // 4 for s in range(blocks)]
    mirror = [s + 6 - 4 * ((s % 8) // 2) for s in range(blocks)]
    cut = lax.dynamic_slice(in_weight, (0, 0, col_start), (in_weight.shape[0], 3, chans))
    own_weight = jnp.concatenate([cut[:, g] for g in range(3)], axis=1)
    pairs = [(s, mirror[s]) for s in range(blocks)]
    halves = [[s for s in range(blocks) if near[s] == h] for h in range(2)]
    gather = lambda x: lax.all_gather(x, "seq", axis=0, tiled=True, axis_index_groups=halves)
    weight = gather(own_weight)
    rim = lax.ppermute(inputs[-2:], "seq", [(i, i + 1) for i in range(blocks - 1)])
    tokens = jnp.concatenate([inputs, rim, jnp.zeros((HALO - 2, chans), inputs.dtype)], axis=0)
    swaps = []
    for c in range(count):
        for s in range(blocks):
            to = (c, s) if c % 2 == near[s] else (c ^ 1, mirror[s])
            swaps.append((c * blocks + s, to[0] * blocks + to[1]))
    features = ring(lax.ppermute(tokens, ("ch", "seq"), swaps), "ch")
    here = lax.axis_index("ch")

    rate, turn = decay.T, angle.T
    length = rows // SUB
    pack = lambda pair: jnp.concatenate(pair, axis=1)
    step = pack(powers(jnp.ones((1,), jnp.float32), rate, turn))[0]
    join = pack(powers(jnp.full((1,), length, jnp.float32), rate, turn))[0]
    reach = pack(powers((jnp.arange(SUB) * length).astype(jnp.float32), rate, turn))
    reach = reach.transpose(1, 0, 2)
    gap = place - 1 - jnp.arange(blocks)
    jump = pack(powers((jnp.maximum(gap, 0) * rows).astype(jnp.float32), rate, turn))
    jump = jnp.where((gap >= 0)[:, None, None], jump, 0.0).transpose(1, 0, 2)
    poles = jnp.concatenate([residue[0].T, residue[1].T], axis=0)

    f32, b16 = jnp.float32, jnp.bfloat16
    padded, depth = rows + HALO, chans * count // 2
    params = pltpu.CompilerParams(vmem_limit_bytes=VMEM)
    shape = jax.ShapeDtypeStruct
    half = lax.rem(place, 8) // 4
    anywhere = pl.BlockSpec(memory_space=pl.ANY)
    both = pl.pallas_call(
        beside_kernel,
        in_specs=[IN_HBM, IN_VMEM, anywhere, anywhere],
        out_shape=shape((out_weight.shape[0], 2 * out_weight.shape[1]), b16),
        scratch_shapes=[pltpu.SemaphoreType.DMA(())],
        compiler_params=params,
        name="beside",
    )(in_hbm(out_weight), lax.ppermute(out_weight, "seq", pairs), features[-2], features[-1])
    second = gather(both)
    keep, send, lhs = pl.pallas_call(
        functools.partial(mixin_project_kernel, count),
        in_specs=[IN_SMEM] + [IN_VMEM] * count + [IN_HBM],
        out_shape=[
            shape((padded, 2 * chans), f32),
            shape((padded, 2 * chans), b16),
            shape((2, padded, depth), b16),
        ],
        scratch_shapes=[pltpu.VMEM((depth, 2 * chans), b16), pltpu.SemaphoreType.DMA((2,))],
        compiler_params=params,
        cost_estimate=pl.CostEstimate(
            flops=8 * padded * depth * chans, bytes_accessed=4 * depth * chans, transcendentals=0
        ),
        name="project_mixin",
    )(jnp.stack([half, here]).astype(jnp.int32), *features, in_hbm(weight))
    more = lax.ppermute(send, "seq", pairs)
    query_keep, query_send = pl.pallas_call(
        query_project_kernel,
        in_specs=[IN_VMEM, IN_HBM],
        out_shape=[shape((padded, chans), f32), shape((padded, chans), b16)],
        scratch_shapes=[pltpu.VMEM((depth, chans), b16), pltpu.SemaphoreType.DMA((1,))],
        compiler_params=params,
        cost_estimate=pl.CostEstimate(
            flops=4 * padded * depth * chans, bytes_accessed=2 * depth * chans, transcendentals=0
        ),
        name="project_query",
    )(lhs, in_hbm(weight))
    taps = short_filter.reshape(9, chans)
    mixin, begin, final, query_send = pl.pallas_call(
        functools.partial(scan_kernel, rows, chans),
        out_shape=[
            shape((chans // LANES, rows, LANES), f32),
            shape((4, SUB, chans), f32),
            shape((4, chans), f32),
            shape((padded, chans), b16),
        ],
        compiler_params=params,
        name="scan",
    )(keep, more, query_send, taps, step, join)
    query_more = lax.ppermute(query_send, "seq", pairs)

    states = spread(final, "seq")
    gated = pl.pallas_call(
        functools.partial(gate_kernel, rows, chans),
        out_shape=shape((rows, chans), b16),
        scratch_shapes=[pltpu.VMEM((chans // LANES, rows, LANES), f32)],
        compiler_params=params,
        name="gate",
    )(states, jump, begin, reach, step, poles, bias[None, :], mixin, query_keep, query_more, taps)

    which = jnp.stack([lax.rem(here + hop + count, count) for hop in ring_hops(count)] + [half])
    parts = ring(gated, "ch")
    first, rest = mix(parts[:-1], which.astype(jnp.int32), second, out_weight.shape[1])
    return pl.pallas_call(
        last_mix_kernel,
        out_shape=shape(first.shape, b16),
        compiler_params=params,
        name="last_mix",
    )(parts[-1], rest, first)


def solution(mesh):
    placed = (
        P("seq", "ch"),
        P("seq", None, None),
        P("seq", "ch"),
        P(None, None, "ch"),
        P("ch", None),
        P("ch", None),
        P(None, "ch", None),
        P("ch"),
    )
    return jax.shard_map(
        body, mesh=mesh, in_specs=placed, out_specs=P("seq", "ch"), check_vma=False
    )
```

```python
import functools

import jax
import jax.numpy as jnp
from jax import lax
from jax.experimental import pallas as pl
from jax.experimental.pallas import tpu as pltpu
from jax.sharding import PartitionSpec as P

HALO = 16
LANES = 128
SUB = 8
VMEM = 24 * 1024 * 1024


def spread(x, axis):
    count = lax.axis_size(axis)
    return lax.all_to_all(
        jnp.broadcast_to(x[None], (count,) + x.shape), axis, 0, 0, tiled=True
    )


def ring_hops(count):
    hops = [0]
    for hop in range(1, count // 2 + 1):
        hops += [-hop, hop] if 2 * hop < count else [-hop]
    return hops


def ring(x, axis):
    count = lax.axis_size(axis)
    up = [(c, (c + 1) % count) for c in range(count)]
    down = [(c, (c - 1) % count) for c in range(count)]
    arrived = [x]
    below = above = x
    for hop in range(1, count // 2 + 1):
        below = lax.ppermute(below, axis, up)
        arrived.append(below)
        if 2 * hop < count:
            above = lax.ppermute(above, axis, down)
            arrived.append(above)
    return arrived


def powers(exponent, rate, turn):
    mag = jnp.exp(-exponent[:, None, None] * rate[None])
    phase = exponent[:, None, None] * turn[None]
    return mag * jnp.cos(phase), mag * jnp.sin(phase)


def fetch(w_ref, w, sems, starts, sizes):
    copies = []
    for j, (start, size) in enumerate(zip(starts, sizes)):
        at = sum(sizes[:j])
        copies.append(
            pltpu.make_async_copy(w_ref.at[:, pl.ds(start, size)], w.at[:, pl.ds(at, size)], sems.at[j])
        )
        copies[-1].start()
    return copies


def product(lhs_ref, w, copies, chans, keep_ref, send_ref):
    sides, rows, depth = lhs_ref.shape
    both = lhs_ref[...].reshape(sides * rows, depth)
    for j, copy in enumerate(copies):
        copy.wait()
        cols = slice(j * chans, (j + 1) * chans)
        part = jnp.dot(both, w[:, cols], preferred_element_type=jnp.float32)
        keep_ref[:, cols] = part[:rows]
        send_ref[:, cols] = part[rows:].astype(send_ref.dtype)


def mixin_project_kernel(count, place_ref, *refs):
    x_refs, (w_ref, keep_ref, send_ref, lhs_ref, w, sems) = refs[:count], refs[count:]
    chans = x_refs[0].shape[1]
    copies = fetch(w_ref, w, sems, (chans, 2 * chans), (chans, chans))
    half, here = place_ref[0], place_ref[1]
    for x_ref, hop in zip(x_refs, ring_hops(count)):
        origin = lax.rem(here + hop + count, count)
        side = jnp.where(lax.rem(origin, 2) == half, 0, 1)
        at = pl.multiple_of(lax.div(origin, 2) * chans, chans)
        lhs_ref[side, :, pl.ds(at, chans)] = x_ref[...]
    product(lhs_ref, w, copies, chans, keep_ref, send_ref)


def query_project_kernel(lhs_ref, w_ref, keep_ref, send_ref, w, sems):
    chans = keep_ref.shape[1]
    copies = fetch(w_ref, w, sems, (0,), (chans,))
    product(lhs_ref, w, copies, chans, keep_ref, send_ref)


def beside_kernel(x_ref, y_ref, out_ref, sem):
    cols = x_ref.shape[1]
    copy = pltpu.make_async_copy(x_ref, out_ref.at[:, pl.ds(0, cols)], sem)
    copy.start()
    out_ref[:, cols:] = y_ref[...]
    copy.wait()


def short_conv(rows, branch, total, taps_ref):
    now = total[:rows]
    past = total[rows : rows + 8]
    one = jnp.concatenate([past[1:2], now[:-1]], axis=0)
    two = jnp.concatenate([past[0:2], now[:-2]], axis=0)
    tap = [taps_ref[3 * j + branch : 3 * j + branch + 1, :] for j in range(3)]
    return tap[0] * now + tap[1] * one + tap[2] * two


def scan_kernel(
    rows,
    chans,
    keep_ref,
    more_ref,
    query_ref,
    taps_ref,
    step_ref,
    join_ref,
    mixin_ref,
    begin_ref,
    final_ref,
    send_ref,
):
    send_ref[...] = query_ref[...]
    length = rows // SUB

    def filtered(branch):
        cols = slice((branch - 1) * chans, branch * chans)
        total = keep_ref[:, cols] + more_ref[:, cols].astype(jnp.float32)
        return short_conv(rows, branch, total, taps_ref)

    mixin = filtered(1) * filtered(2)
    for q in range(chans // LANES):
        mixin_ref[q] = mixin[:, q * LANES : (q + 1) * LANES]
    for q in range(chans // LANES):
        cols = slice(q * LANES, (q + 1) * LANES)
        wide = lambda row: jnp.broadcast_to(row, (SUB, LANES))
        ar = [wide(step_ref[n : n + 1, cols]) for n in range(2)]
        ai = [wide(step_ref[2 + n : 3 + n, cols]) for n in range(2)]
        re = [jnp.zeros((SUB, LANES), jnp.float32)] * 2
        im = [jnp.zeros((SUB, LANES), jnp.float32)] * 2
        for i in range(length):
            u = mixin_ref[q, pl.ds(i, SUB, stride=length), :]
            for n in range(2):
                re[n], im[n] = ar[n] * re[n] - ai[n] * im[n] + u, ar[n] * im[n] + ai[n] * re[n]
        for n in range(2):
            jr = join_ref[n : n + 1, cols]
            ji = join_ref[2 + n : 3 + n, cols]
            er = jnp.zeros((1, LANES), jnp.float32)
            ei = jnp.zeros((1, LANES), jnp.float32)
            for b in range(SUB):
                begin_ref[n, b : b + 1, cols] = er
                begin_ref[2 + n, b : b + 1, cols] = ei
                er, ei = (
                    jr * er - ji * ei + re[n][b : b + 1],
                    jr * ei + ji * er + im[n][b : b + 1],
                )
            final_ref[n : n + 1, cols] = er
            final_ref[2 + n : 3 + n, cols] = ei


def gate_kernel(
    rows, chans, all_ref, jump_ref, begin_ref, reach_ref, step_ref, residue_ref, bias_ref, mixin_ref, keep_ref, more_ref, taps_ref, out_ref, long
):
    query = short_conv(rows, 0, keep_ref[...] + more_ref[...].astype(jnp.float32), taps_ref)
    length = rows // SUB
    entry = []
    for n in range(2):
        fr, fi = all_ref[:, n, :], all_ref[:, 2 + n, :]
        cr, ci = jump_ref[n], jump_ref[2 + n]
        gr = jnp.sum(cr * fr - ci * fi, axis=0, keepdims=True)
        gi = jnp.sum(cr * fi + ci * fr, axis=0, keepdims=True)
        rr, ri = reach_ref[n], reach_ref[2 + n]
        entry.append((begin_ref[n] + rr * gr - ri * gi, begin_ref[2 + n] + rr * gi + ri * gr))
    for q in range(chans // LANES):
        cols = slice(q * LANES, (q + 1) * LANES)
        wide = lambda row: jnp.broadcast_to(row, (SUB, LANES))
        ar = [wide(step_ref[n : n + 1, cols]) for n in range(2)]
        ai = [wide(step_ref[2 + n : 3 + n, cols]) for n in range(2)]
        pr = [wide(residue_ref[n : n + 1, cols]) for n in range(2)]
        pi = [wide(residue_ref[2 + n : 3 + n, cols]) for n in range(2)]
        direct = wide(bias_ref[:, cols])
        re = [entry[n][0][:, cols] for n in range(2)]
        im = [entry[n][1][:, cols] for n in range(2)]
        for i in range(length):
            u = mixin_ref[q, pl.ds(i, SUB, stride=length), :]
            y = direct * u
            for n in range(2):
                re[n], im[n] = ar[n] * re[n] - ai[n] * im[n] + u, ar[n] * im[n] + ai[n] * re[n]
                y = y + (pr[n] * re[n] - pi[n] * im[n])
            long[q, pl.ds(i, SUB, stride=length), :] = y
        out_ref[:, cols] = (query[:, cols] * long[q]).astype(out_ref.dtype)


def mix_kernel(count, which_ref, *refs):
    x_refs, (w_ref, out_ref, rest_ref, w, sems) = refs[: count - 1], refs[count - 1 :]
    chans = x_refs[0].shape[1]
    part = chans // 2
    copies = []
    for j in range(count):
        block = which_ref[j]
        other = jnp.where(lax.rem(block, 2) == which_ref[count], 0, 1)
        col = pl.multiple_of(other * chans, chans)
        pair = []
        for e in range(2):
            row = pl.multiple_of(lax.div(block, 2) * chans + jnp.where(other == e, 0, part), part)
            dst = rest_ref if j == count - 1 else w.at[j]
            pair.append(
                pltpu.make_async_copy(
                    w_ref.at[pl.ds(row, part), pl.ds(col, out_ref.shape[1])],
                    dst.at[pl.ds(e * part, part)],
                    sems.at[j, e],
                )
            )
            pair[-1].start()
        copies.append(pair)
    total = jnp.zeros(out_ref.shape, jnp.float32)
    for j in range(count):
        for copy in copies[j]:
            copy.wait()
        if j < count - 1:
            total = total + jnp.dot(x_refs[j][...], w[j], preferred_element_type=jnp.float32)
    out_ref[...] = total


def last_mix_kernel(x_ref, w_ref, base_ref, out_ref):
    total = base_ref[...] + jnp.dot(x_ref[...], w_ref[...], preferred_element_type=jnp.float32)
    out_ref[...] = total.astype(out_ref.dtype)


IN_VMEM = pl.BlockSpec(memory_space=pltpu.VMEM)
IN_SMEM = pl.BlockSpec(memory_space=pltpu.SMEM)
IN_HBM = pl.BlockSpec(memory_space=pltpu.HBM)
in_hbm = functools.partial(pltpu.with_memory_space_constraint, memory_space=pltpu.HBM)


def mix(blocks, which, weight, cols):
    rows, chans = blocks[0].shape
    count = len(blocks) + 1
    return pl.pallas_call(
        functools.partial(mix_kernel, count),
        in_specs=[IN_SMEM] + [IN_VMEM] * (count - 1) + [IN_HBM],
        out_shape=[
            jax.ShapeDtypeStruct((rows, cols), jnp.float32),
            jax.ShapeDtypeStruct((chans, cols), weight.dtype),
        ],
        scratch_shapes=[
            pltpu.VMEM((count - 1, chans, cols), weight.dtype),
            pltpu.SemaphoreType.DMA((count, 2)),
        ],
        compiler_params=pltpu.CompilerParams(vmem_limit_bytes=VMEM),
        cost_estimate=pl.CostEstimate(
            flops=2 * count * rows * chans * cols,
            bytes_accessed=2 * count * chans * cols,
            transcendentals=0,
        ),
        name="mix",
    )(which, *blocks, in_hbm(weight))


def body(inputs, in_weight, out_weight, short_filter, decay, angle, residue, bias):
    rows, chans = inputs.shape
    place, blocks = lax.axis_index("seq"), lax.axis_size("seq")
    count = lax.axis_size("ch")
    col_start = lax.axis_index("ch") * chans
    near = [(s % 8) // 4 for s in range(blocks)]
    mirror = [s + 6 - 4 * ((s % 8) // 2) for s in range(blocks)]
    cut = lax.dynamic_slice(in_weight, (0, 0, col_start), (in_weight.shape[0], 3, chans))
    own_weight = jnp.concatenate([cut[:, g] for g in range(3)], axis=1)
    pairs = [(s, mirror[s]) for s in range(blocks)]
    halves = [[s for s in range(blocks) if near[s] == h] for h in range(2)]
    gather = lambda x: lax.all_gather(x, "seq", axis=0, tiled=True, axis_index_groups=halves)
    weight = gather(own_weight)
    f32, b16 = jnp.float32, jnp.bfloat16
    padded, depth = rows + HALO, chans * count // 2
    params = pltpu.CompilerParams(vmem_limit_bytes=VMEM)
    shape = jax.ShapeDtypeStruct
    half = lax.rem(place, 8) // 4
    rim = lax.ppermute(inputs[-2:], "seq", [(i, i + 1) for i in range(blocks - 1)])
    mirrored = lax.ppermute(out_weight, "seq", pairs)
    rim, mirrored = lax.optimization_barrier((rim, mirrored))
    tokens = jnp.concatenate([inputs, rim, jnp.zeros((HALO - 2, chans), inputs.dtype)], axis=0)
    swaps = []
    for c in range(count):
        for s in range(blocks):
            to = (c, s) if c % 2 == near[s] else (c ^ 1, mirror[s])
            swaps.append((c * blocks + s, to[0] * blocks + to[1]))
    swapped = lax.ppermute(tokens, ("ch", "seq"), swaps)
    rate, turn = decay.T, angle.T
    length = rows // SUB
    pack = lambda pair: jnp.concatenate(pair, axis=1)
    step = pack(powers(jnp.ones((1,), jnp.float32), rate, turn))[0]
    join = pack(powers(jnp.full((1,), length, jnp.float32), rate, turn))[0]
    reach = pack(powers((jnp.arange(SUB) * length).astype(jnp.float32), rate, turn))
    reach = reach.transpose(1, 0, 2)
    gap = place - 1 - jnp.arange(blocks)
    jump = pack(powers((jnp.maximum(gap, 0) * rows).astype(jnp.float32), rate, turn))
    jump = jnp.where((gap >= 0)[:, None, None], jump, 0.0).transpose(1, 0, 2)
    poles = jnp.concatenate([residue[0].T, residue[1].T], axis=0)
    both = pl.pallas_call(
        beside_kernel,
        in_specs=[IN_HBM, IN_VMEM],
        out_shape=shape((out_weight.shape[0], 2 * out_weight.shape[1]), b16),
        scratch_shapes=[pltpu.SemaphoreType.DMA(())],
        compiler_params=params,
        name="beside",
    )(in_hbm(out_weight), mirrored)
    tied = lax.optimization_barrier((swapped, both, step, join, reach, jump, poles))
    swapped, both, step, join, reach, jump, poles = tied
    second = gather(both)
    features = ring(swapped, "ch")
    here = lax.axis_index("ch")

    keep, send, lhs = pl.pallas_call(
        functools.partial(mixin_project_kernel, count),
        in_specs=[IN_SMEM] + [IN_VMEM] * count + [IN_HBM],
        out_shape=[
            shape((padded, 2 * chans), f32),
            shape((padded, 2 * chans), b16),
            shape((2, padded, depth), b16),
        ],
        scratch_shapes=[pltpu.VMEM((depth, 2 * chans), b16), pltpu.SemaphoreType.DMA((2,))],
        compiler_params=params,
        cost_estimate=pl.CostEstimate(
            flops=8 * padded * depth * chans, bytes_accessed=4 * depth * chans, transcendentals=0
        ),
        name="project_mixin",
    )(jnp.stack([half, here]).astype(jnp.int32), *features, in_hbm(weight))
    more = lax.ppermute(send, "seq", pairs)
    query_keep, query_send = pl.pallas_call(
        query_project_kernel,
        in_specs=[IN_VMEM, IN_HBM],
        out_shape=[shape((padded, chans), f32), shape((padded, chans), b16)],
        scratch_shapes=[pltpu.VMEM((depth, chans), b16), pltpu.SemaphoreType.DMA((1,))],
        compiler_params=params,
        cost_estimate=pl.CostEstimate(
            flops=4 * padded * depth * chans, bytes_accessed=2 * depth * chans, transcendentals=0
        ),
        name="project_query",
    )(lhs, in_hbm(weight))
    taps = short_filter.reshape(9, chans)
    mixin, begin, final, query_send = pl.pallas_call(
        functools.partial(scan_kernel, rows, chans),
        out_shape=[
            shape((chans // LANES, rows, LANES), f32),
            shape((4, SUB, chans), f32),
            shape((4, chans), f32),
            shape((padded, chans), b16),
        ],
        compiler_params=params,
        name="scan",
    )(keep, more, query_send, taps, step, join)
    query_more = lax.ppermute(query_send, "seq", pairs)

    states = spread(final, "seq")
    gated = pl.pallas_call(
        functools.partial(gate_kernel, rows, chans),
        out_shape=shape((rows, chans), b16),
        scratch_shapes=[pltpu.VMEM((chans // LANES, rows, LANES), f32)],
        compiler_params=params,
        name="gate",
    )(states, jump, begin, reach, step, poles, bias[None, :], mixin, query_keep, query_more, taps)

    which = jnp.stack([lax.rem(here + hop + count, count) for hop in ring_hops(count)] + [half])
    parts = ring(gated, "ch")
    first, rest = mix(parts[:-1], which.astype(jnp.int32), second, out_weight.shape[1])
    return pl.pallas_call(
        last_mix_kernel,
        out_shape=shape(first.shape, b16),
        compiler_params=params,
        name="last_mix",
    )(parts[-1], rest, first)


def solution(mesh):
    placed = (
        P("seq", "ch"),
        P("seq", None, None),
        P("seq", "ch"),
        P(None, None, "ch"),
        P("ch", None),
        P("ch", None),
        P(None, "ch", None),
        P("ch"),
    )
    return jax.shard_map(
        body, mesh=mesh, in_specs=placed, out_specs=P("seq", "ch"), check_vma=False
    )
```

```python
import functools

import jax
import jax.numpy as jnp
from jax import lax
from jax.experimental import pallas as pl
from jax.experimental.pallas import tpu as pltpu
from jax.sharding import PartitionSpec as P

HALO = 16
LANES = 128
SUB = 8
VMEM = 24 * 1024 * 1024


def spread(x, axis):
    count = lax.axis_size(axis)
    return lax.all_to_all(
        jnp.broadcast_to(x[None], (count,) + x.shape), axis, 0, 0, tiled=True
    )


def ring_hops(count):
    hops = [0]
    for hop in range(1, count // 2 + 1):
        hops += [-hop, hop] if 2 * hop < count else [-hop]
    return hops


def ring(x):
    count, blocks = lax.axis_size("ch"), lax.axis_size("seq")
    onward = []
    for c in range(count):
        for s in range(blocks):
            to = (c + 1) % count if s % 2 == 0 else (c - 1) % count
            onward.append((c * blocks + s, to * blocks + s))
    hand = lambda block: lax.ppermute(block, "seq", [(s, s ^ 1) for s in range(blocks)])
    pair = jnp.stack([x, hand(x)])
    arrived = [x]
    for hop in range(1, count // 2):
        pair = lax.ppermute(pair, ("ch", "seq"), onward)
        arrived += [pair[0], hand(pair[1])]
    arrived.append(lax.ppermute(pair[0], ("ch", "seq"), onward))
    return arrived


def powers(exponent, rate, turn):
    mag = jnp.exp(-exponent[:, None, None] * rate[None])
    phase = exponent[:, None, None] * turn[None]
    return mag * jnp.cos(phase), mag * jnp.sin(phase)


def fetch(w_ref, w, sems, starts, sizes):
    copies = []
    for j, (start, size) in enumerate(zip(starts, sizes)):
        at = sum(sizes[:j])
        copies.append(
            pltpu.make_async_copy(w_ref.at[:, pl.ds(start, size)], w.at[:, pl.ds(at, size)], sems.at[j])
        )
        copies[-1].start()
    return copies


def product(lhs_ref, w, copies, chans, keep_ref, send_ref):
    sides, rows, depth = lhs_ref.shape
    both = lhs_ref[...].reshape(sides * rows, depth)
    for j, copy in enumerate(copies):
        copy.wait()
        cols = slice(j * chans, (j + 1) * chans)
        part = jnp.dot(both, w[:, cols], preferred_element_type=jnp.float32)
        keep_ref[:, cols] = part[:rows]
        send_ref[:, cols] = part[rows:].astype(send_ref.dtype)


def mixin_project_kernel(count, place_ref, *refs):
    x_refs, (w_ref, keep_ref, send_ref, lhs_ref, w, sems) = refs[:count], refs[count:]
    chans = x_refs[0].shape[1]
    copies = fetch(w_ref, w, sems, (chans, 2 * chans), (chans, chans))
    half, here, sign = place_ref[0], place_ref[1], place_ref[2]
    for x_ref, hop in zip(x_refs, ring_hops(count)):
        origin = lax.rem(here + sign * hop + count, count)
        side = jnp.where(lax.rem(origin, 2) == half, 0, 1)
        at = pl.multiple_of(lax.div(origin, 2) * chans, chans)
        lhs_ref[side, :, pl.ds(at, chans)] = x_ref[...]
    product(lhs_ref, w, copies, chans, keep_ref, send_ref)


def query_project_kernel(lhs_ref, w_ref, keep_ref, send_ref, w, sems):
    chans = keep_ref.shape[1]
    copies = fetch(w_ref, w, sems, (0,), (chans,))
    product(lhs_ref, w, copies, chans, keep_ref, send_ref)


def beside_kernel(x_ref, y_ref, out_ref, sem):
    cols = x_ref.shape[1]
    copy = pltpu.make_async_copy(x_ref, out_ref.at[:, pl.ds(0, cols)], sem)
    copy.start()
    out_ref[:, cols:] = y_ref[...]
    copy.wait()


def short_conv(rows, branch, total, taps_ref):
    now = total[:rows]
    past = total[rows : rows + 8]
    one = jnp.concatenate([past[1:2], now[:-1]], axis=0)
    two = jnp.concatenate([past[0:2], now[:-2]], axis=0)
    tap = [taps_ref[3 * j + branch : 3 * j + branch + 1, :] for j in range(3)]
    return tap[0] * now + tap[1] * one + tap[2] * two


def scan_kernel(
    rows,
    chans,
    keep_ref,
    more_ref,
    query_ref,
    taps_ref,
    step_ref,
    join_ref,
    mixin_ref,
    begin_ref,
    final_ref,
    send_ref,
):
    send_ref[...] = query_ref[...]
    length = rows // SUB

    def filtered(branch):
        cols = slice((branch - 1) * chans, branch * chans)
        total = keep_ref[:, cols] + more_ref[:, cols].astype(jnp.float32)
        return short_conv(rows, branch, total, taps_ref)

    mixin = filtered(1) * filtered(2)
    for q in range(chans // LANES):
        mixin_ref[q] = mixin[:, q * LANES : (q + 1) * LANES]
    for q in range(chans // LANES):
        cols = slice(q * LANES, (q + 1) * LANES)
        wide = lambda row: jnp.broadcast_to(row, (SUB, LANES))
        ar = [wide(step_ref[n : n + 1, cols]) for n in range(2)]
        ai = [wide(step_ref[2 + n : 3 + n, cols]) for n in range(2)]
        re = [jnp.zeros((SUB, LANES), jnp.float32)] * 2
        im = [jnp.zeros((SUB, LANES), jnp.float32)] * 2
        for i in range(length):
            u = mixin_ref[q, pl.ds(i, SUB, stride=length), :]
            for n in range(2):
                re[n], im[n] = ar[n] * re[n] - ai[n] * im[n] + u, ar[n] * im[n] + ai[n] * re[n]
        for n in range(2):
            jr = join_ref[n : n + 1, cols]
            ji = join_ref[2 + n : 3 + n, cols]
            er = jnp.zeros((1, LANES), jnp.float32)
            ei = jnp.zeros((1, LANES), jnp.float32)
            for b in range(SUB):
                begin_ref[n, b : b + 1, cols] = er
                begin_ref[2 + n, b : b + 1, cols] = ei
                er, ei = (
                    jr * er - ji * ei + re[n][b : b + 1],
                    jr * ei + ji * er + im[n][b : b + 1],
                )
            final_ref[n : n + 1, cols] = er
            final_ref[2 + n : 3 + n, cols] = ei


def gate_kernel(
    rows, chans, all_ref, jump_ref, begin_ref, reach_ref, step_ref, residue_ref, bias_ref, mixin_ref, keep_ref, more_ref, taps_ref, out_ref, long
):
    query = short_conv(rows, 0, keep_ref[...] + more_ref[...].astype(jnp.float32), taps_ref)
    length = rows // SUB
    entry = []
    for n in range(2):
        fr, fi = all_ref[:, n, :], all_ref[:, 2 + n, :]
        cr, ci = jump_ref[n], jump_ref[2 + n]
        gr = jnp.sum(cr * fr - ci * fi, axis=0, keepdims=True)
        gi = jnp.sum(cr * fi + ci * fr, axis=0, keepdims=True)
        rr, ri = reach_ref[n], reach_ref[2 + n]
        entry.append((begin_ref[n] + rr * gr - ri * gi, begin_ref[2 + n] + rr * gi + ri * gr))
    for q in range(chans // LANES):
        cols = slice(q * LANES, (q + 1) * LANES)
        wide = lambda row: jnp.broadcast_to(row, (SUB, LANES))
        ar = [wide(step_ref[n : n + 1, cols]) for n in range(2)]
        ai = [wide(step_ref[2 + n : 3 + n, cols]) for n in range(2)]
        pr = [wide(residue_ref[n : n + 1, cols]) for n in range(2)]
        pi = [wide(residue_ref[2 + n : 3 + n, cols]) for n in range(2)]
        direct = wide(bias_ref[:, cols])
        re = [entry[n][0][:, cols] for n in range(2)]
        im = [entry[n][1][:, cols] for n in range(2)]
        for i in range(length):
            u = mixin_ref[q, pl.ds(i, SUB, stride=length), :]
            y = direct * u
            for n in range(2):
                re[n], im[n] = ar[n] * re[n] - ai[n] * im[n] + u, ar[n] * im[n] + ai[n] * re[n]
                y = y + (pr[n] * re[n] - pi[n] * im[n])
            long[q, pl.ds(i, SUB, stride=length), :] = y
        out_ref[:, cols] = (query[:, cols] * long[q]).astype(out_ref.dtype)


def mix_kernel(count, which_ref, *refs):
    x_refs, (w_ref, out_ref, rest_ref, w, sems) = refs[: count - 1], refs[count - 1 :]
    chans = x_refs[0].shape[1]
    part = chans // 2
    copies = []
    for j in range(count):
        block = which_ref[j]
        other = jnp.where(lax.rem(block, 2) == which_ref[count], 0, 1)
        col = pl.multiple_of(other * chans, chans)
        pair = []
        for e in range(2):
            row = pl.multiple_of(lax.div(block, 2) * chans + jnp.where(other == e, 0, part), part)
            dst = rest_ref if j == count - 1 else w.at[j]
            pair.append(
                pltpu.make_async_copy(
                    w_ref.at[pl.ds(row, part), pl.ds(col, out_ref.shape[1])],
                    dst.at[pl.ds(e * part, part)],
                    sems.at[j, e],
                )
            )
            pair[-1].start()
        copies.append(pair)
    total = jnp.zeros(out_ref.shape, jnp.float32)
    for j in range(count):
        for copy in copies[j]:
            copy.wait()
        if j < count - 1:
            total = total + jnp.dot(x_refs[j][...], w[j], preferred_element_type=jnp.float32)
    out_ref[...] = total


def last_mix_kernel(x_ref, w_ref, base_ref, out_ref):
    total = base_ref[...] + jnp.dot(x_ref[...], w_ref[...], preferred_element_type=jnp.float32)
    out_ref[...] = total.astype(out_ref.dtype)


IN_VMEM = pl.BlockSpec(memory_space=pltpu.VMEM)
IN_SMEM = pl.BlockSpec(memory_space=pltpu.SMEM)
IN_HBM = pl.BlockSpec(memory_space=pltpu.HBM)
in_hbm = functools.partial(pltpu.with_memory_space_constraint, memory_space=pltpu.HBM)


def mix(blocks, which, weight, cols):
    rows, chans = blocks[0].shape
    count = len(blocks) + 1
    return pl.pallas_call(
        functools.partial(mix_kernel, count),
        in_specs=[IN_SMEM] + [IN_VMEM] * (count - 1) + [IN_HBM],
        out_shape=[
            jax.ShapeDtypeStruct((rows, cols), jnp.float32),
            jax.ShapeDtypeStruct((chans, cols), weight.dtype),
        ],
        scratch_shapes=[
            pltpu.VMEM((count - 1, chans, cols), weight.dtype),
            pltpu.SemaphoreType.DMA((count, 2)),
        ],
        compiler_params=pltpu.CompilerParams(vmem_limit_bytes=VMEM),
        cost_estimate=pl.CostEstimate(
            flops=2 * count * rows * chans * cols,
            bytes_accessed=2 * count * chans * cols,
            transcendentals=0,
        ),
        name="mix",
    )(which, *blocks, in_hbm(weight))


def body(inputs, in_weight, out_weight, short_filter, decay, angle, residue, bias):
    rows, chans = inputs.shape
    place, blocks = lax.axis_index("seq"), lax.axis_size("seq")
    count = lax.axis_size("ch")
    col_start = lax.axis_index("ch") * chans
    near = [(s % 8) // 4 for s in range(blocks)]
    mirror = [s + 6 - 4 * ((s % 8) // 2) for s in range(blocks)]
    cut = lax.dynamic_slice(in_weight, (0, 0, col_start), (in_weight.shape[0], 3, chans))
    own_weight = jnp.concatenate([cut[:, g] for g in range(3)], axis=1)
    pairs = [(s, mirror[s]) for s in range(blocks)]
    halves = [[s for s in range(blocks) if near[s] == h] for h in range(2)]
    gather = lambda x: lax.all_gather(x, "seq", axis=0, tiled=True, axis_index_groups=halves)
    weight = gather(own_weight)
    f32, b16 = jnp.float32, jnp.bfloat16
    padded, depth = rows + HALO, chans * count // 2
    params = pltpu.CompilerParams(vmem_limit_bytes=VMEM)
    shape = jax.ShapeDtypeStruct
    half = lax.rem(place, 8) // 4
    rim = lax.ppermute(inputs[-2:], "seq", [(i, i + 1) for i in range(blocks - 1)])
    mirrored = lax.ppermute(out_weight, "seq", pairs)
    rim, mirrored = lax.optimization_barrier((rim, mirrored))
    tokens = jnp.concatenate([inputs, rim, jnp.zeros((HALO - 2, chans), inputs.dtype)], axis=0)
    swaps = []
    for c in range(count):
        for s in range(blocks):
            to = (c, s) if c % 2 == near[s] else (c ^ 1, mirror[s])
            swaps.append((c * blocks + s, to[0] * blocks + to[1]))
    swapped = lax.ppermute(tokens, ("ch", "seq"), swaps)
    rate, turn = decay.T, angle.T
    length = rows // SUB
    pack = lambda pair: jnp.concatenate(pair, axis=1)
    step = pack(powers(jnp.ones((1,), jnp.float32), rate, turn))[0]
    join = pack(powers(jnp.full((1,), length, jnp.float32), rate, turn))[0]
    reach = pack(powers((jnp.arange(SUB) * length).astype(jnp.float32), rate, turn))
    reach = reach.transpose(1, 0, 2)
    gap = place - 1 - jnp.arange(blocks)
    jump = pack(powers((jnp.maximum(gap, 0) * rows).astype(jnp.float32), rate, turn))
    jump = jnp.where((gap >= 0)[:, None, None], jump, 0.0).transpose(1, 0, 2)
    poles = jnp.concatenate([residue[0].T, residue[1].T], axis=0)
    both = pl.pallas_call(
        beside_kernel,
        in_specs=[IN_HBM, IN_VMEM],
        out_shape=shape((out_weight.shape[0], 2 * out_weight.shape[1]), b16),
        scratch_shapes=[pltpu.SemaphoreType.DMA(())],
        compiler_params=params,
        name="beside",
    )(in_hbm(out_weight), mirrored)
    tied = lax.optimization_barrier((swapped, both, step, join, reach, jump, poles))
    swapped, both, step, join, reach, jump, poles = tied
    second = gather(both)
    features = ring(swapped)
    here = lax.axis_index("ch")
    sign = 1 - 2 * lax.rem(place, 2)

    keep, send, lhs = pl.pallas_call(
        functools.partial(mixin_project_kernel, count),
        in_specs=[IN_SMEM] + [IN_VMEM] * count + [IN_HBM],
        out_shape=[
            shape((padded, 2 * chans), f32),
            shape((padded, 2 * chans), b16),
            shape((2, padded, depth), b16),
        ],
        scratch_shapes=[pltpu.VMEM((depth, 2 * chans), b16), pltpu.SemaphoreType.DMA((2,))],
        compiler_params=params,
        cost_estimate=pl.CostEstimate(
            flops=8 * padded * depth * chans, bytes_accessed=4 * depth * chans, transcendentals=0
        ),
        name="project_mixin",
    )(jnp.stack([half, here, sign]).astype(jnp.int32), *features, in_hbm(weight))
    more = lax.ppermute(send, "seq", pairs)
    query_keep, query_send = pl.pallas_call(
        query_project_kernel,
        in_specs=[IN_VMEM, IN_HBM],
        out_shape=[shape((padded, chans), f32), shape((padded, chans), b16)],
        scratch_shapes=[pltpu.VMEM((depth, chans), b16), pltpu.SemaphoreType.DMA((1,))],
        compiler_params=params,
        cost_estimate=pl.CostEstimate(
            flops=4 * padded * depth * chans, bytes_accessed=2 * depth * chans, transcendentals=0
        ),
        name="project_query",
    )(lhs, in_hbm(weight))
    taps = short_filter.reshape(9, chans)
    mixin, begin, final, query_send = pl.pallas_call(
        functools.partial(scan_kernel, rows, chans),
        out_shape=[
            shape((chans // LANES, rows, LANES), f32),
            shape((4, SUB, chans), f32),
            shape((4, chans), f32),
            shape((padded, chans), b16),
        ],
        compiler_params=params,
        name="scan",
    )(keep, more, query_send, taps, step, join)
    query_more = lax.ppermute(query_send, "seq", pairs)

    states = spread(final, "seq")
    gated = pl.pallas_call(
        functools.partial(gate_kernel, rows, chans),
        out_shape=shape((rows, chans), b16),
        scratch_shapes=[pltpu.VMEM((chans // LANES, rows, LANES), f32)],
        compiler_params=params,
        name="gate",
    )(states, jump, begin, reach, step, poles, bias[None, :], mixin, query_keep, query_more, taps)

    which = jnp.stack([lax.rem(here + sign * hop + count, count) for hop in ring_hops(count)] + [half])
    parts = ring(gated)
    first, rest = mix(parts[:-1], which.astype(jnp.int32), second, out_weight.shape[1])
    return pl.pallas_call(
        last_mix_kernel,
        out_shape=shape(first.shape, b16),
        compiler_params=params,
        name="last_mix",
    )(parts[-1], rest, first)


def solution(mesh):
    placed = (
        P("seq", "ch"),
        P("seq", None, None),
        P("seq", "ch"),
        P(None, None, "ch"),
        P("ch", None),
        P("ch", None),
        P(None, "ch", None),
        P("ch"),
    )
    return jax.shard_map(
        body, mesh=mesh, in_specs=placed, out_specs=P("seq", "ch"), check_vma=False
    )
```

```python
import functools

import jax
import jax.numpy as jnp
from jax import lax
from jax.experimental import pallas as pl
from jax.experimental.pallas import tpu as pltpu
from jax.sharding import PartitionSpec as P

HALO = 16
LANES = 128
SUB = 8
VMEM = 24 * 1024 * 1024


def spread(x, axis):
    count = lax.axis_size(axis)
    return lax.all_to_all(
        jnp.broadcast_to(x[None], (count,) + x.shape), axis, 0, 0, tiled=True
    )


def ring_hops(count):
    hops = [0]
    for hop in range(1, count // 2 + 1):
        hops += [-hop, hop] if 2 * hop < count else [-hop]
    return hops


def ring(x, axis):
    count = lax.axis_size(axis)
    up = [(c, (c + 1) % count) for c in range(count)]
    down = [(c, (c - 1) % count) for c in range(count)]
    arrived = [x]
    below = above = x
    for hop in range(1, count // 2 + 1):
        below = lax.ppermute(below, axis, up)
        arrived.append(below)
        if 2 * hop < count:
            above = lax.ppermute(above, axis, down)
            arrived.append(above)
    return arrived


def powers_kernel(rows, place_ref, rate_ref, turn_ref, residue_ref, step_ref, join_ref, reach_ref, jump_ref, poles_ref):
    chans = rate_ref.shape[1]
    length = rows // SUB
    blocks = jump_ref.shape[1]
    gap = place_ref[0] - 1 - lax.broadcasted_iota(jnp.int32, (blocks, chans), 0)
    far = (jnp.maximum(gap, 0) * rows).astype(jnp.float32)
    near = (lax.broadcasted_iota(jnp.int32, (SUB, chans), 0) * length).astype(jnp.float32)
    short = jnp.where(lax.broadcasted_iota(jnp.int32, (SUB, chans), 0) == 0, 1.0, float(length))
    for n in range(2):
        rate, turn = rate_ref[n : n + 1, :], turn_ref[n : n + 1, :]
        mag, phase = jnp.exp(-far * rate), far * turn
        jump_ref[n] = jnp.where(gap >= 0, mag * jnp.cos(phase), 0.0)
        jump_ref[2 + n] = jnp.where(gap >= 0, mag * jnp.sin(phase), 0.0)
        mag, phase = jnp.exp(-near * rate), near * turn
        reach_ref[n] = mag * jnp.cos(phase)
        reach_ref[2 + n] = mag * jnp.sin(phase)
        mag, phase = jnp.exp(-short * rate), short * turn
        re, im = mag * jnp.cos(phase), mag * jnp.sin(phase)
        step_ref[n : n + 1, :] = re[0:1]
        step_ref[2 + n : 3 + n, :] = im[0:1]
        join_ref[n : n + 1, :] = re[1:2]
        join_ref[2 + n : 3 + n, :] = im[1:2]
        poles_ref[n : n + 1, :] = residue_ref[0, n : n + 1, :]
        poles_ref[2 + n : 3 + n, :] = residue_ref[1, n : n + 1, :]


def fetch(w_ref, w, sems, starts, sizes):
    copies = []
    for j, (start, size) in enumerate(zip(starts, sizes)):
        at = sum(sizes[:j])
        copies.append(
            pltpu.make_async_copy(w_ref.at[:, pl.ds(start, size)], w.at[:, pl.ds(at, size)], sems.at[j])
        )
        copies[-1].start()
    return copies


def product(lhs_ref, w, copies, chans, keep_ref, send_ref):
    sides, rows, depth = lhs_ref.shape
    both = lhs_ref[...].reshape(sides * rows, depth)
    for j, copy in enumerate(copies):
        copy.wait()
        cols = slice(j * chans, (j + 1) * chans)
        part = jnp.dot(both, w[:, cols], preferred_element_type=jnp.float32)
        keep_ref[:, cols] = part[:rows]
        send_ref[:, cols] = part[rows:].astype(send_ref.dtype)


def mixin_project_kernel(count, place_ref, *refs):
    x_refs, (w_ref, keep_ref, send_ref, lhs_ref, w, sems) = refs[:count], refs[count:]
    chans = x_refs[0].shape[1]
    copies = fetch(w_ref, w, sems, (chans, 2 * chans), (chans, chans))
    half, here = place_ref[0], place_ref[1]
    for x_ref, hop in zip(x_refs, ring_hops(count)):
        origin = lax.rem(here + hop + count, count)
        side = jnp.where(lax.rem(origin, 2) == half, 0, 1)
        at = pl.multiple_of(lax.div(origin, 2) * chans, chans)
        lhs_ref[side, :, pl.ds(at, chans)] = x_ref[...]
    product(lhs_ref, w, copies, chans, keep_ref, send_ref)


def query_project_kernel(lhs_ref, w_ref, keep_ref, send_ref, w, sems):
    chans = keep_ref.shape[1]
    copies = fetch(w_ref, w, sems, (0,), (chans,))
    product(lhs_ref, w, copies, chans, keep_ref, send_ref)


def beside_kernel(x_ref, y_ref, out_ref, sem):
    cols = x_ref.shape[1]
    copy = pltpu.make_async_copy(x_ref, out_ref.at[:, pl.ds(0, cols)], sem)
    copy.start()
    out_ref[:, cols:] = y_ref[...]
    copy.wait()


def short_conv(rows, branch, total, taps_ref):
    now = total[:rows]
    past = total[rows : rows + 8]
    one = jnp.concatenate([past[1:2], now[:-1]], axis=0)
    two = jnp.concatenate([past[0:2], now[:-2]], axis=0)
    tap = [taps_ref[j, branch : branch + 1, :] for j in range(3)]
    return tap[0] * now + tap[1] * one + tap[2] * two


def scan_kernel(
    rows,
    chans,
    keep_ref,
    more_ref,
    query_ref,
    taps_ref,
    step_ref,
    join_ref,
    mixin_ref,
    begin_ref,
    final_ref,
    send_ref,
):
    send_ref[...] = query_ref[...]
    length = rows // SUB

    def filtered(branch):
        cols = slice((branch - 1) * chans, branch * chans)
        total = keep_ref[:, cols] + more_ref[:, cols].astype(jnp.float32)
        return short_conv(rows, branch, total, taps_ref)

    mixin = filtered(1) * filtered(2)
    for q in range(chans // LANES):
        mixin_ref[q] = mixin[:, q * LANES : (q + 1) * LANES]
    for q in range(chans // LANES):
        cols = slice(q * LANES, (q + 1) * LANES)
        wide = lambda row: jnp.broadcast_to(row, (SUB, LANES))
        ar = [wide(step_ref[n : n + 1, cols]) for n in range(2)]
        ai = [wide(step_ref[2 + n : 3 + n, cols]) for n in range(2)]
        re = [jnp.zeros((SUB, LANES), jnp.float32)] * 2
        im = [jnp.zeros((SUB, LANES), jnp.float32)] * 2
        for i in range(length):
            u = mixin_ref[q, pl.ds(i, SUB, stride=length), :]
            for n in range(2):
                re[n], im[n] = ar[n] * re[n] - ai[n] * im[n] + u, ar[n] * im[n] + ai[n] * re[n]
        for n in range(2):
            jr = join_ref[n : n + 1, cols]
            ji = join_ref[2 + n : 3 + n, cols]
            er = jnp.zeros((1, LANES), jnp.float32)
            ei = jnp.zeros((1, LANES), jnp.float32)
            for b in range(SUB):
                begin_ref[n, b : b + 1, cols] = er
                begin_ref[2 + n, b : b + 1, cols] = ei
                er, ei = (
                    jr * er - ji * ei + re[n][b : b + 1],
                    jr * ei + ji * er + im[n][b : b + 1],
                )
            final_ref[n : n + 1, cols] = er
            final_ref[2 + n : 3 + n, cols] = ei


def gate_kernel(
    rows, chans, all_ref, jump_ref, begin_ref, reach_ref, step_ref, residue_ref, bias_ref, mixin_ref, keep_ref, more_ref, taps_ref, out_ref, long
):
    query = short_conv(rows, 0, keep_ref[...] + more_ref[...].astype(jnp.float32), taps_ref)
    length = rows // SUB
    entry = []
    for n in range(2):
        fr, fi = all_ref[:, n, :], all_ref[:, 2 + n, :]
        cr, ci = jump_ref[n], jump_ref[2 + n]
        gr = jnp.sum(cr * fr - ci * fi, axis=0, keepdims=True)
        gi = jnp.sum(cr * fi + ci * fr, axis=0, keepdims=True)
        rr, ri = reach_ref[n], reach_ref[2 + n]
        entry.append((begin_ref[n] + rr * gr - ri * gi, begin_ref[2 + n] + rr * gi + ri * gr))
    for q in range(chans // LANES):
        cols = slice(q * LANES, (q + 1) * LANES)
        wide = lambda row: jnp.broadcast_to(row, (SUB, LANES))
        ar = [wide(step_ref[n : n + 1, cols]) for n in range(2)]
        ai = [wide(step_ref[2 + n : 3 + n, cols]) for n in range(2)]
        pr = [wide(residue_ref[n : n + 1, cols]) for n in range(2)]
        pi = [wide(residue_ref[2 + n : 3 + n, cols]) for n in range(2)]
        direct = wide(bias_ref[:, cols])
        re = [entry[n][0][:, cols] for n in range(2)]
        im = [entry[n][1][:, cols] for n in range(2)]
        for i in range(length):
            u = mixin_ref[q, pl.ds(i, SUB, stride=length), :]
            y = direct * u
            for n in range(2):
                re[n], im[n] = ar[n] * re[n] - ai[n] * im[n] + u, ar[n] * im[n] + ai[n] * re[n]
                y = y + (pr[n] * re[n] - pi[n] * im[n])
            long[q, pl.ds(i, SUB, stride=length), :] = y
        out_ref[:, cols] = (query[:, cols] * long[q]).astype(out_ref.dtype)


def mix_kernel(count, which_ref, *refs):
    x_refs, (w_ref, out_ref, rest_ref, w, sems) = refs[: count - 1], refs[count - 1 :]
    chans = x_refs[0].shape[1]
    part = chans // 2
    copies = []
    for j in range(count):
        block = which_ref[j]
        other = jnp.where(lax.rem(block, 2) == which_ref[count], 0, 1)
        col = pl.multiple_of(other * chans, chans)
        pair = []
        for e in range(2):
            row = pl.multiple_of(lax.div(block, 2) * chans + jnp.where(other == e, 0, part), part)
            dst = rest_ref if j == count - 1 else w.at[j]
            pair.append(
                pltpu.make_async_copy(
                    w_ref.at[pl.ds(row, part), pl.ds(col, out_ref.shape[1])],
                    dst.at[pl.ds(e * part, part)],
                    sems.at[j, e],
                )
            )
            pair[-1].start()
        copies.append(pair)
    total = jnp.zeros(out_ref.shape, jnp.float32)
    for j in range(count):
        for copy in copies[j]:
            copy.wait()
        if j < count - 1:
            total = total + jnp.dot(x_refs[j][...], w[j], preferred_element_type=jnp.float32)
    out_ref[...] = total


def last_mix_kernel(x_ref, w_ref, base_ref, out_ref):
    total = base_ref[...] + jnp.dot(x_ref[...], w_ref[...], preferred_element_type=jnp.float32)
    out_ref[...] = total.astype(out_ref.dtype)


IN_VMEM = pl.BlockSpec(memory_space=pltpu.VMEM)
IN_SMEM = pl.BlockSpec(memory_space=pltpu.SMEM)
IN_HBM = pl.BlockSpec(memory_space=pltpu.HBM)
in_hbm = functools.partial(pltpu.with_memory_space_constraint, memory_space=pltpu.HBM)


def mix(blocks, which, weight, cols):
    rows, chans = blocks[0].shape
    count = len(blocks) + 1
    return pl.pallas_call(
        functools.partial(mix_kernel, count),
        in_specs=[IN_SMEM] + [IN_VMEM] * (count - 1) + [IN_HBM],
        out_shape=[
            jax.ShapeDtypeStruct((rows, cols), jnp.float32),
            jax.ShapeDtypeStruct((chans, cols), weight.dtype),
        ],
        scratch_shapes=[
            pltpu.VMEM((count - 1, chans, cols), weight.dtype),
            pltpu.SemaphoreType.DMA((count, 2)),
        ],
        compiler_params=pltpu.CompilerParams(vmem_limit_bytes=VMEM),
        cost_estimate=pl.CostEstimate(
            flops=2 * count * rows * chans * cols,
            bytes_accessed=2 * count * chans * cols,
            transcendentals=0,
        ),
        name="mix",
    )(which, *blocks, in_hbm(weight))


def body(inputs, in_weight, out_weight, short_filter, decay, angle, residue, bias):
    rows, chans = inputs.shape
    place, blocks = lax.axis_index("seq"), lax.axis_size("seq")
    count = lax.axis_size("ch")
    col_start = lax.axis_index("ch") * chans
    near = [(s % 8) // 4 for s in range(blocks)]
    mirror = [s + 6 - 4 * ((s % 8) // 2) for s in range(blocks)]
    cut = lax.dynamic_slice(in_weight, (0, 0, col_start), (in_weight.shape[0], 3, chans))
    own_weight = jnp.concatenate([cut[:, g] for g in range(3)], axis=1)
    pairs = [(s, mirror[s]) for s in range(blocks)]
    halves = [[s for s in range(blocks) if near[s] == h] for h in range(2)]
    gather = lambda x: lax.all_gather(x, "seq", axis=0, tiled=True, axis_index_groups=halves)
    weight = gather(own_weight)
    f32, b16 = jnp.float32, jnp.bfloat16
    padded, depth = rows + HALO, chans * count // 2
    params = pltpu.CompilerParams(vmem_limit_bytes=VMEM)
    shape = jax.ShapeDtypeStruct
    half = lax.rem(place, 8) // 4
    rim = lax.ppermute(inputs[-2:], "seq", [(i, i + 1) for i in range(blocks - 1)])
    mirrored = lax.ppermute(out_weight, "seq", pairs)
    rim, mirrored = lax.optimization_barrier((rim, mirrored))
    tokens = jnp.concatenate([inputs, rim, jnp.zeros((HALO - 2, chans), inputs.dtype)], axis=0)
    swaps = []
    for c in range(count):
        for s in range(blocks):
            to = (c, s) if c % 2 == near[s] else (c ^ 1, mirror[s])
            swaps.append((c * blocks + s, to[0] * blocks + to[1]))
    swapped = lax.ppermute(tokens, ("ch", "seq"), swaps)
    step, join, reach, jump, poles = pl.pallas_call(
        functools.partial(powers_kernel, rows),
        in_specs=[IN_SMEM] + [IN_VMEM] * 3,
        out_shape=[
            shape((4, chans), f32),
            shape((4, chans), f32),
            shape((4, SUB, chans), f32),
            shape((4, blocks, chans), f32),
            shape((4, chans), f32),
        ],
        compiler_params=params,
        name="powers",
    )(place.reshape(1).astype(jnp.int32), decay.T, angle.T, residue.transpose(0, 2, 1))
    both = pl.pallas_call(
        beside_kernel,
        in_specs=[IN_HBM, IN_VMEM],
        out_shape=shape((out_weight.shape[0], 2 * out_weight.shape[1]), b16),
        scratch_shapes=[pltpu.SemaphoreType.DMA(())],
        compiler_params=params,
        name="beside",
    )(in_hbm(out_weight), mirrored)
    tied = lax.optimization_barrier((swapped, both, step, join, reach, jump, poles))
    swapped, both, step, join, reach, jump, poles = tied
    second = gather(both)
    features = ring(swapped, "ch")
    here = lax.axis_index("ch")

    keep, send, lhs = pl.pallas_call(
        functools.partial(mixin_project_kernel, count),
        in_specs=[IN_SMEM] + [IN_VMEM] * count + [IN_HBM],
        out_shape=[
            pltpu.VMEM((padded, 2 * chans), f32),
            pltpu.VMEM((padded, 2 * chans), b16),
            shape((2, padded, depth), b16),
        ],
        scratch_shapes=[pltpu.VMEM((depth, 2 * chans), b16), pltpu.SemaphoreType.DMA((2,))],
        compiler_params=params,
        cost_estimate=pl.CostEstimate(
            flops=8 * padded * depth * chans, bytes_accessed=4 * depth * chans, transcendentals=0
        ),
        name="project_mixin",
    )(jnp.stack([half, here]).astype(jnp.int32), *features, in_hbm(weight))
    more = lax.ppermute(send, "seq", pairs)
    query_keep, query_send = pl.pallas_call(
        query_project_kernel,
        in_specs=[IN_VMEM, IN_HBM],
        out_shape=[shape((padded, chans), f32), shape((padded, chans), b16)],
        scratch_shapes=[pltpu.VMEM((depth, chans), b16), pltpu.SemaphoreType.DMA((1,))],
        compiler_params=params,
        cost_estimate=pl.CostEstimate(
            flops=4 * padded * depth * chans, bytes_accessed=2 * depth * chans, transcendentals=0
        ),
        name="project_query",
    )(lhs, in_hbm(weight))
    taps = short_filter
    mixin, begin, final, query_send = pl.pallas_call(
        functools.partial(scan_kernel, rows, chans),
        out_shape=[
            shape((chans // LANES, rows, LANES), f32),
            shape((4, SUB, chans), f32),
            shape((4, chans), f32),
            shape((padded, chans), b16),
        ],
        compiler_params=params,
        name="scan",
    )(keep, more, query_send, taps, step, join)
    query_more = lax.ppermute(query_send, "seq", pairs)

    states = spread(final, "seq")
    gated = pl.pallas_call(
        functools.partial(gate_kernel, rows, chans),
        out_shape=shape((rows, chans), b16),
        scratch_shapes=[pltpu.VMEM((chans // LANES, rows, LANES), f32)],
        compiler_params=params,
        name="gate",
    )(states, jump, begin, reach, step, poles, bias[None, :], mixin, query_keep, query_more, taps)

    which = jnp.stack([lax.rem(here + hop + count, count) for hop in ring_hops(count)] + [half])
    parts = ring(gated, "ch")
    first, rest = mix(parts[:-1], which.astype(jnp.int32), second, out_weight.shape[1])
    return pl.pallas_call(
        last_mix_kernel,
        out_shape=shape(first.shape, b16),
        compiler_params=params,
        name="last_mix",
    )(parts[-1], rest, first)


def solution(mesh):
    placed = (
        P("seq", "ch"),
        P("seq", None, None),
        P("seq", "ch"),
        P(None, None, "ch"),
        P("ch", None),
        P("ch", None),
        P(None, "ch", None),
        P("ch"),
    )
    return jax.shard_map(
        body, mesh=mesh, in_specs=placed, out_specs=P("seq", "ch"), check_vma=False
    )
```

```python
import functools

import jax
import jax.numpy as jnp
from jax import lax
from jax.experimental import pallas as pl
from jax.experimental.pallas import tpu as pltpu
from jax.sharding import PartitionSpec as P

HALO = 16
LANES = 128
SUB = 8
VMEM = 24 * 1024 * 1024


def spread(x, axis):
    count = lax.axis_size(axis)
    return lax.all_to_all(
        jnp.broadcast_to(x[None], (count,) + x.shape), axis, 0, 0, tiled=True
    )


def ring_hops(count):
    hops = [0]
    for hop in range(1, count // 2 + 1):
        hops += [-hop, hop] if 2 * hop < count else [-hop]
    return hops


def ring(x):
    count, blocks = lax.axis_size("ch"), lax.axis_size("seq")

    def onward(turn):
        pairs = []
        for c in range(count):
            for s in range(blocks):
                to = (c + 1 if s % 2 == turn else c - 1) % count
                pairs.append((c * blocks + s, to * blocks + s))
        return pairs

    first, second = onward(0), onward(1)
    arrived = [x]
    below = above = x
    for hop in range(1, count // 2 + 1):
        below = lax.ppermute(below, ("ch", "seq"), first)
        arrived.append(below)
        if 2 * hop < count:
            above = lax.ppermute(above, ("ch", "seq"), second)
            arrived.append(above)
    return arrived


def powers_kernel(rows, place_ref, rate_ref, turn_ref, residue_ref, step_ref, join_ref, reach_ref, jump_ref, poles_ref):
    chans = rate_ref.shape[1]
    length = rows // SUB
    blocks = jump_ref.shape[1]
    gap = place_ref[0] - 1 - lax.broadcasted_iota(jnp.int32, (blocks, chans), 0)
    far = (jnp.maximum(gap, 0) * rows).astype(jnp.float32)
    near = (lax.broadcasted_iota(jnp.int32, (SUB, chans), 0) * length).astype(jnp.float32)
    short = jnp.where(lax.broadcasted_iota(jnp.int32, (SUB, chans), 0) == 0, 1.0, float(length))
    for n in range(2):
        rate, turn = rate_ref[n : n + 1, :], turn_ref[n : n + 1, :]
        mag, phase = jnp.exp(-far * rate), far * turn
        jump_ref[n] = jnp.where(gap >= 0, mag * jnp.cos(phase), 0.0)
        jump_ref[2 + n] = jnp.where(gap >= 0, mag * jnp.sin(phase), 0.0)
        mag, phase = jnp.exp(-near * rate), near * turn
        reach_ref[n] = mag * jnp.cos(phase)
        reach_ref[2 + n] = mag * jnp.sin(phase)
        mag, phase = jnp.exp(-short * rate), short * turn
        re, im = mag * jnp.cos(phase), mag * jnp.sin(phase)
        step_ref[n : n + 1, :] = re[0:1]
        step_ref[2 + n : 3 + n, :] = im[0:1]
        join_ref[n : n + 1, :] = re[1:2]
        join_ref[2 + n : 3 + n, :] = im[1:2]
        poles_ref[n : n + 1, :] = residue_ref[0, n : n + 1, :]
        poles_ref[2 + n : 3 + n, :] = residue_ref[1, n : n + 1, :]


def fetch(w_ref, w, sems, starts, sizes):
    copies = []
    for j, (start, size) in enumerate(zip(starts, sizes)):
        at = sum(sizes[:j])
        copies.append(
            pltpu.make_async_copy(w_ref.at[:, pl.ds(start, size)], w.at[:, pl.ds(at, size)], sems.at[j])
        )
        copies[-1].start()
    return copies


def product(lhs_ref, w, copies, chans, keep_ref, send_ref):
    sides, rows, depth = lhs_ref.shape
    both = lhs_ref[...].reshape(sides * rows, depth)
    for j, copy in enumerate(copies):
        copy.wait()
        cols = slice(j * chans, (j + 1) * chans)
        part = jnp.dot(both, w[:, cols], preferred_element_type=jnp.float32)
        keep_ref[:, cols] = part[:rows]
        send_ref[:, cols] = part[rows:].astype(send_ref.dtype)


def mixin_project_kernel(count, place_ref, *refs):
    x_refs, (w_ref, keep_ref, send_ref, lhs_ref, w, sems) = refs[:count], refs[count:]
    chans = x_refs[0].shape[1]
    copies = fetch(w_ref, w, sems, (chans, 2 * chans), (chans, chans))
    half, here, sign = place_ref[0], place_ref[1], place_ref[2]
    for x_ref, hop in zip(x_refs, ring_hops(count)):
        origin = lax.rem(here + sign * hop + count, count)
        side = jnp.where(lax.rem(origin, 2) == half, 0, 1)
        at = pl.multiple_of(lax.div(origin, 2) * chans, chans)
        lhs_ref[side, :, pl.ds(at, chans)] = x_ref[...]
    product(lhs_ref, w, copies, chans, keep_ref, send_ref)


def query_project_kernel(lhs_ref, w_ref, keep_ref, send_ref, w, sems):
    chans = keep_ref.shape[1]
    copies = fetch(w_ref, w, sems, (0,), (chans,))
    product(lhs_ref, w, copies, chans, keep_ref, send_ref)


def beside_kernel(x_ref, y_ref, out_ref, sem):
    cols = x_ref.shape[1]
    copy = pltpu.make_async_copy(x_ref, out_ref.at[:, pl.ds(0, cols)], sem)
    copy.start()
    out_ref[:, cols:] = y_ref[...]
    copy.wait()


def short_conv(rows, branch, total, taps_ref):
    now = total[:rows]
    past = total[rows : rows + 8]
    one = jnp.concatenate([past[1:2], now[:-1]], axis=0)
    two = jnp.concatenate([past[0:2], now[:-2]], axis=0)
    tap = [taps_ref[j, branch : branch + 1, :] for j in range(3)]
    return tap[0] * now + tap[1] * one + tap[2] * two


def scan_kernel(
    rows,
    chans,
    keep_ref,
    more_ref,
    query_ref,
    taps_ref,
    step_ref,
    join_ref,
    mixin_ref,
    begin_ref,
    final_ref,
    send_ref,
):
    send_ref[...] = query_ref[...]
    length = rows // SUB

    def filtered(branch):
        cols = slice((branch - 1) * chans, branch * chans)
        total = keep_ref[:, cols] + more_ref[:, cols].astype(jnp.float32)
        return short_conv(rows, branch, total, taps_ref)

    mixin = filtered(1) * filtered(2)
    for q in range(chans // LANES):
        mixin_ref[q] = mixin[:, q * LANES : (q + 1) * LANES]
    for q in range(chans // LANES):
        cols = slice(q * LANES, (q + 1) * LANES)
        wide = lambda row: jnp.broadcast_to(row, (SUB, LANES))
        ar = [wide(step_ref[n : n + 1, cols]) for n in range(2)]
        ai = [wide(step_ref[2 + n : 3 + n, cols]) for n in range(2)]
        re = [jnp.zeros((SUB, LANES), jnp.float32)] * 2
        im = [jnp.zeros((SUB, LANES), jnp.float32)] * 2
        for i in range(length):
            u = mixin_ref[q, pl.ds(i, SUB, stride=length), :]
            for n in range(2):
                re[n], im[n] = ar[n] * re[n] - ai[n] * im[n] + u, ar[n] * im[n] + ai[n] * re[n]
        for n in range(2):
            jr = join_ref[n : n + 1, cols]
            ji = join_ref[2 + n : 3 + n, cols]
            er = jnp.zeros((1, LANES), jnp.float32)
            ei = jnp.zeros((1, LANES), jnp.float32)
            for b in range(SUB):
                begin_ref[n, b : b + 1, cols] = er
                begin_ref[2 + n, b : b + 1, cols] = ei
                er, ei = (
                    jr * er - ji * ei + re[n][b : b + 1],
                    jr * ei + ji * er + im[n][b : b + 1],
                )
            final_ref[n : n + 1, cols] = er
            final_ref[2 + n : 3 + n, cols] = ei


def gate_kernel(
    rows, chans, all_ref, jump_ref, begin_ref, reach_ref, step_ref, residue_ref, bias_ref, mixin_ref, keep_ref, more_ref, taps_ref, out_ref, long
):
    query = short_conv(rows, 0, keep_ref[...] + more_ref[...].astype(jnp.float32), taps_ref)
    length = rows // SUB
    entry = []
    for n in range(2):
        fr, fi = all_ref[:, n, :], all_ref[:, 2 + n, :]
        cr, ci = jump_ref[n], jump_ref[2 + n]
        gr = jnp.sum(cr * fr - ci * fi, axis=0, keepdims=True)
        gi = jnp.sum(cr * fi + ci * fr, axis=0, keepdims=True)
        rr, ri = reach_ref[n], reach_ref[2 + n]
        entry.append((begin_ref[n] + rr * gr - ri * gi, begin_ref[2 + n] + rr * gi + ri * gr))
    for q in range(chans // LANES):
        cols = slice(q * LANES, (q + 1) * LANES)
        wide = lambda row: jnp.broadcast_to(row, (SUB, LANES))
        ar = [wide(step_ref[n : n + 1, cols]) for n in range(2)]
        ai = [wide(step_ref[2 + n : 3 + n, cols]) for n in range(2)]
        pr = [wide(residue_ref[n : n + 1, cols]) for n in range(2)]
        pi = [wide(residue_ref[2 + n : 3 + n, cols]) for n in range(2)]
        direct = wide(bias_ref[:, cols])
        re = [entry[n][0][:, cols] for n in range(2)]
        im = [entry[n][1][:, cols] for n in range(2)]
        for i in range(length):
            u = mixin_ref[q, pl.ds(i, SUB, stride=length), :]
            y = direct * u
            for n in range(2):
                re[n], im[n] = ar[n] * re[n] - ai[n] * im[n] + u, ar[n] * im[n] + ai[n] * re[n]
                y = y + (pr[n] * re[n] - pi[n] * im[n])
            long[q, pl.ds(i, SUB, stride=length), :] = y
        out_ref[:, cols] = (query[:, cols] * long[q]).astype(out_ref.dtype)


def mix_kernel(count, which_ref, *refs):
    x_refs, (w_ref, out_ref, rest_ref, w, sems) = refs[: count - 1], refs[count - 1 :]
    chans = x_refs[0].shape[1]
    part = chans // 2
    copies = []
    for j in range(count):
        block = which_ref[j]
        other = jnp.where(lax.rem(block, 2) == which_ref[count], 0, 1)
        col = pl.multiple_of(other * chans, chans)
        pair = []
        for e in range(2):
            row = pl.multiple_of(lax.div(block, 2) * chans + jnp.where(other == e, 0, part), part)
            dst = rest_ref if j == count - 1 else w.at[j]
            pair.append(
                pltpu.make_async_copy(
                    w_ref.at[pl.ds(row, part), pl.ds(col, out_ref.shape[1])],
                    dst.at[pl.ds(e * part, part)],
                    sems.at[j, e],
                )
            )
            pair[-1].start()
        copies.append(pair)
    total = jnp.zeros(out_ref.shape, jnp.float32)
    for j in range(count):
        for copy in copies[j]:
            copy.wait()
        if j < count - 1:
            total = total + jnp.dot(x_refs[j][...], w[j], preferred_element_type=jnp.float32)
    out_ref[...] = total


def last_mix_kernel(x_ref, w_ref, base_ref, out_ref):
    total = base_ref[...] + jnp.dot(x_ref[...], w_ref[...], preferred_element_type=jnp.float32)
    out_ref[...] = total.astype(out_ref.dtype)


IN_VMEM = pl.BlockSpec(memory_space=pltpu.VMEM)
IN_SMEM = pl.BlockSpec(memory_space=pltpu.SMEM)
IN_HBM = pl.BlockSpec(memory_space=pltpu.HBM)
in_hbm = functools.partial(pltpu.with_memory_space_constraint, memory_space=pltpu.HBM)


def mix(blocks, which, weight, cols):
    rows, chans = blocks[0].shape
    count = len(blocks) + 1
    return pl.pallas_call(
        functools.partial(mix_kernel, count),
        in_specs=[IN_SMEM] + [IN_VMEM] * (count - 1) + [IN_HBM],
        out_shape=[
            jax.ShapeDtypeStruct((rows, cols), jnp.float32),
            jax.ShapeDtypeStruct((chans, cols), weight.dtype),
        ],
        scratch_shapes=[
            pltpu.VMEM((count - 1, chans, cols), weight.dtype),
            pltpu.SemaphoreType.DMA((count, 2)),
        ],
        compiler_params=pltpu.CompilerParams(vmem_limit_bytes=VMEM),
        cost_estimate=pl.CostEstimate(
            flops=2 * count * rows * chans * cols,
            bytes_accessed=2 * count * chans * cols,
            transcendentals=0,
        ),
        name="mix",
    )(which, *blocks, in_hbm(weight))


def body(inputs, in_weight, out_weight, short_filter, decay, angle, residue, bias):
    rows, chans = inputs.shape
    place, blocks = lax.axis_index("seq"), lax.axis_size("seq")
    count = lax.axis_size("ch")
    col_start = lax.axis_index("ch") * chans
    near = [(s % 8) // 4 for s in range(blocks)]
    mirror = [s + 6 - 4 * ((s % 8) // 2) for s in range(blocks)]
    cut = lax.dynamic_slice(in_weight, (0, 0, col_start), (in_weight.shape[0], 3, chans))
    own_weight = jnp.concatenate([cut[:, g] for g in range(3)], axis=1)
    pairs = [(s, mirror[s]) for s in range(blocks)]
    halves = [[s for s in range(blocks) if near[s] == h] for h in range(2)]
    gather = lambda x: lax.all_gather(x, "seq", axis=0, tiled=True, axis_index_groups=halves)
    weight = gather(own_weight)
    f32, b16 = jnp.float32, jnp.bfloat16
    padded, depth = rows + HALO, chans * count // 2
    params = pltpu.CompilerParams(vmem_limit_bytes=VMEM)
    shape = jax.ShapeDtypeStruct
    half = lax.rem(place, 8) // 4
    rim = lax.ppermute(inputs[-2:], "seq", [(i, i + 1) for i in range(blocks - 1)])
    mirrored = lax.ppermute(out_weight, "seq", pairs)
    rim, mirrored = lax.optimization_barrier((rim, mirrored))
    tokens = jnp.concatenate([inputs, rim, jnp.zeros((HALO - 2, chans), inputs.dtype)], axis=0)
    swaps = []
    for c in range(count):
        for s in range(blocks):
            to = (c, s) if c % 2 == near[s] else (c ^ 1, mirror[s])
            swaps.append((c * blocks + s, to[0] * blocks + to[1]))
    swapped = lax.ppermute(tokens, ("ch", "seq"), swaps)
    step, join, reach, jump, poles = pl.pallas_call(
        functools.partial(powers_kernel, rows),
        in_specs=[IN_SMEM] + [IN_VMEM] * 3,
        out_shape=[
            shape((4, chans), f32),
            shape((4, chans), f32),
            shape((4, SUB, chans), f32),
            shape((4, blocks, chans), f32),
            shape((4, chans), f32),
        ],
        compiler_params=params,
        name="powers",
    )(place.reshape(1).astype(jnp.int32), decay.T, angle.T, residue.transpose(0, 2, 1))
    both = pl.pallas_call(
        beside_kernel,
        in_specs=[IN_HBM, IN_VMEM],
        out_shape=shape((out_weight.shape[0], 2 * out_weight.shape[1]), b16),
        scratch_shapes=[pltpu.SemaphoreType.DMA(())],
        compiler_params=params,
        name="beside",
    )(in_hbm(out_weight), mirrored)
    tied = lax.optimization_barrier((swapped, both, step, join, reach, jump, poles))
    swapped, both, step, join, reach, jump, poles = tied
    second = gather(both)
    features = ring(swapped)
    here = lax.axis_index("ch")
    sign = 1 - 2 * lax.rem(place, 2)

    keep, send, lhs = pl.pallas_call(
        functools.partial(mixin_project_kernel, count),
        in_specs=[IN_SMEM] + [IN_VMEM] * count + [IN_HBM],
        out_shape=[
            pltpu.VMEM((padded, 2 * chans), f32),
            pltpu.VMEM((padded, 2 * chans), b16),
            shape((2, padded, depth), b16),
        ],
        scratch_shapes=[pltpu.VMEM((depth, 2 * chans), b16), pltpu.SemaphoreType.DMA((2,))],
        compiler_params=params,
        cost_estimate=pl.CostEstimate(
            flops=8 * padded * depth * chans, bytes_accessed=4 * depth * chans, transcendentals=0
        ),
        name="project_mixin",
    )(jnp.stack([half, here, sign]).astype(jnp.int32), *features, in_hbm(weight))
    more = lax.ppermute(send, "seq", pairs)
    query_keep, query_send = pl.pallas_call(
        query_project_kernel,
        in_specs=[IN_VMEM, IN_HBM],
        out_shape=[shape((padded, chans), f32), shape((padded, chans), b16)],
        scratch_shapes=[pltpu.VMEM((depth, chans), b16), pltpu.SemaphoreType.DMA((1,))],
        compiler_params=params,
        cost_estimate=pl.CostEstimate(
            flops=4 * padded * depth * chans, bytes_accessed=2 * depth * chans, transcendentals=0
        ),
        name="project_query",
    )(lhs, in_hbm(weight))
    taps = short_filter
    mixin, begin, final, query_send = pl.pallas_call(
        functools.partial(scan_kernel, rows, chans),
        out_shape=[
            shape((chans // LANES, rows, LANES), f32),
            shape((4, SUB, chans), f32),
            shape((4, chans), f32),
            shape((padded, chans), b16),
        ],
        compiler_params=params,
        name="scan",
    )(keep, more, query_send, taps, step, join)
    query_more = lax.ppermute(query_send, "seq", pairs)

    states = spread(final, "seq")
    gated = pl.pallas_call(
        functools.partial(gate_kernel, rows, chans),
        out_shape=shape((rows, chans), b16),
        scratch_shapes=[pltpu.VMEM((chans // LANES, rows, LANES), f32)],
        compiler_params=params,
        name="gate",
    )(states, jump, begin, reach, step, poles, bias[None, :], mixin, query_keep, query_more, taps)

    which = jnp.stack([lax.rem(here + sign * hop + count, count) for hop in ring_hops(count)] + [half])
    parts = ring(gated)
    first, rest = mix(parts[:-1], which.astype(jnp.int32), second, out_weight.shape[1])
    return pl.pallas_call(
        last_mix_kernel,
        out_shape=shape(first.shape, b16),
        compiler_params=params,
        name="last_mix",
    )(parts[-1], rest, first)


def solution(mesh):
    placed = (
        P("seq", "ch"),
        P("seq", None, None),
        P("seq", "ch"),
        P(None, None, "ch"),
        P("ch", None),
        P("ch", None),
        P(None, "ch", None),
        P("ch"),
    )
    return jax.shard_map(
        body, mesh=mesh, in_specs=placed, out_specs=P("seq", "ch"), check_vma=False
    )
```

```python
import functools

import jax
import jax.numpy as jnp
from jax import lax
from jax.experimental import pallas as pl
from jax.experimental.pallas import tpu as pltpu
from jax.sharding import PartitionSpec as P

HALO = 16
LANES = 128
SUB = 8
VMEM = 24 * 1024 * 1024


def spread(x, axis):
    count = lax.axis_size(axis)
    return lax.all_to_all(
        jnp.broadcast_to(x[None], (count,) + x.shape), axis, 0, 0, tiled=True
    )


def ring_hops(count):
    hops = [0]
    for hop in range(1, count // 2 + 1):
        hops += [-hop, hop] if 2 * hop < count else [-hop]
    return hops


def ring(x, axis):
    count = lax.axis_size(axis)
    up = [(c, (c + 1) % count) for c in range(count)]
    down = [(c, (c - 1) % count) for c in range(count)]
    arrived = [x]
    below = above = x
    for hop in range(1, count // 2 + 1):
        below = lax.ppermute(below, axis, up)
        arrived.append(below)
        if 2 * hop < count:
            above = lax.ppermute(above, axis, down)
            arrived.append(above)
    return arrived


def powers_kernel(rows, place_ref, rate_ref, turn_ref, residue_ref, step_ref, join_ref, reach_ref, jump_ref, poles_ref):
    chans = rate_ref.shape[1]
    length = rows // SUB
    blocks = jump_ref.shape[1]
    gap = place_ref[0] - 1 - lax.broadcasted_iota(jnp.int32, (blocks, chans), 0)
    far = (jnp.maximum(gap, 0) * rows).astype(jnp.float32)
    near = (lax.broadcasted_iota(jnp.int32, (SUB, chans), 0) * length).astype(jnp.float32)
    short = jnp.where(lax.broadcasted_iota(jnp.int32, (SUB, chans), 0) == 0, 1.0, float(length))
    for n in range(2):
        rate, turn = rate_ref[n : n + 1, :], turn_ref[n : n + 1, :]
        mag, phase = jnp.exp(-far * rate), far * turn
        jump_ref[n] = jnp.where(gap >= 0, mag * jnp.cos(phase), 0.0)
        jump_ref[2 + n] = jnp.where(gap >= 0, mag * jnp.sin(phase), 0.0)
        mag, phase = jnp.exp(-near * rate), near * turn
        reach_ref[n] = mag * jnp.cos(phase)
        reach_ref[2 + n] = mag * jnp.sin(phase)
        mag, phase = jnp.exp(-short * rate), short * turn
        re, im = mag * jnp.cos(phase), mag * jnp.sin(phase)
        step_ref[n : n + 1, :] = re[0:1]
        step_ref[2 + n : 3 + n, :] = im[0:1]
        join_ref[n : n + 1, :] = re[1:2]
        join_ref[2 + n : 3 + n, :] = im[1:2]
        poles_ref[n : n + 1, :] = residue_ref[0, n : n + 1, :]
        poles_ref[2 + n : 3 + n, :] = residue_ref[1, n : n + 1, :]


def fetch(w_ref, w, sems, branches):
    copies = []
    for j, branch in enumerate(branches):
        chans = w_ref.shape[2]
        copies.append(
            pltpu.make_async_copy(w_ref.at[branch], w.at[:, pl.ds(j * chans, chans)], sems.at[j])
        )
        copies[-1].start()
    return copies


def product(lhs_ref, w, copies, chans, keep_ref, send_ref):
    sides, rows, depth = lhs_ref.shape
    both = lhs_ref[...].reshape(sides * rows, depth)
    for j, copy in enumerate(copies):
        copy.wait()
        cols = slice(j * chans, (j + 1) * chans)
        part = jnp.dot(both, w[:, cols], preferred_element_type=jnp.float32)
        keep_ref[:, cols] = part[:rows]
        send_ref[:, cols] = part[rows:].astype(send_ref.dtype)


def mixin_project_kernel(count, place_ref, *refs):
    x_refs, (w_ref, keep_ref, send_ref, lhs_ref, w, sems) = refs[:count], refs[count:]
    chans = x_refs[0].shape[1]
    copies = fetch(w_ref, w, sems, (1, 2))
    half, here = place_ref[0], place_ref[1]
    for x_ref, hop in zip(x_refs, ring_hops(count)):
        origin = lax.rem(here + hop + count, count)
        side = jnp.where(lax.rem(origin, 2) == half, 0, 1)
        at = pl.multiple_of(lax.div(origin, 2) * chans, chans)
        lhs_ref[side, :, pl.ds(at, chans)] = x_ref[...]
    product(lhs_ref, w, copies, chans, keep_ref, send_ref)


def query_project_kernel(lhs_ref, w_ref, keep_ref, send_ref, w, sems):
    chans = keep_ref.shape[1]
    copies = fetch(w_ref, w, sems, (0,))
    product(lhs_ref, w, copies, chans, keep_ref, send_ref)


def cut_kernel(place_ref, w_ref, out_ref, sem):
    cols = out_ref.shape[2]
    at = pl.multiple_of(place_ref[0] * cols, cols)
    copy = pltpu.make_async_copy(w_ref.at[:, :, pl.ds(at, cols)], out_ref, sem)
    copy.start()
    copy.wait()


def beside_kernel(x_ref, y_ref, out_ref, sem):
    cols = x_ref.shape[1]
    copy = pltpu.make_async_copy(x_ref, out_ref.at[:, pl.ds(0, cols)], sem)
    copy.start()
    out_ref[:, cols:] = y_ref[...]
    copy.wait()


def short_conv(rows, branch, total, taps_ref):
    now = total[:rows]
    past = total[rows : rows + 8]
    one = jnp.concatenate([past[1:2], now[:-1]], axis=0)
    two = jnp.concatenate([past[0:2], now[:-2]], axis=0)
    tap = [taps_ref[j, branch : branch + 1, :] for j in range(3)]
    return tap[0] * now + tap[1] * one + tap[2] * two


def scan_kernel(
    rows,
    chans,
    keep_ref,
    more_ref,
    query_ref,
    taps_ref,
    step_ref,
    join_ref,
    mixin_ref,
    begin_ref,
    final_ref,
    send_ref,
):
    send_ref[...] = query_ref[...]
    length = rows // SUB

    def filtered(branch):
        cols = slice((branch - 1) * chans, branch * chans)
        total = keep_ref[:, cols] + more_ref[:, cols].astype(jnp.float32)
        return short_conv(rows, branch, total, taps_ref)

    mixin = filtered(1) * filtered(2)
    for q in range(chans // LANES):
        mixin_ref[q] = mixin[:, q * LANES : (q + 1) * LANES]
    for q in range(chans // LANES):
        cols = slice(q * LANES, (q + 1) * LANES)
        wide = lambda row: jnp.broadcast_to(row, (SUB, LANES))
        ar = [wide(step_ref[n : n + 1, cols]) for n in range(2)]
        ai = [wide(step_ref[2 + n : 3 + n, cols]) for n in range(2)]
        re = [jnp.zeros((SUB, LANES), jnp.float32)] * 2
        im = [jnp.zeros((SUB, LANES), jnp.float32)] * 2
        for i in range(length):
            u = mixin_ref[q, pl.ds(i, SUB, stride=length), :]
            for n in range(2):
                re[n], im[n] = ar[n] * re[n] - ai[n] * im[n] + u, ar[n] * im[n] + ai[n] * re[n]
        for n in range(2):
            jr = join_ref[n : n + 1, cols]
            ji = join_ref[2 + n : 3 + n, cols]
            er = jnp.zeros((1, LANES), jnp.float32)
            ei = jnp.zeros((1, LANES), jnp.float32)
            for b in range(SUB):
                begin_ref[n, b : b + 1, cols] = er
                begin_ref[2 + n, b : b + 1, cols] = ei
                er, ei = (
                    jr * er - ji * ei + re[n][b : b + 1],
                    jr * ei + ji * er + im[n][b : b + 1],
                )
            final_ref[n : n + 1, cols] = er
            final_ref[2 + n : 3 + n, cols] = ei


def gate_kernel(
    rows, chans, all_ref, jump_ref, begin_ref, reach_ref, step_ref, residue_ref, bias_ref, mixin_ref, keep_ref, more_ref, taps_ref, out_ref, long
):
    query = short_conv(rows, 0, keep_ref[...] + more_ref[...].astype(jnp.float32), taps_ref)
    length = rows // SUB
    entry = []
    for n in range(2):
        fr, fi = all_ref[:, n, :], all_ref[:, 2 + n, :]
        cr, ci = jump_ref[n], jump_ref[2 + n]
        gr = jnp.sum(cr * fr - ci * fi, axis=0, keepdims=True)
        gi = jnp.sum(cr * fi + ci * fr, axis=0, keepdims=True)
        rr, ri = reach_ref[n], reach_ref[2 + n]
        entry.append((begin_ref[n] + rr * gr - ri * gi, begin_ref[2 + n] + rr * gi + ri * gr))
    for q in range(chans // LANES):
        cols = slice(q * LANES, (q + 1) * LANES)
        wide = lambda row: jnp.broadcast_to(row, (SUB, LANES))
        ar = [wide(step_ref[n : n + 1, cols]) for n in range(2)]
        ai = [wide(step_ref[2 + n : 3 + n, cols]) for n in range(2)]
        pr = [wide(residue_ref[n : n + 1, cols]) for n in range(2)]
        pi = [wide(residue_ref[2 + n : 3 + n, cols]) for n in range(2)]
        direct = wide(bias_ref[:, cols])
        re = [entry[n][0][:, cols] for n in range(2)]
        im = [entry[n][1][:, cols] for n in range(2)]
        for i in range(length):
            u = mixin_ref[q, pl.ds(i, SUB, stride=length), :]
            y = direct * u
            for n in range(2):
                re[n], im[n] = ar[n] * re[n] - ai[n] * im[n] + u, ar[n] * im[n] + ai[n] * re[n]
                y = y + (pr[n] * re[n] - pi[n] * im[n])
            long[q, pl.ds(i, SUB, stride=length), :] = y
        out_ref[:, cols] = (query[:, cols] * long[q]).astype(out_ref.dtype)


def mix_kernel(count, which_ref, *refs):
    x_refs, (w_ref, out_ref, rest_ref, w, sems) = refs[: count - 1], refs[count - 1 :]
    chans = x_refs[0].shape[1]
    part = chans // 2
    copies = []
    for j in range(count):
        block = which_ref[j]
        other = jnp.where(lax.rem(block, 2) == which_ref[count], 0, 1)
        col = pl.multiple_of(other * chans, chans)
        pair = []
        for e in range(2):
            row = pl.multiple_of(lax.div(block, 2) * chans + jnp.where(other == e, 0, part), part)
            dst = rest_ref if j == count - 1 else w.at[j]
            pair.append(
                pltpu.make_async_copy(
                    w_ref.at[pl.ds(row, part), pl.ds(col, out_ref.shape[1])],
                    dst.at[pl.ds(e * part, part)],
                    sems.at[j, e],
                )
            )
            pair[-1].start()
        copies.append(pair)
    total = jnp.zeros(out_ref.shape, jnp.float32)
    for j in range(count):
        for copy in copies[j]:
            copy.wait()
        if j < count - 1:
            total = total + jnp.dot(x_refs[j][...], w[j], preferred_element_type=jnp.float32)
    out_ref[...] = total


def last_mix_kernel(x_ref, w_ref, base_ref, out_ref):
    total = base_ref[...] + jnp.dot(x_ref[...], w_ref[...], preferred_element_type=jnp.float32)
    out_ref[...] = total.astype(out_ref.dtype)


IN_VMEM = pl.BlockSpec(memory_space=pltpu.VMEM)
IN_SMEM = pl.BlockSpec(memory_space=pltpu.SMEM)
IN_HBM = pl.BlockSpec(memory_space=pltpu.HBM)
in_hbm = functools.partial(pltpu.with_memory_space_constraint, memory_space=pltpu.HBM)


def mix(blocks, which, weight, cols):
    rows, chans = blocks[0].shape
    count = len(blocks) + 1
    return pl.pallas_call(
        functools.partial(mix_kernel, count),
        in_specs=[IN_SMEM] + [IN_VMEM] * (count - 1) + [IN_HBM],
        out_shape=[
            jax.ShapeDtypeStruct((rows, cols), jnp.float32),
            jax.ShapeDtypeStruct((chans, cols), weight.dtype),
        ],
        scratch_shapes=[
            pltpu.VMEM((count - 1, chans, cols), weight.dtype),
            pltpu.SemaphoreType.DMA((count, 2)),
        ],
        compiler_params=pltpu.CompilerParams(vmem_limit_bytes=VMEM),
        cost_estimate=pl.CostEstimate(
            flops=2 * count * rows * chans * cols,
            bytes_accessed=2 * count * chans * cols,
            transcendentals=0,
        ),
        name="mix",
    )(which, *blocks, in_hbm(weight))


def body(inputs, in_weight, out_weight, short_filter, decay, angle, residue, bias):
    rows, chans = inputs.shape
    place, blocks = lax.axis_index("seq"), lax.axis_size("seq")
    count = lax.axis_size("ch")
    near = [(s % 8) // 4 for s in range(blocks)]
    mirror = [s + 6 - 4 * ((s % 8) // 2) for s in range(blocks)]
    cut = pl.pallas_call(
        cut_kernel,
        in_specs=[IN_SMEM, IN_HBM],
        out_shape=jax.ShapeDtypeStruct((3, in_weight.shape[0], chans), jnp.bfloat16),
        scratch_shapes=[pltpu.SemaphoreType.DMA(())],
        compiler_params=pltpu.CompilerParams(vmem_limit_bytes=VMEM),
        name="cut",
    )(lax.axis_index("ch").reshape(1).astype(jnp.int32), in_hbm(in_weight.transpose(1, 0, 2)))
    pairs = [(s, mirror[s]) for s in range(blocks)]
    halves = [[s for s in range(blocks) if near[s] == h] for h in range(2)]
    gather = lambda x, axis: lax.all_gather(x, "seq", axis=axis, tiled=True, axis_index_groups=halves)
    weight = gather(cut, 1)
    f32, b16 = jnp.float32, jnp.bfloat16
    padded, depth = rows + HALO, chans * count // 2
    params = pltpu.CompilerParams(vmem_limit_bytes=VMEM)
    shape = jax.ShapeDtypeStruct
    half = lax.rem(place, 8) // 4
    rim = lax.ppermute(inputs[-2:], "seq", [(i, i + 1) for i in range(blocks - 1)])
    mirrored = lax.ppermute(out_weight, "seq", pairs)
    rim, mirrored = lax.optimization_barrier((rim, mirrored))
    tokens = jnp.concatenate([inputs, rim, jnp.zeros((HALO - 2, chans), inputs.dtype)], axis=0)
    swaps = []
    for c in range(count):
        for s in range(blocks):
            to = (c, s) if c % 2 == near[s] else (c ^ 1, mirror[s])
            swaps.append((c * blocks + s, to[0] * blocks + to[1]))
    swapped = lax.ppermute(tokens, ("ch", "seq"), swaps)
    step, join, reach, jump, poles = pl.pallas_call(
        functools.partial(powers_kernel, rows),
        in_specs=[IN_SMEM] + [IN_VMEM] * 3,
        out_shape=[
            shape((4, chans), f32),
            shape((4, chans), f32),
            shape((4, SUB, chans), f32),
            shape((4, blocks, chans), f32),
            shape((4, chans), f32),
        ],
        compiler_params=params,
        name="powers",
    )(place.reshape(1).astype(jnp.int32), decay.T, angle.T, residue.transpose(0, 2, 1))
    both = pl.pallas_call(
        beside_kernel,
        in_specs=[IN_HBM, IN_VMEM],
        out_shape=shape((out_weight.shape[0], 2 * out_weight.shape[1]), b16),
        scratch_shapes=[pltpu.SemaphoreType.DMA(())],
        compiler_params=params,
        name="beside",
    )(in_hbm(out_weight), mirrored)
    tied = lax.optimization_barrier((swapped, both, step, join, reach, jump, poles))
    swapped, both, step, join, reach, jump, poles = tied
    second = gather(both, 0)
    features = ring(swapped, "ch")
    here = lax.axis_index("ch")

    keep, send, lhs = pl.pallas_call(
        functools.partial(mixin_project_kernel, count),
        in_specs=[IN_SMEM] + [IN_VMEM] * count + [IN_HBM],
        out_shape=[
            pltpu.VMEM((padded, 2 * chans), f32),
            pltpu.VMEM((padded, 2 * chans), b16),
            shape((2, padded, depth), b16),
        ],
        scratch_shapes=[pltpu.VMEM((depth, 2 * chans), b16), pltpu.SemaphoreType.DMA((2,))],
        compiler_params=params,
        cost_estimate=pl.CostEstimate(
            flops=8 * padded * depth * chans, bytes_accessed=4 * depth * chans, transcendentals=0
        ),
        name="project_mixin",
    )(jnp.stack([half, here]).astype(jnp.int32), *features, in_hbm(weight))
    more = lax.ppermute(send, "seq", pairs)
    query_keep, query_send = pl.pallas_call(
        query_project_kernel,
        in_specs=[IN_VMEM, IN_HBM],
        out_shape=[shape((padded, chans), f32), shape((padded, chans), b16)],
        scratch_shapes=[pltpu.VMEM((depth, chans), b16), pltpu.SemaphoreType.DMA((1,))],
        compiler_params=params,
        cost_estimate=pl.CostEstimate(
            flops=4 * padded * depth * chans, bytes_accessed=2 * depth * chans, transcendentals=0
        ),
        name="project_query",
    )(lhs, in_hbm(weight))
    taps = short_filter
    mixin, begin, final, query_send = pl.pallas_call(
        functools.partial(scan_kernel, rows, chans),
        out_shape=[
            shape((chans // LANES, rows, LANES), f32),
            shape((4, SUB, chans), f32),
            shape((4, chans), f32),
            shape((padded, chans), b16),
        ],
        compiler_params=params,
        name="scan",
    )(keep, more, query_send, taps, step, join)
    query_more = lax.ppermute(query_send, "seq", pairs)

    states = spread(final, "seq")
    gated = pl.pallas_call(
        functools.partial(gate_kernel, rows, chans),
        out_shape=shape((rows, chans), b16),
        scratch_shapes=[pltpu.VMEM((chans // LANES, rows, LANES), f32)],
        compiler_params=params,
        name="gate",
    )(states, jump, begin, reach, step, poles, bias[None, :], mixin, query_keep, query_more, taps)

    which = jnp.stack([lax.rem(here + hop + count, count) for hop in ring_hops(count)] + [half])
    parts = ring(gated, "ch")
    first, rest = mix(parts[:-1], which.astype(jnp.int32), second, out_weight.shape[1])
    return pl.pallas_call(
        last_mix_kernel,
        out_shape=shape(first.shape, b16),
        compiler_params=params,
        name="last_mix",
    )(parts[-1], rest, first)


def solution(mesh):
    placed = (
        P("seq", "ch"),
        P("seq", None, None),
        P("seq", "ch"),
        P(None, None, "ch"),
        P("ch", None),
        P("ch", None),
        P(None, "ch", None),
        P("ch"),
    )
    return jax.shard_map(
        body, mesh=mesh, in_specs=placed, out_specs=P("seq", "ch"), check_vma=False
    )
```

```python
import functools

import jax
import jax.numpy as jnp
from jax import lax
from jax.experimental import pallas as pl
from jax.experimental.pallas import tpu as pltpu
from jax.sharding import PartitionSpec as P

HALO = 16
LANES = 128
SUB = 8
VMEM = 24 * 1024 * 1024


def spread(x, axis):
    count = lax.axis_size(axis)
    return lax.all_to_all(
        jnp.broadcast_to(x[None], (count,) + x.shape), axis, 0, 0, tiled=True
    )


def ring_hops(count):
    hops = [0]
    for hop in range(1, count // 2 + 1):
        hops += [-hop, hop] if 2 * hop < count else [-hop]
    return hops


def ring(x, axis, tied=()):
    tied = list(tied)
    count = lax.axis_size(axis)
    up = [(c, (c + 1) % count) for c in range(count)]
    down = [(c, (c - 1) % count) for c in range(count)]
    arrived = [x]
    below = above = x
    for hop in range(1, count // 2 + 1):
        below = lax.ppermute(below, axis, up)
        arrived.append(below)
        if 2 * hop < count:
            above = lax.ppermute(above, axis, down)
            arrived.append(above)
        if hop <= len(tied):
            below, tied[hop - 1] = lax.optimization_barrier((below, tied[hop - 1]))
            arrived[2 * hop - 1] = below
    return arrived, tied


def powers_kernel(rows, place_ref, rate_ref, turn_ref, residue_ref, step_ref, join_ref, reach_ref, jump_ref, poles_ref):
    chans = rate_ref.shape[1]
    length = rows // SUB
    blocks = jump_ref.shape[1]
    gap = place_ref[0] - 1 - lax.broadcasted_iota(jnp.int32, (blocks, chans), 0)
    far = (jnp.maximum(gap, 0) * rows).astype(jnp.float32)
    near = (lax.broadcasted_iota(jnp.int32, (SUB, chans), 0) * length).astype(jnp.float32)
    short = jnp.where(lax.broadcasted_iota(jnp.int32, (SUB, chans), 0) == 0, 1.0, float(length))
    for n in range(2):
        rate, turn = rate_ref[n : n + 1, :], turn_ref[n : n + 1, :]
        mag, phase = jnp.exp(-far * rate), far * turn
        jump_ref[n] = jnp.where(gap >= 0, mag * jnp.cos(phase), 0.0)
        jump_ref[2 + n] = jnp.where(gap >= 0, mag * jnp.sin(phase), 0.0)
        mag, phase = jnp.exp(-near * rate), near * turn
        reach_ref[n] = mag * jnp.cos(phase)
        reach_ref[2 + n] = mag * jnp.sin(phase)
        mag, phase = jnp.exp(-short * rate), short * turn
        re, im = mag * jnp.cos(phase), mag * jnp.sin(phase)
        step_ref[n : n + 1, :] = re[0:1]
        step_ref[2 + n : 3 + n, :] = im[0:1]
        join_ref[n : n + 1, :] = re[1:2]
        join_ref[2 + n : 3 + n, :] = im[1:2]
        poles_ref[n : n + 1, :] = residue_ref[0, n : n + 1, :]
        poles_ref[2 + n : 3 + n, :] = residue_ref[1, n : n + 1, :]


def fetch(w_ref, w, sems, branches):
    copies = []
    for j, branch in enumerate(branches):
        chans = w_ref.shape[2]
        copies.append(
            pltpu.make_async_copy(w_ref.at[branch], w.at[:, pl.ds(j * chans, chans)], sems.at[j])
        )
        copies[-1].start()
    return copies


def product(lhs_ref, w, copies, chans, keep_ref, send_ref):
    sides, rows, depth = lhs_ref.shape
    both = lhs_ref[...].reshape(sides * rows, depth)
    for j, copy in enumerate(copies):
        copy.wait()
        cols = slice(j * chans, (j + 1) * chans)
        part = jnp.dot(both, w[:, cols], preferred_element_type=jnp.float32)
        keep_ref[:, cols] = part[:rows]
        send_ref[:, cols] = part[rows:].astype(send_ref.dtype)


def mixin_project_kernel(count, place_ref, *refs):
    x_refs, (w_ref, keep_ref, send_ref, lhs_ref, w, sems) = refs[:count], refs[count:]
    chans = x_refs[0].shape[1]
    copies = fetch(w_ref, w, sems, (1, 2))
    half, here = place_ref[0], place_ref[1]
    for x_ref, hop in zip(x_refs, ring_hops(count)):
        origin = lax.rem(here + hop + count, count)
        side = jnp.where(lax.rem(origin, 2) == half, 0, 1)
        at = pl.multiple_of(lax.div(origin, 2) * chans, chans)
        lhs_ref[side, :, pl.ds(at, chans)] = x_ref[...]
    product(lhs_ref, w, copies, chans, keep_ref, send_ref)


def query_project_kernel(lhs_ref, w_ref, keep_ref, send_ref, w, sems):
    chans = keep_ref.shape[1]
    copies = fetch(w_ref, w, sems, (0,))
    product(lhs_ref, w, copies, chans, keep_ref, send_ref)


def cut_kernel(place_ref, w_ref, out_ref, sem):
    cols = out_ref.shape[2]
    at = pl.multiple_of(place_ref[0] * cols, cols)
    copy = pltpu.make_async_copy(w_ref.at[:, :, pl.ds(at, cols)], out_ref, sem)
    copy.start()
    copy.wait()


def beside_kernel(x_ref, y_ref, out_ref, sem):
    cols = x_ref.shape[1]
    copy = pltpu.make_async_copy(x_ref, out_ref.at[:, pl.ds(0, cols)], sem)
    copy.start()
    out_ref[:, cols:] = y_ref[...]
    copy.wait()


def short_conv(rows, branch, total, taps_ref):
    now = total[:rows]
    past = total[rows : rows + 8]
    one = jnp.concatenate([past[1:2], now[:-1]], axis=0)
    two = jnp.concatenate([past[0:2], now[:-2]], axis=0)
    tap = [taps_ref[j, branch : branch + 1, :] for j in range(3)]
    return tap[0] * now + tap[1] * one + tap[2] * two


def scan_kernel(
    rows,
    chans,
    keep_ref,
    more_ref,
    query_ref,
    taps_ref,
    step_ref,
    join_ref,
    mixin_ref,
    begin_ref,
    final_ref,
    send_ref,
):
    send_ref[...] = query_ref[...]
    length = rows // SUB

    def filtered(branch):
        cols = slice((branch - 1) * chans, branch * chans)
        total = keep_ref[:, cols] + more_ref[:, cols].astype(jnp.float32)
        return short_conv(rows, branch, total, taps_ref)

    mixin = filtered(1) * filtered(2)
    for q in range(chans // LANES):
        mixin_ref[q] = mixin[:, q * LANES : (q + 1) * LANES]
    for q in range(chans // LANES):
        cols = slice(q * LANES, (q + 1) * LANES)
        wide = lambda row: jnp.broadcast_to(row, (SUB, LANES))
        ar = [wide(step_ref[n : n + 1, cols]) for n in range(2)]
        ai = [wide(step_ref[2 + n : 3 + n, cols]) for n in range(2)]
        re = [jnp.zeros((SUB, LANES), jnp.float32)] * 2
        im = [jnp.zeros((SUB, LANES), jnp.float32)] * 2
        for i in range(length):
            u = mixin_ref[q, pl.ds(i, SUB, stride=length), :]
            for n in range(2):
                re[n], im[n] = ar[n] * re[n] - ai[n] * im[n] + u, ar[n] * im[n] + ai[n] * re[n]
        for n in range(2):
            jr = join_ref[n : n + 1, cols]
            ji = join_ref[2 + n : 3 + n, cols]
            er = jnp.zeros((1, LANES), jnp.float32)
            ei = jnp.zeros((1, LANES), jnp.float32)
            for b in range(SUB):
                begin_ref[n, b : b + 1, cols] = er
                begin_ref[2 + n, b : b + 1, cols] = ei
                er, ei = (
                    jr * er - ji * ei + re[n][b : b + 1],
                    jr * ei + ji * er + im[n][b : b + 1],
                )
            final_ref[n : n + 1, cols] = er
            final_ref[2 + n : 3 + n, cols] = ei


def gate_kernel(
    rows, chans, all_ref, jump_ref, begin_ref, reach_ref, step_ref, residue_ref, bias_ref, mixin_ref, keep_ref, more_ref, taps_ref, out_ref, long
):
    query = short_conv(rows, 0, keep_ref[...] + more_ref[...].astype(jnp.float32), taps_ref)
    length = rows // SUB
    entry = []
    for n in range(2):
        fr, fi = all_ref[:, n, :], all_ref[:, 2 + n, :]
        cr, ci = jump_ref[n], jump_ref[2 + n]
        gr = jnp.sum(cr * fr - ci * fi, axis=0, keepdims=True)
        gi = jnp.sum(cr * fi + ci * fr, axis=0, keepdims=True)
        rr, ri = reach_ref[n], reach_ref[2 + n]
        entry.append((begin_ref[n] + rr * gr - ri * gi, begin_ref[2 + n] + rr * gi + ri * gr))
    for q in range(chans // LANES):
        cols = slice(q * LANES, (q + 1) * LANES)
        wide = lambda row: jnp.broadcast_to(row, (SUB, LANES))
        ar = [wide(step_ref[n : n + 1, cols]) for n in range(2)]
        ai = [wide(step_ref[2 + n : 3 + n, cols]) for n in range(2)]
        pr = [wide(residue_ref[n : n + 1, cols]) for n in range(2)]
        pi = [wide(residue_ref[2 + n : 3 + n, cols]) for n in range(2)]
        direct = wide(bias_ref[:, cols])
        re = [entry[n][0][:, cols] for n in range(2)]
        im = [entry[n][1][:, cols] for n in range(2)]
        for i in range(length):
            u = mixin_ref[q, pl.ds(i, SUB, stride=length), :]
            y = direct * u
            for n in range(2):
                re[n], im[n] = ar[n] * re[n] - ai[n] * im[n] + u, ar[n] * im[n] + ai[n] * re[n]
                y = y + (pr[n] * re[n] - pi[n] * im[n])
            long[q, pl.ds(i, SUB, stride=length), :] = y
        out_ref[:, cols] = (query[:, cols] * long[q]).astype(out_ref.dtype)


def mix_kernel(count, which_ref, *refs):
    x_refs, (w_ref, out_ref, rest_ref, w, sems) = refs[: count - 1], refs[count - 1 :]
    chans = x_refs[0].shape[1]
    part = chans // 2
    copies = []
    for j in range(count):
        block = which_ref[j]
        other = jnp.where(lax.rem(block, 2) == which_ref[count], 0, 1)
        col = pl.multiple_of(other * chans, chans)
        pair = []
        for e in range(2):
            row = pl.multiple_of(lax.div(block, 2) * chans + jnp.where(other == e, 0, part), part)
            dst = rest_ref if j == count - 1 else w.at[j]
            pair.append(
                pltpu.make_async_copy(
                    w_ref.at[pl.ds(row, part), pl.ds(col, out_ref.shape[1])],
                    dst.at[pl.ds(e * part, part)],
                    sems.at[j, e],
                )
            )
            pair[-1].start()
        copies.append(pair)
    total = jnp.zeros(out_ref.shape, jnp.float32)
    for j in range(count):
        for copy in copies[j]:
            copy.wait()
        if j < count - 1:
            total = total + jnp.dot(x_refs[j][...], w[j], preferred_element_type=jnp.float32)
    out_ref[...] = total


def last_mix_kernel(x_ref, w_ref, base_ref, out_ref):
    total = base_ref[...] + jnp.dot(x_ref[...], w_ref[...], preferred_element_type=jnp.float32)
    out_ref[...] = total.astype(out_ref.dtype)


IN_VMEM = pl.BlockSpec(memory_space=pltpu.VMEM)
IN_SMEM = pl.BlockSpec(memory_space=pltpu.SMEM)
IN_HBM = pl.BlockSpec(memory_space=pltpu.HBM)
in_hbm = functools.partial(pltpu.with_memory_space_constraint, memory_space=pltpu.HBM)


def mix(blocks, which, weight, cols):
    rows, chans = blocks[0].shape
    count = len(blocks) + 1
    return pl.pallas_call(
        functools.partial(mix_kernel, count),
        in_specs=[IN_SMEM] + [IN_VMEM] * (count - 1) + [IN_HBM],
        out_shape=[
            jax.ShapeDtypeStruct((rows, cols), jnp.float32),
            jax.ShapeDtypeStruct((chans, cols), weight.dtype),
        ],
        scratch_shapes=[
            pltpu.VMEM((count - 1, chans, cols), weight.dtype),
            pltpu.SemaphoreType.DMA((count, 2)),
        ],
        compiler_params=pltpu.CompilerParams(vmem_limit_bytes=VMEM),
        cost_estimate=pl.CostEstimate(
            flops=2 * count * rows * chans * cols,
            bytes_accessed=2 * count * chans * cols,
            transcendentals=0,
        ),
        name="mix",
    )(which, *blocks, in_hbm(weight))


def body(inputs, in_weight, out_weight, short_filter, decay, angle, residue, bias):
    rows, chans = inputs.shape
    place, blocks = lax.axis_index("seq"), lax.axis_size("seq")
    count = lax.axis_size("ch")
    near = [(s % 8) // 4 for s in range(blocks)]
    mirror = [s + 6 - 4 * ((s % 8) // 2) for s in range(blocks)]
    cut = pl.pallas_call(
        cut_kernel,
        in_specs=[IN_SMEM, IN_HBM],
        out_shape=jax.ShapeDtypeStruct((3, in_weight.shape[0], chans), jnp.bfloat16),
        scratch_shapes=[pltpu.SemaphoreType.DMA(())],
        compiler_params=pltpu.CompilerParams(vmem_limit_bytes=VMEM),
        name="cut",
    )(lax.axis_index("ch").reshape(1).astype(jnp.int32), in_hbm(in_weight.transpose(1, 0, 2)))
    pairs = [(s, mirror[s]) for s in range(blocks)]
    halves = [[s for s in range(blocks) if near[s] == h] for h in range(2)]
    gather = lambda x, axis: lax.all_gather(x, "seq", axis=axis, tiled=True, axis_index_groups=halves)
    weight = gather(cut, 1)
    f32, b16 = jnp.float32, jnp.bfloat16
    padded, depth = rows + HALO, chans * count // 2
    params = pltpu.CompilerParams(vmem_limit_bytes=VMEM)
    shape = jax.ShapeDtypeStruct
    half = lax.rem(place, 8) // 4
    rim = lax.ppermute(inputs[-2:], "seq", [(i, i + 1) for i in range(blocks - 1)])
    mirrored = lax.ppermute(out_weight, "seq", pairs)
    rim, mirrored = lax.optimization_barrier((rim, mirrored))
    tokens = jnp.concatenate([inputs, rim, jnp.zeros((HALO - 2, chans), inputs.dtype)], axis=0)
    swaps = []
    for c in range(count):
        for s in range(blocks):
            to = (c, s) if c % 2 == near[s] else (c ^ 1, mirror[s])
            swaps.append((c * blocks + s, to[0] * blocks + to[1]))
    swapped = lax.ppermute(tokens, ("ch", "seq"), swaps)
    step, join, reach, jump, poles = pl.pallas_call(
        functools.partial(powers_kernel, rows),
        in_specs=[IN_SMEM] + [IN_VMEM] * 3,
        out_shape=[
            shape((4, chans), f32),
            shape((4, chans), f32),
            shape((4, SUB, chans), f32),
            shape((4, blocks, chans), f32),
            shape((4, chans), f32),
        ],
        compiler_params=params,
        name="powers",
    )(place.reshape(1).astype(jnp.int32), decay.T, angle.T, residue.transpose(0, 2, 1))
    both = pl.pallas_call(
        beside_kernel,
        in_specs=[IN_HBM, IN_VMEM],
        out_shape=shape((out_weight.shape[0], 2 * out_weight.shape[1]), b16),
        scratch_shapes=[pltpu.SemaphoreType.DMA(())],
        compiler_params=params,
        name="beside",
    )(in_hbm(out_weight), mirrored)
    features, tied = ring(swapped, "ch", (both, (step, join, reach, jump, poles)))
    second = gather(tied[0], 0)
    step, join, reach, jump, poles = tied[1]
    here = lax.axis_index("ch")

    keep, send, lhs = pl.pallas_call(
        functools.partial(mixin_project_kernel, count),
        in_specs=[IN_SMEM] + [IN_VMEM] * count + [IN_HBM],
        out_shape=[
            pltpu.VMEM((padded, 2 * chans), f32),
            pltpu.VMEM((padded, 2 * chans), b16),
            shape((2, padded, depth), b16),
        ],
        scratch_shapes=[pltpu.VMEM((depth, 2 * chans), b16), pltpu.SemaphoreType.DMA((2,))],
        compiler_params=params,
        cost_estimate=pl.CostEstimate(
            flops=8 * padded * depth * chans, bytes_accessed=4 * depth * chans, transcendentals=0
        ),
        name="project_mixin",
    )(jnp.stack([half, here]).astype(jnp.int32), *features, in_hbm(weight))
    more = lax.ppermute(send, "seq", pairs)
    query_keep, query_send = pl.pallas_call(
        query_project_kernel,
        in_specs=[IN_VMEM, IN_HBM],
        out_shape=[shape((padded, chans), f32), shape((padded, chans), b16)],
        scratch_shapes=[pltpu.VMEM((depth, chans), b16), pltpu.SemaphoreType.DMA((1,))],
        compiler_params=params,
        cost_estimate=pl.CostEstimate(
            flops=4 * padded * depth * chans, bytes_accessed=2 * depth * chans, transcendentals=0
        ),
        name="project_query",
    )(lhs, in_hbm(weight))
    taps = short_filter
    mixin, begin, final, query_send = pl.pallas_call(
        functools.partial(scan_kernel, rows, chans),
        out_shape=[
            shape((chans // LANES, rows, LANES), f32),
            shape((4, SUB, chans), f32),
            shape((4, chans), f32),
            shape((padded, chans), b16),
        ],
        compiler_params=params,
        name="scan",
    )(keep, more, query_send, taps, step, join)
    query_more = lax.ppermute(query_send, "seq", pairs)

    states = spread(final, "seq")
    gated = pl.pallas_call(
        functools.partial(gate_kernel, rows, chans),
        out_shape=shape((rows, chans), b16),
        scratch_shapes=[pltpu.VMEM((chans // LANES, rows, LANES), f32)],
        compiler_params=params,
        name="gate",
    )(states, jump, begin, reach, step, poles, bias[None, :], mixin, query_keep, query_more, taps)

    which = jnp.stack([lax.rem(here + hop + count, count) for hop in ring_hops(count)] + [half])
    parts, _ = ring(gated, "ch")
    first, rest = mix(parts[:-1], which.astype(jnp.int32), second, out_weight.shape[1])
    return pl.pallas_call(
        last_mix_kernel,
        out_shape=shape(first.shape, b16),
        compiler_params=params,
        name="last_mix",
    )(parts[-1], rest, first)


def solution(mesh):
    placed = (
        P("seq", "ch"),
        P("seq", None, None),
        P("seq", "ch"),
        P(None, None, "ch"),
        P("ch", None),
        P("ch", None),
        P(None, "ch", None),
        P("ch"),
    )
    return jax.shard_map(
        body, mesh=mesh, in_specs=placed, out_specs=P("seq", "ch"), check_vma=False
    )
```

```python
import functools

import jax
import jax.numpy as jnp
from jax import lax
from jax.experimental import pallas as pl
from jax.experimental.pallas import tpu as pltpu
from jax.sharding import PartitionSpec as P

HALO = 16
LANES = 128
SUB = 8
VMEM = 24 * 1024 * 1024


def spread(x, axis):
    count = lax.axis_size(axis)
    return lax.all_to_all(
        jnp.broadcast_to(x[None], (count,) + x.shape), axis, 0, 0, tiled=True
    )


def ring_hops(count):
    hops = [0]
    for hop in range(1, count // 2 + 1):
        hops += [-hop, hop] if 2 * hop < count else [-hop]
    return hops


def ring(x, axis, tied=()):
    tied = list(tied)
    count = lax.axis_size(axis)
    up = [(c, (c + 1) % count) for c in range(count)]
    down = [(c, (c - 1) % count) for c in range(count)]
    arrived = [x]
    below = above = x
    for hop in range(1, count // 2 + 1):
        below = lax.ppermute(below, axis, up)
        arrived.append(below)
        if 2 * hop < count:
            above = lax.ppermute(above, axis, down)
            arrived.append(above)
        if hop <= len(tied):
            below, above, tied[hop - 1] = lax.optimization_barrier((below, above, tied[hop - 1]))
            arrived[2 * hop - 1 :] = [below, above]
    return arrived, tied


def powers_kernel(rows, place_ref, rate_ref, turn_ref, residue_ref, step_ref, join_ref, reach_ref, jump_ref, poles_ref):
    chans = rate_ref.shape[1]
    length = rows // SUB
    blocks = jump_ref.shape[1]
    gap = place_ref[0] - 1 - lax.broadcasted_iota(jnp.int32, (blocks, chans), 0)
    far = (jnp.maximum(gap, 0) * rows).astype(jnp.float32)
    near = (lax.broadcasted_iota(jnp.int32, (SUB, chans), 0) * length).astype(jnp.float32)
    short = jnp.where(lax.broadcasted_iota(jnp.int32, (SUB, chans), 0) == 0, 1.0, float(length))
    for n in range(2):
        rate, turn = rate_ref[n : n + 1, :], turn_ref[n : n + 1, :]
        mag, phase = jnp.exp(-far * rate), far * turn
        jump_ref[n] = jnp.where(gap >= 0, mag * jnp.cos(phase), 0.0)
        jump_ref[2 + n] = jnp.where(gap >= 0, mag * jnp.sin(phase), 0.0)
        mag, phase = jnp.exp(-near * rate), near * turn
        reach_ref[n] = mag * jnp.cos(phase)
        reach_ref[2 + n] = mag * jnp.sin(phase)
        mag, phase = jnp.exp(-short * rate), short * turn
        re, im = mag * jnp.cos(phase), mag * jnp.sin(phase)
        step_ref[n : n + 1, :] = re[0:1]
        step_ref[2 + n : 3 + n, :] = im[0:1]
        join_ref[n : n + 1, :] = re[1:2]
        join_ref[2 + n : 3 + n, :] = im[1:2]
        poles_ref[n : n + 1, :] = residue_ref[0, n : n + 1, :]
        poles_ref[2 + n : 3 + n, :] = residue_ref[1, n : n + 1, :]


def fetch(w_ref, w, sems, branches):
    copies = []
    for j, branch in enumerate(branches):
        chans = w_ref.shape[2]
        copies.append(
            pltpu.make_async_copy(w_ref.at[branch], w.at[:, pl.ds(j * chans, chans)], sems.at[j])
        )
        copies[-1].start()
    return copies


def product(lhs_ref, w, copies, chans, keep_ref, send_ref):
    sides, rows, depth = lhs_ref.shape
    both = lhs_ref[...].reshape(sides * rows, depth)
    for j, copy in enumerate(copies):
        copy.wait()
        cols = slice(j * chans, (j + 1) * chans)
        part = jnp.dot(both, w[:, cols], preferred_element_type=jnp.float32)
        keep_ref[:, cols] = part[:rows]
        send_ref[:, cols] = part[rows:].astype(send_ref.dtype)


def mixin_project_kernel(count, place_ref, *refs):
    x_refs, (w_ref, keep_ref, send_ref, lhs_ref, w, sems) = refs[:count], refs[count:]
    chans = x_refs[0].shape[1]
    copies = fetch(w_ref, w, sems, (1, 2))
    half, here = place_ref[0], place_ref[1]
    for x_ref, hop in zip(x_refs, ring_hops(count)):
        origin = lax.rem(here + hop + count, count)
        side = jnp.where(lax.rem(origin, 2) == half, 0, 1)
        at = pl.multiple_of(lax.div(origin, 2) * chans, chans)
        lhs_ref[side, :, pl.ds(at, chans)] = x_ref[...]
    product(lhs_ref, w, copies, chans, keep_ref, send_ref)


def query_project_kernel(lhs_ref, w_ref, keep_ref, send_ref, w, sems):
    chans = keep_ref.shape[1]
    copies = fetch(w_ref, w, sems, (0,))
    product(lhs_ref, w, copies, chans, keep_ref, send_ref)


def cut_kernel(place_ref, w_ref, out_ref, sem):
    cols = out_ref.shape[2]
    at = pl.multiple_of(place_ref[0] * cols, cols)
    copy = pltpu.make_async_copy(w_ref.at[:, :, pl.ds(at, cols)], out_ref, sem)
    copy.start()
    copy.wait()


def beside_kernel(x_ref, y_ref, out_ref, sem):
    cols = x_ref.shape[1]
    copy = pltpu.make_async_copy(x_ref, out_ref.at[:, pl.ds(0, cols)], sem)
    copy.start()
    out_ref[:, cols:] = y_ref[...]
    copy.wait()


def short_conv(rows, branch, total, taps_ref):
    now = total[:rows]
    past = total[rows : rows + 8]
    one = jnp.concatenate([past[1:2], now[:-1]], axis=0)
    two = jnp.concatenate([past[0:2], now[:-2]], axis=0)
    tap = [taps_ref[j, branch : branch + 1, :] for j in range(3)]
    return tap[0] * now + tap[1] * one + tap[2] * two


def scan_kernel(
    rows,
    chans,
    keep_ref,
    more_ref,
    query_ref,
    taps_ref,
    step_ref,
    join_ref,
    mixin_ref,
    begin_ref,
    final_ref,
    send_ref,
):
    send_ref[...] = query_ref[...]
    length = rows // SUB

    def filtered(branch):
        cols = slice((branch - 1) * chans, branch * chans)
        total = keep_ref[:, cols] + more_ref[:, cols].astype(jnp.float32)
        return short_conv(rows, branch, total, taps_ref)

    mixin = filtered(1) * filtered(2)
    for q in range(chans // LANES):
        mixin_ref[q] = mixin[:, q * LANES : (q + 1) * LANES]
    for q in range(chans // LANES):
        cols = slice(q * LANES, (q + 1) * LANES)
        wide = lambda row: jnp.broadcast_to(row, (SUB, LANES))
        ar = [wide(step_ref[n : n + 1, cols]) for n in range(2)]
        ai = [wide(step_ref[2 + n : 3 + n, cols]) for n in range(2)]
        re = [jnp.zeros((SUB, LANES), jnp.float32)] * 2
        im = [jnp.zeros((SUB, LANES), jnp.float32)] * 2
        for i in range(length):
            u = mixin_ref[q, pl.ds(i, SUB, stride=length), :]
            for n in range(2):
                re[n], im[n] = ar[n] * re[n] - ai[n] * im[n] + u, ar[n] * im[n] + ai[n] * re[n]
        for n in range(2):
            jr = join_ref[n : n + 1, cols]
            ji = join_ref[2 + n : 3 + n, cols]
            er = jnp.zeros((1, LANES), jnp.float32)
            ei = jnp.zeros((1, LANES), jnp.float32)
            for b in range(SUB):
                begin_ref[n, b : b + 1, cols] = er
                begin_ref[2 + n, b : b + 1, cols] = ei
                er, ei = (
                    jr * er - ji * ei + re[n][b : b + 1],
                    jr * ei + ji * er + im[n][b : b + 1],
                )
            final_ref[n : n + 1, cols] = er
            final_ref[2 + n : 3 + n, cols] = ei


def gate_kernel(
    rows, chans, all_ref, jump_ref, begin_ref, reach_ref, step_ref, residue_ref, bias_ref, mixin_ref, keep_ref, more_ref, taps_ref, out_ref, long
):
    query = short_conv(rows, 0, keep_ref[...] + more_ref[...].astype(jnp.float32), taps_ref)
    length = rows // SUB
    entry = []
    for n in range(2):
        fr, fi = all_ref[:, n, :], all_ref[:, 2 + n, :]
        cr, ci = jump_ref[n], jump_ref[2 + n]
        gr = jnp.sum(cr * fr - ci * fi, axis=0, keepdims=True)
        gi = jnp.sum(cr * fi + ci * fr, axis=0, keepdims=True)
        rr, ri = reach_ref[n], reach_ref[2 + n]
        entry.append((begin_ref[n] + rr * gr - ri * gi, begin_ref[2 + n] + rr * gi + ri * gr))
    for q in range(chans // LANES):
        cols = slice(q * LANES, (q + 1) * LANES)
        wide = lambda row: jnp.broadcast_to(row, (SUB, LANES))
        ar = [wide(step_ref[n : n + 1, cols]) for n in range(2)]
        ai = [wide(step_ref[2 + n : 3 + n, cols]) for n in range(2)]
        pr = [wide(residue_ref[n : n + 1, cols]) for n in range(2)]
        pi = [wide(residue_ref[2 + n : 3 + n, cols]) for n in range(2)]
        direct = wide(bias_ref[:, cols])
        re = [entry[n][0][:, cols] for n in range(2)]
        im = [entry[n][1][:, cols] for n in range(2)]
        for i in range(length):
            u = mixin_ref[q, pl.ds(i, SUB, stride=length), :]
            y = direct * u
            for n in range(2):
                re[n], im[n] = ar[n] * re[n] - ai[n] * im[n] + u, ar[n] * im[n] + ai[n] * re[n]
                y = y + (pr[n] * re[n] - pi[n] * im[n])
            long[q, pl.ds(i, SUB, stride=length), :] = y
        out_ref[:, cols] = (query[:, cols] * long[q]).astype(out_ref.dtype)


def mix_kernel(count, which_ref, *refs):
    x_refs, (w_ref, out_ref, rest_ref, w, sems) = refs[: count - 1], refs[count - 1 :]
    chans = x_refs[0].shape[1]
    part = chans // 2
    copies = []
    for j in range(count):
        block = which_ref[j]
        other = jnp.where(lax.rem(block, 2) == which_ref[count], 0, 1)
        col = pl.multiple_of(other * chans, chans)
        pair = []
        for e in range(2):
            row = pl.multiple_of(lax.div(block, 2) * chans + jnp.where(other == e, 0, part), part)
            dst = rest_ref if j == count - 1 else w.at[j]
            pair.append(
                pltpu.make_async_copy(
                    w_ref.at[pl.ds(row, part), pl.ds(col, out_ref.shape[1])],
                    dst.at[pl.ds(e * part, part)],
                    sems.at[j, e],
                )
            )
            pair[-1].start()
        copies.append(pair)
    total = jnp.zeros(out_ref.shape, jnp.float32)
    for j in range(count):
        for copy in copies[j]:
            copy.wait()
        if j < count - 1:
            total = total + jnp.dot(x_refs[j][...], w[j], preferred_element_type=jnp.float32)
    out_ref[...] = total


def last_mix_kernel(x_ref, w_ref, base_ref, out_ref):
    total = base_ref[...] + jnp.dot(x_ref[...], w_ref[...], preferred_element_type=jnp.float32)
    out_ref[...] = total.astype(out_ref.dtype)


IN_VMEM = pl.BlockSpec(memory_space=pltpu.VMEM)
IN_SMEM = pl.BlockSpec(memory_space=pltpu.SMEM)
IN_HBM = pl.BlockSpec(memory_space=pltpu.HBM)
in_hbm = functools.partial(pltpu.with_memory_space_constraint, memory_space=pltpu.HBM)


def mix(blocks, which, weight, cols):
    rows, chans = blocks[0].shape
    count = len(blocks) + 1
    return pl.pallas_call(
        functools.partial(mix_kernel, count),
        in_specs=[IN_SMEM] + [IN_VMEM] * (count - 1) + [IN_HBM],
        out_shape=[
            jax.ShapeDtypeStruct((rows, cols), jnp.float32),
            jax.ShapeDtypeStruct((chans, cols), weight.dtype),
        ],
        scratch_shapes=[
            pltpu.VMEM((count - 1, chans, cols), weight.dtype),
            pltpu.SemaphoreType.DMA((count, 2)),
        ],
        compiler_params=pltpu.CompilerParams(vmem_limit_bytes=VMEM),
        cost_estimate=pl.CostEstimate(
            flops=2 * count * rows * chans * cols,
            bytes_accessed=2 * count * chans * cols,
            transcendentals=0,
        ),
        name="mix",
    )(which, *blocks, in_hbm(weight))


def body(inputs, in_weight, out_weight, short_filter, decay, angle, residue, bias):
    rows, chans = inputs.shape
    place, blocks = lax.axis_index("seq"), lax.axis_size("seq")
    count = lax.axis_size("ch")
    near = [(s % 8) // 4 for s in range(blocks)]
    mirror = [s + 6 - 4 * ((s % 8) // 2) for s in range(blocks)]
    cut = pl.pallas_call(
        cut_kernel,
        in_specs=[IN_SMEM, IN_HBM],
        out_shape=jax.ShapeDtypeStruct((3, in_weight.shape[0], chans), jnp.bfloat16),
        scratch_shapes=[pltpu.SemaphoreType.DMA(())],
        compiler_params=pltpu.CompilerParams(vmem_limit_bytes=VMEM),
        name="cut",
    )(lax.axis_index("ch").reshape(1).astype(jnp.int32), in_hbm(in_weight.transpose(1, 0, 2)))
    pairs = [(s, mirror[s]) for s in range(blocks)]
    halves = [[s for s in range(blocks) if near[s] == h] for h in range(2)]
    gather = lambda x, axis: lax.all_gather(x, "seq", axis=axis, tiled=True, axis_index_groups=halves)
    weight = gather(cut, 1)
    f32, b16 = jnp.float32, jnp.bfloat16
    padded, depth = rows + HALO, chans * count // 2
    params = pltpu.CompilerParams(vmem_limit_bytes=VMEM)
    shape = jax.ShapeDtypeStruct
    half = lax.rem(place, 8) // 4
    rim = lax.ppermute(inputs[-2:], "seq", [(i, i + 1) for i in range(blocks - 1)])
    mirrored = lax.ppermute(out_weight, "seq", pairs)
    rim, mirrored = lax.optimization_barrier((rim, mirrored))
    tokens = jnp.concatenate([inputs, rim, jnp.zeros((HALO - 2, chans), inputs.dtype)], axis=0)
    swaps = []
    for c in range(count):
        for s in range(blocks):
            to = (c, s) if c % 2 == near[s] else (c ^ 1, mirror[s])
            swaps.append((c * blocks + s, to[0] * blocks + to[1]))
    swapped = lax.ppermute(tokens, ("ch", "seq"), swaps)
    step, join, reach, jump, poles = pl.pallas_call(
        functools.partial(powers_kernel, rows),
        in_specs=[IN_SMEM] + [IN_VMEM] * 3,
        out_shape=[
            shape((4, chans), f32),
            shape((4, chans), f32),
            shape((4, SUB, chans), f32),
            shape((4, blocks, chans), f32),
            shape((4, chans), f32),
        ],
        compiler_params=params,
        name="powers",
    )(place.reshape(1).astype(jnp.int32), decay.T, angle.T, residue.transpose(0, 2, 1))
    both = pl.pallas_call(
        beside_kernel,
        in_specs=[IN_HBM, IN_VMEM],
        out_shape=shape((out_weight.shape[0], 2 * out_weight.shape[1]), b16),
        scratch_shapes=[pltpu.SemaphoreType.DMA(())],
        compiler_params=params,
        name="beside",
    )(in_hbm(out_weight), mirrored)
    features, tied = ring(swapped, "ch", (both, (step, join, reach, jump, poles)))
    second = gather(tied[0], 0)
    step, join, reach, jump, poles = tied[1]
    here = lax.axis_index("ch")

    keep, send, lhs = pl.pallas_call(
        functools.partial(mixin_project_kernel, count),
        in_specs=[IN_SMEM] + [IN_VMEM] * count + [IN_HBM],
        out_shape=[
            pltpu.VMEM((padded, 2 * chans), f32),
            pltpu.VMEM((padded, 2 * chans), b16),
            shape((2, padded, depth), b16),
        ],
        scratch_shapes=[pltpu.VMEM((depth, 2 * chans), b16), pltpu.SemaphoreType.DMA((2,))],
        compiler_params=params,
        cost_estimate=pl.CostEstimate(
            flops=8 * padded * depth * chans, bytes_accessed=4 * depth * chans, transcendentals=0
        ),
        name="project_mixin",
    )(jnp.stack([half, here]).astype(jnp.int32), *features, in_hbm(weight))
    more = lax.ppermute(send, "seq", pairs)
    query_keep, query_send = pl.pallas_call(
        query_project_kernel,
        in_specs=[IN_VMEM, IN_HBM],
        out_shape=[shape((padded, chans), f32), shape((padded, chans), b16)],
        scratch_shapes=[pltpu.VMEM((depth, chans), b16), pltpu.SemaphoreType.DMA((1,))],
        compiler_params=params,
        cost_estimate=pl.CostEstimate(
            flops=4 * padded * depth * chans, bytes_accessed=2 * depth * chans, transcendentals=0
        ),
        name="project_query",
    )(lhs, in_hbm(weight))
    taps = short_filter
    mixin, begin, final, query_send = pl.pallas_call(
        functools.partial(scan_kernel, rows, chans),
        out_shape=[
            shape((chans // LANES, rows, LANES), f32),
            shape((4, SUB, chans), f32),
            shape((4, chans), f32),
            shape((padded, chans), b16),
        ],
        compiler_params=params,
        name="scan",
    )(keep, more, query_send, taps, step, join)
    query_more = lax.ppermute(query_send, "seq", pairs)

    states = spread(final, "seq")
    gated = pl.pallas_call(
        functools.partial(gate_kernel, rows, chans),
        out_shape=shape((rows, chans), b16),
        scratch_shapes=[pltpu.VMEM((chans // LANES, rows, LANES), f32)],
        compiler_params=params,
        name="gate",
    )(states, jump, begin, reach, step, poles, bias[None, :], mixin, query_keep, query_more, taps)

    which = jnp.stack([lax.rem(here + hop + count, count) for hop in ring_hops(count)] + [half])
    parts, _ = ring(gated, "ch")
    first, rest = mix(parts[:-1], which.astype(jnp.int32), second, out_weight.shape[1])
    return pl.pallas_call(
        last_mix_kernel,
        out_shape=shape(first.shape, b16),
        compiler_params=params,
        name="last_mix",
    )(parts[-1], rest, first)


def solution(mesh):
    placed = (
        P("seq", "ch"),
        P("seq", None, None),
        P("seq", "ch"),
        P(None, None, "ch"),
        P("ch", None),
        P("ch", None),
        P(None, "ch", None),
        P("ch"),
    )
    return jax.shard_map(
        body, mesh=mesh, in_specs=placed, out_specs=P("seq", "ch"), check_vma=False
    )
```
